32 devices in a mesh: seq: 8 (over y, x, core), shard: 4 (over z).
Axes of the slice: x: 2, y: 2, z: 4, core: 2. Of those that a mesh axis runs over, the one named last changes fastest.
Arguments:
- tokens: bfloat16 [4, 1024, 768], P('shard', 'seq'), may hold values from -6 to 6
- norm_gain: bfloat16 [768], P('shard'), may hold values from 0.5 to 1.5
- w_qkv: bfloat16 [768, 2304], P('shard'), may hold values from -0.3125 to 0.3125
- w_out: bfloat16 [768, 768], P('shard'), may hold values from -0.875 to 0.875
- ffn_gain: bfloat16 [768], P('shard'), may hold values from 0.5 to 1.5
- w_in: bfloat16 [768, 2304], P('shard'), may hold values from -0.21875 to 0.21875
- w_back: bfloat16 [1152, 768], P('shard'), may hold values from -0.375 to 0.375
- seq_ids: int32 [4, 16], P('shard'), may hold values from 0 to 0, as said below
- cotangent: bfloat16 [4, 1024, 768], P('shard', 'seq'), may hold values from -6 to 6
Outputs:
- mixed: bfloat16 [4, 1024, 768], P('shard', 'seq')
- grad_tokens: bfloat16 [4, 1024, 768], P('shard', 'seq')
- grad_norm_gain: float32 [768], P('shard')
- grad_w_qkv: float32 [768, 2304], P('shard')
- grad_w_out: float32 [768, 768], P('shard')
- grad_ffn_gain: float32 [768], P('shard')
- grad_w_in: float32 [768, 2304], P('shard')
- grad_w_back: float32 [1152, 768], P('shard')
The draws below stay inside these ranges and needn't reach their ends.
Inputs may be any that keep to these rules, and one draw needn't show every extreme that they name: `seq_ids`: along a row ids never fall and each id 0 to 0 appears; the j-th boundary (j = 1 .. 0) lies within 16 spans of j * 64, the last sequence takes the rest of the set.
All inputs are finite; a program needn't handle non-finite values.
Results may differ from the reference program's by a relative error of at most 0.02.
Values may be sent and summed in bfloat16 or wider, within the bound.
No kernel may reach another device: no remote copies, remote signals or barrier semaphores. Data moves between devices by JAX's collectives and lax.ppermute only.
A program may use at most 128 MiB of HBM per device.

```python
import math
import jax
import jax.numpy as jnp
from jax import lax

D = 768
HEADS = 12
HEAD_DIM = 64
FF = 1152
HALF = 64
GROUPS = 4
GROUP_TOK = 1024
NCHUNK = 16
SEQ_SPANS = 64


def draw_seq_ids(key, part):
    key = jax.random.fold_in(key, 11)
    count = max(1, NCHUNK // SEQ_SPANS)
    reach = SEQ_SPANS // 4
    jitter = jax.random.randint(key, (GROUPS, count - 1), -reach, reach + 1)
    bounds = (jnp.arange(1, count)[None, :] * SEQ_SPANS + jitter).astype(jnp.int32)
    places = jnp.arange(NCHUNK).astype(jnp.int32)[None, :, None]
    passed = (places >= bounds[:, None, :]).astype(jnp.int32)
    return jnp.sum(passed, axis=-1).astype(jnp.int32)


def block_scale(key, dims, shards, least, high):
    def one(axis_at, parts):
        steps = jax.random.uniform(jax.random.fold_in(jax.random.fold_in(key, 6), axis_at), (parts,), jnp.float32, least / len(shards), high / len(shards))
        return jnp.repeat(jnp.exp(steps), dims[axis_at] // parts).reshape((-1,) + (1,) * (len(dims) - axis_at - 1))

    loudness = one(*shards[0])
    for cut in shards[1:]:
        loudness = loudness * one(*cut)
    return loudness


def bell_draw(key, extent, scale, most, pieces=(), kind=jnp.bfloat16):
    level = block_scale(key, extent, pieces, -0.22, 0.18) if pieces else 1.0
    entries = jax.random.normal(key, extent, jnp.float32) * scale * level
    return jnp.minimum(jnp.maximum(entries, -most), most).astype(kind)


def setup_inputs(seed: int = 0) -> dict:
    arg_keys = jax.random.split(jax.random.key(seed), 10)
    return {
        "tokens": bell_draw(arg_keys[0], (GROUPS, GROUP_TOK, D), 1.0, 6.0, ((0, 4), (1, 8))),
        "norm_gain": jnp.clip(1.0 + 0.1 * jax.random.normal(arg_keys[1], (D,), jnp.float32), 0.5, 1.5).astype(jnp.bfloat16),
        "w_qkv": bell_draw(arg_keys[2], (D, 3 * D), (D // 2) ** -0.5, 0.3125, ((0, 4),)),
        "w_out": bell_draw(arg_keys[3], (D, D), (D // 16) ** -0.5, 0.875, ((0, 4),)),
        "ffn_gain": jnp.clip(1.0 + 0.1 * jax.random.normal(arg_keys[4], (D,), jnp.float32), 0.5, 1.5).astype(jnp.bfloat16),
        "w_in": bell_draw(arg_keys[5], (D, 2 * FF), D ** -0.5, 0.21875, ((0, 4),)),
        "w_back": bell_draw(arg_keys[6], (FF, D), (FF // 4) ** -0.5, 0.375, ((0, 4),)),
        "seq_ids": draw_seq_ids(jax.random.fold_in(arg_keys[9], 71), 0),
        "cotangent": bell_draw(arg_keys[8], (GROUPS, GROUP_TOK, D), 1.0, 6.0, ((0, 4), (1, 8))),
    }


@jax.custom_vjp
def low(v):
    return lax.optimization_barrier(v.astype(jnp.bfloat16)).astype(jnp.float32)

@jax.custom_vjp
def low_back(v):
    return v

def low_keep(v):
    return (low(v), None)

def low_pass(kept, grad):
    return (grad,)

def back_keep(v):
    return (v, None)

def back_low(kept, grad):
    return (low(grad),)
low.defvjp(low_keep, low_pass)
low_back.defvjp(back_keep, back_low)

def matmul(left, right):
    return jnp.dot(left, right, preferred_element_type=jnp.float32, precision=lax.Precision.HIGHEST)

def layer_norm(values, gain_full):
    center = values - lax.optimization_barrier(jnp.mean(values, axis=-1, keepdims=True))
    variance = lax.optimization_barrier(jnp.mean(center * center, axis=-1, keepdims=True))
    return center * lax.rsqrt(variance + 1e-05) * gain_full

def rotate(values, cosine, sine):
    middle = values.shape[-1] // 2
    turned = jnp.concatenate([-values[..., middle:], values[..., :middle]], axis=-1)
    return values * cosine + turned * sine

def attend(queries, keys_all, values_all, token_ids):
    length = queries.shape[0]
    block = math.gcd(512, length)
    padding = ((HALF, HALF), (0, 0), (0, 0))
    keys_pad = jnp.pad(keys_all, padding)
    values_pad = jnp.pad(values_all, padding)
    ids_pad = jnp.pad(token_ids, (HALF, HALF), constant_values=-1)
    offset = jnp.arange(block + 2 * HALF)[None, :] - HALF - jnp.arange(block)[:, None]

    def one_block(number):
        start = (number * block).astype(jnp.int32)
        query_block = lax.dynamic_slice_in_dim(queries, start, block, 0)
        key_block = lax.dynamic_slice_in_dim(keys_pad, start, block + 2 * HALF, 0)
        value_block = lax.dynamic_slice_in_dim(values_pad, start, block + 2 * HALF, 0)
        query_ids = lax.dynamic_slice_in_dim(token_ids, start, block, 0)
        key_ids = lax.dynamic_slice_in_dim(ids_pad, start, block + 2 * HALF, 0)
        allowed = (jnp.abs(offset) <= HALF) & (query_ids[:, None] == key_ids[None, :])
        scores = low_back(jnp.einsum('qhd,khd->hqk', query_block, key_block, precision=lax.Precision.HIGHEST))
        logits = jnp.where(allowed[None], scores * HEAD_DIM ** (-0.5), -1e+30)
        shifted = logits - lax.optimization_barrier(jnp.max(logits, axis=-1, keepdims=True))
        exponent = jnp.exp(shifted)
        probs = low(exponent / lax.optimization_barrier(jnp.sum(exponent, axis=-1, keepdims=True)))
        return jnp.einsum('hqk,khd->qhd', probs, value_block, precision=lax.Precision.HIGHEST)
    blocks = lax.map(jax.checkpoint(one_block), jnp.arange(length // block))
    return blocks.reshape(length, HEADS, HEAD_DIM)

def forward(inputs, gain_one, matrix_qkv, matrix_out, gain_two, matrix_in, matrix_back, token_ids, cosine, sine):
    length = inputs.shape[0]
    input_low = low(layer_norm(inputs, gain_one))
    projected = low_back(matmul(input_low, matrix_qkv))
    queries = low(rotate(projected[:, :D].reshape(length, HEADS, HEAD_DIM), cosine, sine))
    keys_all = low(rotate(projected[:, D:2 * D].reshape(length, HEADS, HEAD_DIM), cosine, sine))
    values_all = low(projected[:, 2 * D:].reshape(length, HEADS, HEAD_DIM))
    context = attend(queries, keys_all, values_all, token_ids)
    attended = low(low_back(context)).reshape(length, D)
    residual = inputs + low_back(matmul(attended, matrix_out))
    middle_low = low(layer_norm(residual, gain_two))
    expanded = low_back(matmul(middle_low, matrix_in))
    hidden_low = low(jax.nn.gelu(expanded[:, :FF], approximate=False) * expanded[:, FF:])
    return residual + low_back(matmul(hidden_low, matrix_back))

def reference(tokens, norm_gain, w_qkv, w_out, ffn_gain, w_in, w_back, seq_ids, cotangent):
    weights = tuple((weight.astype(jnp.float32) for weight in (norm_gain, w_qkv, w_out, ffn_gain, w_in, w_back)))
    length = tokens.shape[1]
    position = jnp.arange(length).astype(jnp.float32)
    frequency = 10000.0 ** (-jnp.arange(0, HEAD_DIM, 2).astype(jnp.float32) / HEAD_DIM)
    angles = position[:, None] * frequency[None, :]
    angles = jnp.concatenate([angles, angles], axis=-1)[:, None, :]
    cosine = jnp.cos(angles)
    sine = jnp.sin(angles)

    def one_set(totals, item):
        inputs, span_ids, upward = item
        token_ids = jnp.repeat(span_ids, HALF)

        def layer(values, *params):
            return forward(values, *params, token_ids, cosine, sine)
        result, pullback = jax.vjp(layer, inputs.astype(jnp.float32), *weights)
        grads = pullback(upward.astype(jnp.float32))
        totals = tuple((running + extra for running, extra in zip(totals, grads[1:])))
        return (totals, (result.astype(jnp.bfloat16), grads[0].astype(jnp.bfloat16)))
    start = tuple((jnp.zeros(weight.shape, jnp.float32) for weight in weights))
    totals, (mixed, grad_tokens) = lax.scan(one_set, start, (tokens, seq_ids, cotangent))
    return (mixed, grad_tokens, totals[0], totals[1], totals[2], totals[3], totals[4], totals[5])
```

```python
import functools

import jax
import jax.numpy as jnp
from jax import lax
from jax.experimental import pallas as pl
from jax.experimental.pallas import tpu as pltpu
from jax.sharding import PartitionSpec as P

HEADS = 12
HEAD_DIM = 64
FF = 1152
HALF = 64
CHIPS = 4
CORES = 2
MEMBERS = CHIPS * CORES
f32 = jnp.float32
bf16 = jnp.bfloat16
SCALE = HEAD_DIM ** (-0.5)
VMEM = 48 * 1024 * 1024


def dot(left, right):
    return lax.dot_general(left, right, (((1,), (0,)), ((), ())), preferred_element_type=f32)


def dot_t(left, right):
    return lax.dot_general(left, right, (((1,), (1,)), ((), ())), preferred_element_type=f32)


def t_dot(left, right):
    return lax.dot_general(left, right, (((0,), (0,)), ((), ())), preferred_element_type=f32)


def swap_seq(value, bits):
    count = lax.axis_size("seq")
    return lax.ppermute(value, "seq", [(i, i ^ bits) for i in range(count)])


def swap_shard(value, bits):
    count = lax.axis_size("shard")
    return lax.ppermute(value, "shard", [(i, i ^ bits) for i in range(count)])


def swap_core(value):
    return swap_seq(value, 1)


def over_chips(value):
    return [value] + [swap_seq(value, CORES * j) for j in range(1, CHIPS)]


def pick(index, items):
    return lax.select_n(index, *items)


def unxor(index, items):
    return [pick(index, [items[place ^ at] for at in range(4)]) for place in range(4)]


def by_core(core, own, other):
    return (jnp.where(core == 0, own, other), jnp.where(core == 0, other, own))


def norm_parts(values):
    center = values - jnp.mean(values, axis=-1, keepdims=True)
    factor = lax.rsqrt(jnp.mean(center * center, axis=-1, keepdims=True) + 1e-05)
    return center * factor, factor


def norm_inward(upward, gain, normed, factor):
    scaled = upward * gain
    return factor * (
        scaled
        - jnp.mean(scaled, axis=-1, keepdims=True)
        - normed * jnp.mean(scaled * normed, axis=-1, keepdims=True)
    )


def first_half(shape):
    return lax.broadcasted_iota(jnp.int32, shape, 1) % HEAD_DIM < HEAD_DIM // 2


def shifted(values):
    return pltpu.roll(values, 96, 1), pltpu.roll(values, 32, 1)


def qkv_kernel(x0, x1, x2, x3, gain, weight, cos, sin, a_out, q_out, kv_out):
    width = x0.shape[-1]
    rows = x0.shape[0]
    local = weight.shape[1] // 3
    for j, ref in enumerate((x0, x1, x2, x3)):
        normed, _ = norm_parts(ref[...].astype(f32))
        a_out[j * rows : (j + 1) * rows, :] = (normed * gain[...]).astype(bf16)
    out = dot(a_out[...], weight[...])
    front = first_half((CHIPS * rows, 128))
    parts = []
    for at in range(0, 2 * local, 128):
        u = out[:, at : at + 128]
        up, down = shifted(u)
        parts.append((u * cos[...] + jnp.where(front, -up, down) * sin[...]).astype(bf16))
    qk = jnp.concatenate(parts, axis=1)
    q_out[...] = qk[:, :local]
    kv_out[:, :local] = qk[:, local:]
    kv_out[:, local:] = out[:, 2 * local :].astype(bf16)


def probs_of(q, k, bias):
    logits = dot_t(q, k) * SCALE + bias
    highest = jnp.max(logits, axis=-1, keepdims=True)
    exponent = jnp.exp(logits - highest)
    return exponent / jnp.sum(exponent, axis=-1, keepdims=True)


def attend_kernel(q, kv, bias, out):
    local = q.shape[-1]
    heads = local // HEAD_DIM
    parts = []
    for h in range(heads):
        lanes = slice(h * HEAD_DIM, (h + 1) * HEAD_DIM)
        prob = probs_of(q[0, :, lanes], kv[0, :, lanes], bias[0]).astype(bf16)
        value = kv[0, :, local + h * HEAD_DIM : local + (h + 1) * HEAD_DIM]
        parts.append(dot(prob, value))
    out[0] = jnp.concatenate(parts, axis=1).astype(bf16)


def attend_back_kernel(q, kv, bias, dh, w_out, attn, dq_out, dkv_out, gw_out):
    local = q.shape[-1]
    heads = local // HEAD_DIM
    dctx = dot_t(dh[0], w_out[...]).astype(bf16)

    @pl.when(pl.program_id(0) == 0)
    def _():
        gw_out[...] = jnp.zeros_like(gw_out)

    gw_out[...] += t_dot(attn[0], dh[0])
    dqs, dks, dvs = [], [], []
    for h in range(heads):
        lanes = slice(h * HEAD_DIM, (h + 1) * HEAD_DIM)
        qh = q[0, :, lanes]
        kh = kv[0, :, lanes]
        vh = kv[0, :, local + h * HEAD_DIM : local + (h + 1) * HEAD_DIM]
        dch = dctx[:, lanes]
        prob = probs_of(qh, kh, bias[0])
        dprob = dot_t(dch, vh)
        inner = jnp.sum(prob * dprob, axis=-1, keepdims=True)
        dscore = (prob * (dprob - inner) * SCALE).astype(bf16)
        dqs.append(dot(dscore, kh))
        dks.append(t_dot(dscore, qh))
        dvs.append(t_dot(prob.astype(bf16), dch))
    dq_out[0] = jnp.concatenate(dqs, axis=1)
    dkv_out[0] = jnp.concatenate(dks + dvs, axis=1)


def turn_back_kernel(dq, dkv, cos, sin, out):
    local = dq.shape[-1]
    front = first_half((dq.shape[0], 128))
    g = jnp.concatenate([dq[...], dkv[:, :local]], axis=1)
    parts = []
    for at in range(0, 2 * local, 128):
        u = g[:, at : at + 128]
        up, down = shifted(u * sin[...])
        parts.append((u * cos[...] + jnp.where(front, up, -down)).astype(bf16))
    out[...] = jnp.concatenate(parts + [dkv[:, local:].astype(bf16)], axis=1)


def cost(flops, moved):
    return pl.CostEstimate(flops=int(flops), bytes_accessed=int(moved), transcendentals=0)


def params():
    return pltpu.CompilerParams(vmem_limit_bytes=VMEM)


def columns_of(rows, chip, parts):
    width = rows.shape[1] // parts
    share = width // CHIPS
    return pick(
        chip,
        [
            jnp.concatenate(
                [rows[:, p * width + b * share : p * width + (b + 1) * share] for p in range(parts)],
                axis=1,
            )
            for b in range(CHIPS)
        ],
    )


def columns_joined(pieces, parts):
    share = pieces[0].shape[1] // parts
    return jnp.concatenate(
        [piece[:, p * share : (p + 1) * share] for p in range(parts) for piece in pieces], axis=1
    )


def shards(tokens, norm_gain, w_qkv, w_out, ffn_gain, w_in, w_back, seq_ids, cotangent):
    length, width = tokens.shape[1:]
    me = lax.axis_index("seq")
    plane = lax.axis_index("shard")
    seq_count = lax.axis_size("seq")
    shard_count = lax.axis_size("shard")
    groups = seq_count // MEMBERS
    group = me // MEMBERS
    chip = (me % MEMBERS) // CORES
    core = me % CORES
    local = width // CHIPS
    units = FF // CHIPS
    many = CHIPS * length

    def gather_columns(weight, parts):
        half = weight.shape[0] // CORES
        piece = columns_of(lax.dynamic_slice_in_dim(weight, core * half, half, 0), chip, parts)
        pieces = [piece] + [swap_shard(piece, i) for i in range(1, shard_count)]
        mine = jnp.stack(unxor(plane, pieces))
        both = by_core(core, mine, swap_core(mine))
        return jnp.stack(both, axis=1).reshape(CORES * shard_count * half, -1)

    def gather_rows(weight):
        half = weight.shape[0] // CORES
        piece = lax.dynamic_slice_in_dim(weight, core * half, half, 0)
        pieces = [piece]
        for i in range(1, shard_count):
            pairs = [
                (m * shard_count + (m % MEMBERS) // CORES, m * shard_count + ((m % MEMBERS) // CORES ^ i))
                for m in range(seq_count)
            ]
            pieces.append(lax.ppermute(piece, ("seq", "shard"), pairs))
        mine = pick(plane ^ chip, pieces)
        both = by_core(core, mine, swap_core(mine))
        return jnp.concatenate(both, axis=0)

    x_own = tokens[0]
    xs = over_chips(x_own)
    wq = gather_columns(w_qkv, 3)
    gain_parts = lax.all_gather(jnp.stack([norm_gain, ffn_gain]), "shard", axis=1, tiled=True)
    gain_one = gain_parts[0].astype(f32)[None]
    gain_two = gain_parts[1].astype(f32)[None]
    w_out_full = lax.all_gather(w_out, "shard", axis=0, tiled=True).reshape(CHIPS, local, width)
    wo = unxor(chip, [w_out_full[b] for b in range(CHIPS)])
    wi = gather_columns(w_in, 2)
    wb = gather_rows(w_back)
    gys = over_chips(cotangent[0])

    block_chip = chip ^ jnp.arange(CHIPS)
    block = (group * CHIPS + block_chip) * CORES + core
    position = (block[:, None] * length + jnp.arange(length)[None]).astype(f32).reshape(many)
    frequency = 10000.0 ** (-jnp.arange(0, HEAD_DIM, 2).astype(f32) / HEAD_DIM)
    angles = position[:, None] * frequency[None]
    cosine, sine = lax.optimization_barrier((jnp.cos(angles), jnp.sin(angles)))
    cosine = jnp.tile(cosine, (1, 4))
    sine = jnp.tile(sine, (1, 4))
    extent = length + 2 * HALF
    spans = length // HALF
    ids = jnp.pad(seq_ids[0], (1, 1), constant_values=-1)
    key_ids = jnp.stack(
        [lax.dynamic_slice_in_dim(ids, block[j] * spans, spans + 2, 0) for j in range(CHIPS)]
    )
    key_ids = jnp.repeat(key_ids, HALF, axis=1)
    query_ids = key_ids[:, HALF : HALF + length]
    offset = jnp.arange(extent)[None, :] - HALF - jnp.arange(length)[:, None]
    allowed = (jnp.abs(offset) <= HALF)[None] & (query_ids[:, :, None] == key_ids[:, None, :])
    bias = jnp.where(allowed, 0.0, -1e30).astype(f32)

    low_one, query, kv = pl.pallas_call(
        qkv_kernel,
        out_shape=(
            jax.ShapeDtypeStruct((many, width), bf16),
            jax.ShapeDtypeStruct((many, local), bf16),
            jax.ShapeDtypeStruct((many, 2 * local), bf16),
        ),
        cost_estimate=cost(2 * many * width * 3 * local, 4e6),
        compiler_params=params(),
        name="qkv",
    )(*xs, gain_one, wq, cosine, sine)
    kv = kv.reshape(CHIPS, length, 2 * local)
    query = query.reshape(CHIPS, length, local)
    kv_other = swap_core(kv)
    others = unxor(chip, [kv_other[j] for j in range(CHIPS)])
    if groups > 1:
        mine_abs = unxor(chip, [kv[j] for j in range(CHIPS)])
        edge = jnp.where(core == 0, mine_abs[0][:HALF], mine_abs[CHIPS - 1][length - HALF :])

        def beyond(value):
            pairs = []
            for m in range(seq_count):
                c, k = (m % MEMBERS) // CORES, m % CORES
                to = m - MEMBERS + 1 if k == 0 else m + MEMBERS - 1
                if 0 <= to < seq_count:
                    pairs.append((m, to))
            return lax.ppermute(value, "seq", pairs)

        rim = beyond(edge)
    else:
        rim = jnp.zeros((HALF, 2 * local), bf16)
    heads_of = [o[:HALF] for o in others]
    tails_of = [o[length - HALF :] for o in others]
    before = [jnp.where(core == 0, ([rim] + tails_of)[b], tails_of[b]) for b in range(CHIPS)]
    after = [jnp.where(core == 0, heads_of[b], (heads_of + [rim])[b + 1]) for b in range(CHIPS)]
    kv_ext = jnp.concatenate(
        [jnp.stack(unxor(chip, before)), kv, jnp.stack(unxor(chip, after))], axis=1
    )

    def block_spec(rows, lanes):
        return pl.BlockSpec((1, rows, lanes), lambda j: (j, 0, 0))

    attn = pl.pallas_call(
        attend_kernel,
        grid=(CHIPS,),
        in_specs=[block_spec(length, local), block_spec(extent, 2 * local), block_spec(length, extent)],
        out_specs=block_spec(length, local),
        out_shape=jax.ShapeDtypeStruct((CHIPS, length, local), bf16),
        cost_estimate=cost(4 * many * extent * local, 2e6),
        compiler_params=params(),
        name="attend",
    )(query, kv_ext, bias)

    received = over_chips(attn)
    hidden = jnp.concatenate(xs, axis=0).astype(f32)
    for i in range(CHIPS):
        rows = jnp.concatenate([received[i][j ^ i] for j in range(CHIPS)], axis=0)
        hidden = hidden + dot(rows, wo[i])
    normed_two, factor_two = norm_parts(hidden)
    low_two = (normed_two * gain_two).astype(bf16)
    expanded = dot(low_two, wi)
    entering = expanded[:, :units]
    gating = expanded[:, units:]
    activated, gelu_pull = jax.vjp(lambda v: jax.nn.gelu(v, approximate=False), entering)
    hidden_low = (activated * gating).astype(bf16)
    upward_low = jnp.concatenate(gys, axis=0)
    grad_hidden = dot_t(upward_low, wb)
    grad_entering = gelu_pull(grad_hidden * gating)[0]
    grad_expanded = jnp.concatenate([grad_entering, grad_hidden * activated], axis=1).astype(bf16)
    grad_middle = dot_t(grad_expanded, wi)

    def sum_over_chips(partial):
        blocks = partial.reshape(CHIPS, length, width)
        total = blocks[0]
        for j in range(1, CHIPS):
            total = total + swap_seq(blocks[j].astype(bf16), CORES * j).astype(f32)
        return total

    grad_middle_own = sum_over_chips(grad_middle)
    grad_residual = cotangent[0].astype(f32) + norm_inward(
        grad_middle_own, gain_two, normed_two[:length], factor_two[:length]
    )
    residual_low = grad_residual.astype(bf16)
    dhs = jnp.stack(over_chips(residual_low))

    mixed = hidden[:length] + sum_over_chips(dot(hidden_low, wb))
    gain_two_sum = jnp.sum(grad_middle * normed_two, axis=0)
    grad_in = t_dot(low_two, grad_expanded)
    grad_back = t_dot(hidden_low, upward_low)

    def whole(*dims):
        return pl.BlockSpec(dims, lambda j: (0,) * len(dims))

    grad_query, grad_kv_ext, grad_out = pl.pallas_call(
        attend_back_kernel,
        grid=(CHIPS,),
        in_specs=[
            block_spec(length, local),
            block_spec(extent, 2 * local),
            block_spec(length, extent),
            block_spec(length, width),
            whole(local, width),
            block_spec(length, local),
        ],
        out_specs=(block_spec(length, local), block_spec(extent, 2 * local), whole(local, width)),
        out_shape=(
            jax.ShapeDtypeStruct((CHIPS, length, local), f32),
            jax.ShapeDtypeStruct((CHIPS, extent, 2 * local), f32),
            jax.ShapeDtypeStruct((local, width), f32),
        ),
        cost_estimate=cost(10 * many * extent * local, 4e6),
        compiler_params=params(),
        name="attend_back",
    )(query, kv_ext, bias, dhs, wo[0], attn)

    before = unxor(chip, [grad_kv_ext[j, :HALF].astype(bf16) for j in range(CHIPS)])
    after = unxor(chip, [grad_kv_ext[j, extent - HALF :].astype(bf16) for j in range(CHIPS)])
    zero = jnp.zeros((HALF, 2 * local), bf16)
    upper = [jnp.where(core == 0, after[b], ([zero] + after)[b]) for b in range(CHIPS)]
    lower = [jnp.where(core == 0, (before + [zero])[b + 1], before[b]) for b in range(CHIPS)]
    back = jnp.stack(
        unxor(chip, [jnp.concatenate([u, l], axis=0) for u, l in zip(upper, lower)])
    )
    grad_kv = grad_kv_ext[:, HALF : HALF + length] + swap_core(back).astype(f32)
    if groups > 1:
        rim = beyond(jnp.where(core == 0, before[0], after[CHIPS - 1])).astype(f32)
        edge_chip = jnp.where(core == 0, 0, CHIPS - 1)
        placed = jnp.where(
            core == 0,
            jnp.pad(rim, ((0, length - HALF), (0, 0))),
            jnp.pad(rim, ((length - HALF, 0), (0, 0))),
        )
        grad_kv = grad_kv + jnp.where((block_chip == edge_chip)[:, None, None], placed[None], 0.0)
    grad_projected = pl.pallas_call(
        turn_back_kernel,
        out_shape=jax.ShapeDtypeStruct((many, 3 * local), bf16),
        cost_estimate=cost(10 * many * 3 * local, 4e6),
        compiler_params=params(),
        name="turn_back",
    )(grad_query.reshape(many, local), grad_kv.reshape(many, 2 * local), cosine, sine)
    grad_qkv = t_dot(low_one, grad_projected)
    grad_low = dot_t(grad_projected, wq)
    normed_all, _ = norm_parts(jnp.concatenate(xs, axis=0).astype(f32))
    gain_one_sum = jnp.sum(grad_low * normed_all, axis=0)
    grad_low_own = sum_over_chips(grad_low)
    normed_one, factor_one = norm_parts(x_own.astype(f32))
    grad_inputs = grad_residual + norm_inward(grad_low_own, gain_one, normed_one, factor_one)

    def over_groups(total):
        step = MEMBERS
        while step < seq_count:
            total = total + swap_seq(total.astype(bf16), step).astype(f32)
            step *= 2
        return total

    def reduce_columns(grad, parts):
        half = grad.shape[0] // (CORES * shard_count)
        split = grad.reshape(shard_count, CORES, half, grad.shape[1])
        keep = pick(core, [split[:, 0], split[:, 1]])
        away = pick(core, [split[:, 1], split[:, 0]]).astype(bf16)
        keep = keep + swap_core(away).astype(f32)
        blocks = unxor(plane, [keep[b] for b in range(shard_count)])
        total = blocks[0]
        for i in range(1, shard_count):
            total = total + swap_shard(blocks[i].astype(bf16), i).astype(f32)
        total = over_groups(total)
        pieces = unxor(chip, over_chips(total.astype(bf16)))
        mine = columns_joined(pieces, parts)
        return jnp.concatenate(by_core(core, mine, swap_core(mine)), axis=0).astype(f32)

    def reduce_rows(grads):
        halves = [g.shape[0] // CORES for g in grads]

        def halves_of(k):
            return jnp.concatenate([g[k * h : (k + 1) * h] for g, h in zip(grads, halves)], axis=0)

        first, second = halves_of(0), halves_of(1)
        keep = pick(core, [first, second])
        away = pick(core, [second, first]).astype(bf16)
        keep = keep + swap_core(away).astype(f32)
        low = keep.astype(bf16)
        total = keep
        for i in range(1, shard_count):
            pairs = [
                (m * shard_count + ((m % MEMBERS) // CORES ^ i), m * shard_count + (m % MEMBERS) // CORES)
                for m in range(seq_count)
            ]
            total = total + lax.ppermute(low, ("seq", "shard"), pairs).astype(f32)
        total = over_groups(total).astype(bf16)
        pieces = [total]
        for j in range(1, CHIPS):
            pairs = []
            for m in range(seq_count):
                z = (m % MEMBERS) // CORES
                pairs.append((m * shard_count + z, (m ^ (CORES * j)) * shard_count + z))
            pieces.append(lax.ppermute(total, ("seq", "shard"), pairs))
        mine = pick(chip ^ plane, pieces)
        both = by_core(core, mine, swap_core(mine))
        results, at = [], 0
        for h in halves:
            results.append(jnp.concatenate([b[at : at + h] for b in both], axis=0).astype(f32))
            at += h
        return results

    owned_in = reduce_columns(grad_in, 2)
    owned_back, owned_out = reduce_rows((grad_back, grad_out))
    owned_qkv = reduce_columns(grad_qkv, 3)
    gains = jnp.stack([gain_one_sum, gain_two_sum])
    step = 1
    while step < seq_count:
        gains = gains + swap_seq(gains, step)
        step *= 2
    step = 1
    while step < shard_count:
        gains = gains + swap_shard(gains, step)
        step *= 2
    share = norm_gain.shape[0]
    gains = lax.dynamic_slice_in_dim(gains, plane * share, share, 1)
    return (
        mixed.astype(bf16)[None],
        grad_inputs.astype(bf16)[None],
        gains[0],
        owned_qkv,
        owned_out,
        gains[1],
        owned_in,
        owned_back,
    )


def solution(mesh):
    return jax.shard_map(
        shards,
        mesh=mesh,
        in_specs=(
            P("shard", "seq", None),
            P("shard"),
            P("shard", None),
            P("shard", None),
            P("shard"),
            P("shard", None),
            P("shard", None),
            P("shard", None),
            P("shard", "seq", None),
        ),
        out_specs=(
            P("shard", "seq", None),
            P("shard", "seq", None),
            P("shard"),
            P("shard", None),
            P("shard", None),
            P("shard"),
            P("shard", None),
            P("shard", None),
        ),
        check_vma=False,
    )
```

```python
import functools

import jax
import jax.numpy as jnp
from jax import lax
from jax.experimental import pallas as pl
from jax.experimental.pallas import tpu as pltpu
from jax.sharding import PartitionSpec as P

HEADS = 12
HEAD_DIM = 64
FF = 1152
HALF = 64
CHIPS = 4
CORES = 2
MEMBERS = CHIPS * CORES
PLANES = 4
EXTRA = 16
f32 = jnp.float32
bf16 = jnp.bfloat16
SCALE = HEAD_DIM ** (-0.5)
VMEM = 20 * 1024 * 1024


def dot(left, right):
    return lax.dot_general(left, right, (((1,), (0,)), ((), ())), preferred_element_type=f32)


def dot_t(left, right):
    return lax.dot_general(left, right, (((1,), (1,)), ((), ())), preferred_element_type=f32)


def t_dot(left, right):
    return lax.dot_general(left, right, (((0,), (0,)), ((), ())), preferred_element_type=f32)


def swap_seq(value, bits):
    count = lax.axis_size("seq")
    return lax.ppermute(value, "seq", [(i, i ^ bits) for i in range(count)])


def swap_shard(value, bits):
    count = lax.axis_size("shard")
    return lax.ppermute(value, "shard", [(i, i ^ bits) for i in range(count)])


def swap_core(value):
    return swap_seq(value, 1)


def over_chips(value):
    return [value] + [swap_seq(value, CORES * j) for j in range(1, CHIPS)]


def over_planes(value):
    return [value] + [swap_shard(value, i) for i in range(1, PLANES)]


def shape(*dims, dtype=bf16):
    return jax.ShapeDtypeStruct(dims, dtype)


def places():
    me = lax.axis_index("seq")
    return (me % MEMBERS) // CORES, me % CORES, lax.axis_index("shard")


def call(kernel, name, outs, *operands, after=(), scratch=(), flops=1e6):
    taken = len(operands)
    specs = [pl.BlockSpec(memory_space=pltpu.VMEM)] * taken
    specs += [pl.BlockSpec(memory_space=pl.ANY)] * len(after)

    def body(*refs):
        kernel(places(), *refs[:taken], *refs[taken + len(after) :])

    moved = sum(o.size * o.dtype.itemsize for o in operands)
    return pl.pallas_call(
        body,
        out_shape=outs,
        in_specs=specs,
        out_specs=jax.tree.map(lambda _: pl.BlockSpec(memory_space=pltpu.VMEM), outs),
        scratch_shapes=list(scratch),
        cost_estimate=pl.CostEstimate(
            flops=int(flops), bytes_accessed=int(moved), transcendentals=0
        ),
        compiler_params=pltpu.CompilerParams(vmem_limit_bytes=VMEM),
        name=name,
    )(*operands, *after)


def norm_parts(values):
    center = values - jnp.mean(values, axis=-1, keepdims=True)
    factor = lax.rsqrt(jnp.mean(center * center, axis=-1, keepdims=True) + 1e-05)
    return center * factor, factor


def norm_inward(upward, gain, normed, factor):
    scaled = upward * gain
    return factor * (
        scaled
        - jnp.mean(scaled, axis=-1, keepdims=True)
        - normed * jnp.mean(scaled * normed, axis=-1, keepdims=True)
    )


def first_half(shape_of):
    return lax.broadcasted_iota(jnp.int32, shape_of, 1) % HEAD_DIM < HEAD_DIM // 2


def shifted(values):
    return pltpu.roll(values, 96, 1), pltpu.roll(values, 32, 1)


def rows_at(start, size):
    return pl.ds(pl.multiple_of(start, 16), size)


def extra_rows(first, second, lanes):
    row = lax.broadcasted_iota(jnp.int32, (EXTRA, lanes), 0)
    pad = jnp.zeros((1, lanes - first.shape[1]), f32)
    first = jnp.concatenate([first, pad], axis=1)
    second = jnp.concatenate([second, pad], axis=1)
    return jnp.where(row == 0, first, jnp.where(row == 1, second, 0.0))


def qkv_piece_kernel(where, w_qkv, gain_one, gain_two, out):
    half = w_qkv.shape[0] // CORES
    width = w_qkv.shape[1] // 3
    local = width // CHIPS
    rows = rows_at(where[1] * half, half)
    for b in range(CHIPS):

        @pl.when(where[0] == b)
        def _():
            for p in range(3):
                at = p * width + b * local
                out[:half, p * local : (p + 1) * local] = w_qkv[rows, at : at + local]

    out[half:, :] = extra_rows(
        gain_one[...].astype(f32)[None], gain_two[...].astype(f32)[None], 3 * local
    ).astype(bf16)


def ffn_piece_kernel(where, w_in, w_out, w_back, cotangent, out, upward):
    upward[...] = cotangent[...]
    half = w_in.shape[0] // CORES
    width = w_out.shape[1]
    units = FF // PLANES // CHIPS
    rows = rows_at(where[1] * half, half)
    lanes = width // CORES
    at_out = 2 * PLANES * units
    at_back = at_out + width
    out[:, at_out:at_back] = w_out[rows, :]
    out[units:, at_back:] = jnp.zeros((half - units, lanes), bf16)
    for b in range(CHIPS):

        @pl.when(where[0] == b)
        def _():
            for p in range(2):
                for z in range(PLANES):
                    at = p * FF + z * units * CHIPS + b * units
                    to = (p * PLANES + z) * units
                    out[:, to : to + units] = w_in[rows, at : at + units]
            for k in range(CORES):

                @pl.when(where[1] == k)
                def _():
                    out[:units, at_back:] = w_back[b * units : (b + 1) * units, k * lanes : (k + 1) * lanes]


def place_kernel(slot, where, p0, p1, p2, p3, out):
    for i, ref in enumerate((p0, p1, p2, p3)):
        out[where[slot] ^ i] = ref[...]


def qkv_kernel(where, x0, x1, x2, x3, mine, other, cos, sin, a_out, q_out, kv_out, w_out, g_out):
    rows = x0.shape[0]
    half = mine.shape[1] - EXTRA
    local = mine.shape[2] // 3
    share = CORES * half
    core = where[1]
    for z in range(PLANES):
        w_out[rows_at(z * share + core * half, half), :] = mine[z, :half, :]
        w_out[rows_at(z * share + (1 - core) * half, half), :] = other[z, :half, :]
        tail = mine[z, half:, :share].astype(f32)
        g_out[:, z * share : (z + 1) * share] = tail[:8]
    gain = g_out[0:1, :]
    for j, ref in enumerate((x0, x1, x2, x3)):
        normed, _ = norm_parts(ref[...].astype(f32))
        a_out[j * rows : (j + 1) * rows, :] = (normed * gain).astype(bf16)
    out = dot(a_out[...], w_out[...])
    front = first_half((CHIPS * rows, 128))
    parts = []
    for at in range(0, 2 * local, 128):
        u = out[:, at : at + 128]
        up, down = shifted(u)
        parts.append((u * cos[...] + jnp.where(front, -up, down) * sin[...]).astype(bf16))
    qk = jnp.concatenate(parts, axis=1)
    value = out[:, 2 * local :].astype(bf16)
    for j in range(CHIPS):
        at = slice(j * rows, (j + 1) * rows)
        q_out[j] = qk[at, :local]
        kv_out[j, :, :local] = qk[at, local:]
        kv_out[j, :, local:] = value[at]


def extended(where, j, kv, other, rim):
    chip, core = where[0], where[1]
    length = kv.shape[1]
    b = chip ^ j
    below = jnp.where(core == 0, jnp.maximum(b - 1, 0), b) ^ chip
    above = jnp.where(core == 0, b, jnp.minimum(b + 1, CHIPS - 1)) ^ chip
    before = other[below, length - HALF :, :]
    after = other[above, :HALF, :]
    if rim is not None:
        before = jnp.where((core == 0) & (b == 0), rim[...], before)
        after = jnp.where((core == 1) & (b == CHIPS - 1), rim[...], after)
    return jnp.concatenate([before, kv[j], after], axis=0)


def probs_of(q, k, bias):
    logits = dot_t(q, k) * SCALE + bias
    highest = jnp.max(logits, axis=-1, keepdims=True)
    exponent = jnp.exp(logits - highest)
    return exponent / jnp.sum(exponent, axis=-1, keepdims=True)


def attend_kernel(edges, where, q, kv, other, bias, *rest):
    rim, out = rest if edges else (None, rest[0])
    local = q.shape[-1]
    for j in range(CHIPS):
        ext = extended(where, j, kv, other, rim)
        parts = []
        for h in range(local // HEAD_DIM):
            lanes = slice(h * HEAD_DIM, (h + 1) * HEAD_DIM)
            prob = probs_of(q[j, :, lanes], ext[:, lanes], bias[j]).astype(bf16)
            parts.append(dot(prob, ext[:, local + h * HEAD_DIM : local + (h + 1) * HEAD_DIM]))
        out[j] = jnp.concatenate(parts, axis=1).astype(bf16)


def ffn_kernel(
    where, t0, t1, t2, t3, x0, x1, x2, x3, y0, y1, y2, y3, mine, other, gains,
    own_out, d1_out, d2_out, d3_out, hid_out, a_out, m_out, dgu_out, gain_out, wb_out, wc_out,
    wi, wo,
):
    chip, core = where[0], where[1]
    rows = x0.shape[0]
    width = x0.shape[1]
    half = mine.shape[1]
    share = CORES * half
    units = FF // CHIPS
    part = units // PLANES
    lanes = width // CORES
    local = width // CHIPS
    at_out, at_back = 2 * units, 2 * units + width
    for z in range(PLANES):
        for k, ref in ((core, mine), (1 - core, other)):
            wi[rows_at(z * share + k * half, half), :] = ref[z, :, :at_out]
            wo[rows_at(z * share + k * half, half), :] = ref[z, :, at_out:at_back]
    own_back = jnp.concatenate([mine[z, :part, at_back:] for z in range(PLANES)], axis=0)
    other_back = jnp.concatenate([other[z, :part, at_back:] for z in range(PLANES)], axis=0)
    wb_out[:, :lanes] = jnp.where(core == 0, own_back, other_back)
    wb_out[:, lanes:] = jnp.where(core == 0, other_back, own_back)
    wc_out[...] = wo[rows_at(chip * local, local), :]
    xs = (x0, x1, x2, x3)
    gain = gains[1:2, :]
    outward = [
        (ref, wo[rows_at((chip ^ i) * local, local), :]) for i, ref in enumerate((t0, t1, t2, t3))
    ]
    normed = []
    for j in range(CHIPS):
        hidden = xs[j][...].astype(f32)
        for i, (ref, weight) in enumerate(outward):
            hidden = hidden + dot(ref[j ^ i], weight)
        if j == 0:
            hid_out[...] = hidden
        norm, _ = norm_parts(hidden)
        normed.append(norm)
        a_out[j * rows : (j + 1) * rows, :] = (norm * gain).astype(bf16)
    total = jnp.zeros((1, width), f32)
    for j in range(CHIPS):
        at = slice(j * rows, (j + 1) * rows)
        gu = dot(a_out[at, :], wi[...])
        entering, gating = gu[:, :units], gu[:, units:]
        rise = 0.5 * (1.0 + lax.erf(entering * (0.5**0.5)))
        slope = rise + entering * jnp.exp(-0.5 * entering * entering) * 0.3989422804014327
        act = entering * rise
        m_out[at, :] = (act * gating).astype(bf16)
        dm = dot_t((y0, y1, y2, y3)[j][...], wb_out[...])
        dgu = jnp.concatenate([dm * gating * slope, dm * act], axis=1).astype(bf16)
        dgu_out[at, :] = dgu
        da = dot_t(dgu, wi[...])
        total = total + jnp.sum(da * normed[j], axis=0, keepdims=True)
        if j == 0:
            own_out[...] = da
        else:
            (d1_out, d2_out, d3_out)[j - 1][...] = da.astype(bf16)
    gain_out[...] = jnp.broadcast_to(total, gain_out.shape)


def ffn_grads_kernel(where, a, m, dgu, y0, y1, y2, y3, wb, keep, away, mixed_own, m1, m2, m3, gin, gb):
    core = where[1]
    rows = y0.shape[0]
    half = keep.shape[1]
    share = CORES * half
    units = m.shape[1]
    part = units // PLANES
    lanes = y0.shape[1] // CORES
    gin[...] = t_dot(a[...], dgu[...])
    upward = jnp.concatenate([ref[...] for ref in (y0, y1, y2, y3)], axis=0)
    back = t_dot(m[...], upward)
    first, second = back[:, :lanes], back[:, lanes:]
    gb[0] = jnp.where(core == 0, first, second)
    gb[1] = jnp.where(core == 0, second, first)
    for z in range(PLANES):
        at = slice(z * part, (z + 1) * part)
        blank = jnp.zeros((half - part, lanes), f32)
        keep[z, :, : 2 * units] = gin[rows_at(z * share + core * half, half), :]
        keep[z, :, 2 * units :] = jnp.concatenate([gb[0, at, :], blank], axis=0)
        away[z, :, : 2 * units] = gin[rows_at(z * share + (1 - core) * half, half), :].astype(bf16)
        away[z, :, 2 * units :] = jnp.concatenate([gb[1, at, :], blank], axis=0).astype(bf16)
    mixed_own[...] = dot(m[:rows, :], wb[...])
    for j, ref in enumerate((m1, m2, m3)):
        ref[...] = dot(m[(j + 1) * rows : (j + 2) * rows, :], wb[...]).astype(bf16)


def dh_kernel(where, own, r1, r2, r3, y0, hidden, gains, dh_out, low_out):
    total = own[...] + r1[...].astype(f32) + r2[...].astype(f32) + r3[...].astype(f32)
    normed, factor = norm_parts(hidden[...])
    dh = y0[...].astype(f32) + norm_inward(total, gains[1:2, :], normed, factor)
    dh_out[...] = dh
    low_out[...] = dh.astype(bf16)


def attend_back_kernel(edges, where, q, kv, other, bias, h0, h1, h2, h3, w_out, *rest):
    rim, rest = (rest[0], rest[1:]) if edges else (None, rest)
    dq_out, dkv_out, back_out = rest[:3]
    chip, core = where[0], where[1]
    local = q.shape[-1]
    length = q.shape[1]
    back_out[...] = jnp.zeros_like(back_out)
    for j, dh in enumerate((h0, h1, h2, h3)):
        dctx = dot_t(dh[...], w_out[...]).astype(bf16)
        ext = extended(where, j, kv, other, rim)
        dqs, dks, dvs = [], [], []
        for h in range(local // HEAD_DIM):
            lanes = slice(h * HEAD_DIM, (h + 1) * HEAD_DIM)
            qh = q[j, :, lanes]
            kh = ext[:, lanes]
            vh = ext[:, local + h * HEAD_DIM : local + (h + 1) * HEAD_DIM]
            dch = dctx[:, lanes]
            prob = probs_of(qh, kh, bias[j])
            dprob = dot_t(dch, vh)
            inner = jnp.sum(prob * dprob, axis=-1, keepdims=True)
            dscore = (prob * (dprob - inner) * SCALE).astype(bf16)
            dqs.append(dot(dscore, kh))
            dks.append(t_dot(dscore, qh))
            dvs.append(t_dot(prob.astype(bf16), dch))
        dq_out[j] = jnp.concatenate(dqs, axis=1)
        grads = jnp.concatenate(dks + dvs, axis=1)
        dkv_out[j] = grads[HALF : HALF + length]
        before = grads[:HALF].astype(bf16)
        after = grads[HALF + length :].astype(bf16)
        b = chip ^ j
        below = jnp.where(core == 0, b - 1, b)
        above = jnp.where(core == 0, b, b + 1)

        @pl.when(below >= 0)
        def _():
            back_out[jnp.maximum(below, 0) ^ chip, length - HALF :, :] = before

        @pl.when(above < CHIPS)
        def _():
            back_out[jnp.minimum(above, CHIPS - 1) ^ chip, :HALF, :] = after

        if edges:
            rim_out = rest[3]

            @pl.when(below < 0)
            def _():
                rim_out[...] = before

            @pl.when(above >= CHIPS)
            def _():
                rim_out[...] = after


def qkv_grads_kernel(edges, where, dq, dkv, back, cos, sin, a, t0, t1, t2, t3, h0, h1, h2, h3, *rest):
    rim, rest = (rest[0], rest[1:]) if edges else (None, rest)
    keep, away, d_out, acc, cols = rest
    chip, core = where[0], where[1]
    length = dq.shape[1]
    local = dq.shape[2]
    width = a.shape[1]
    front = first_half((length, 128))
    for j in range(CHIPS):
        at = slice(j * length, (j + 1) * length)
        gkv = dkv[j] + back[j].astype(f32)
        if edges:
            b = chip ^ j
            blank = jnp.zeros((length - HALF, 2 * local), f32)
            value = rim[...].astype(f32)
            gkv = gkv + jnp.where(
                (core == 0) & (b == 0), jnp.concatenate([value, blank], axis=0), 0.0
            )
            gkv = gkv + jnp.where(
                (core == 1) & (b == CHIPS - 1), jnp.concatenate([blank, value], axis=0), 0.0
            )
        g = jnp.concatenate([dq[j], gkv[:, :local]], axis=1)
        for lane in range(0, 2 * local, 128):
            u = g[:, lane : lane + 128]
            up, down = shifted(u * sin[at, :])
            d_out[at, lane : lane + 128] = (
                u * cos[at, :] + jnp.where(front, up, -down)
            ).astype(bf16)
        d_out[at, 2 * local :] = gkv[:, local:].astype(bf16)
    acc[:, : 3 * local] = t_dot(a[...], d_out[...])
    for b in range(CHIPS):

        @pl.when(chip == b)
        def _():
            for j, ref in enumerate((h0, h1, h2, h3)):
                cols[j * length : (j + 1) * length, :] = ref[:, b * local : (b + 1) * local]

    for i, ref in enumerate((t0, t1, t2, t3)):
        rows = jnp.concatenate([ref[j ^ i] for j in range(CHIPS)], axis=0)
        acc[rows_at((chip ^ i) * local, local), 3 * local :] = t_dot(rows, cols[...])
    half = keep.shape[1]
    share = CORES * half
    for z in range(PLANES):
        keep[z] = acc[rows_at(z * share + core * half, half), :]
        away[z] = acc[rows_at(z * share + (1 - core) * half, half), :].astype(bf16)


def da_kernel(where, d, w, x0, x1, x2, x3, own_mixed, m1, m2, m3, gain_two, own_out, o1, o2, o3, gain_out):
    rows = x0.shape[0]
    total = jnp.zeros((1, w.shape[0]), f32)
    for j, ref in enumerate((x0, x1, x2, x3)):
        da = dot_t(d[j * rows : (j + 1) * rows, :], w[...])
        normed, _ = norm_parts(ref[...].astype(f32))
        total = total + jnp.sum(da * normed, axis=0, keepdims=True)
        if j == 0:
            own_out[:rows, :] = da
            own_out[rows:, :] = own_mixed[...]
        else:
            out = (o1, o2, o3)[j - 1]
            out[:rows, :] = da.astype(bf16)
            out[rows:, :] = (m1, m2, m3)[j - 1][...]
    share = w.shape[0] // PLANES
    for z in range(PLANES):
        at = slice(z * share, (z + 1) * share)
        gain_out[z] = extra_rows(total[:, at], gain_two[0:1, at], gain_out.shape[2])


def to_planes_kernel(where, keep, got, own, o1, o2, o3):
    plane = where[2]
    own[...] = keep[plane] + got[plane].astype(f32)
    for i, ref in enumerate((o1, o2, o3)):
        at = plane ^ (i + 1)
        ref[...] = (keep[at] + got[at].astype(f32)).astype(bf16)


def to_planes_gains_kernel(where, keep, got, gains, own, o1, o2, o3):
    plane = where[2]
    half = keep.shape[1]
    own[:half, :] = keep[plane] + got[plane].astype(f32)
    own[half:, :] = gains[plane]
    for i, ref in enumerate((o1, o2, o3)):
        at = plane ^ (i + 1)
        ref[:half, :] = (keep[at] + got[at].astype(f32)).astype(bf16)
        ref[half:, :] = gains[at].astype(bf16)


def sum_kernel(where, own, r1, r2, r3, out):
    total = own[...] + r1[...].astype(f32) + r2[...].astype(f32) + r3[...].astype(f32)
    out[...] = total.astype(out.dtype)


def last_kernel(where, own, r1, r2, r3, x0, dh, hidden, gains, mixed_out, grad_out):
    rows = dh.shape[0]
    total = own[...] + r1[...].astype(f32) + r2[...].astype(f32) + r3[...].astype(f32)
    mixed_out[0] = (hidden[...] + total[rows:, :]).astype(bf16)
    normed, factor = norm_parts(x0[...].astype(f32))
    grad = dh[...] + norm_inward(total[:rows, :], gains[0:1, :], normed, factor)
    grad_out[0] = grad.astype(bf16)


def ffn_owned_kernel(where, mine, other, in_out, back_out):
    core = where[1]
    half = mine.shape[1]
    units = FF // CHIPS
    part = units // PLANES
    lanes = mine.shape[2] - 2 * units
    for k, ref in ((core, mine), (1 - core, other)):
        rows = rows_at(k * half, half)
        for p in range(2):
            for z in range(PLANES):
                at = (p * PLANES + z) * part
                for b in range(CHIPS):
                    to = p * FF + (z * CHIPS + b) * part
                    in_out[rows, to : to + part] = ref[b, :, at : at + part].astype(f32)
    for b in range(CHIPS):
        own = mine[b, :part, 2 * units :].astype(f32)
        got = other[b, :part, 2 * units :].astype(f32)
        back_out[b * part : (b + 1) * part, :lanes] = jnp.where(core == 0, own, got)
        back_out[b * part : (b + 1) * part, lanes:] = jnp.where(core == 0, got, own)


def qkv_owned_kernel(where, mine, other, qkv_out, w_out, gain_out):
    core = where[1]
    half = mine.shape[1] - EXTRA
    local = w_out.shape[1] // CHIPS
    total = jnp.zeros((EXTRA, local), f32)
    for k, ref in ((core, mine), (1 - core, other)):
        rows = rows_at(k * half, half)
        for b in range(CHIPS):
            for p in range(3):
                to = (p * CHIPS + b) * local
                qkv_out[rows, to : to + local] = ref[b, :half, p * local : (p + 1) * local].astype(f32)
            w_out[rows, b * local : (b + 1) * local] = ref[b, :half, 3 * local :].astype(f32)
            total = total + ref[b, half:, :local].astype(f32)
    gain_out[...] = total


def shards(tokens, norm_gain, w_qkv, w_out, ffn_gain, w_in, w_back, seq_ids, cotangent):
    length, width = tokens.shape[1:]
    me = lax.axis_index("seq")
    seq_count = lax.axis_size("seq")
    edges = seq_count > MEMBERS
    group = me // MEMBERS
    chip = (me % MEMBERS) // CORES
    core = me % CORES
    local = width // CHIPS
    units = FF // CHIPS
    many = CHIPS * length
    half = width // PLANES // CORES
    lanes = width // CORES
    extent = length + 2 * HALF
    kept = half + EXTRA
    in_lanes = 2 * units + width + lanes
    ffn_lanes = 2 * units + lanes
    qkv_lanes = 4 * local

    piece = call(
        qkv_piece_kernel, "qkv_piece", shape(kept, 3 * local), w_qkv, norm_gain, ffn_gain
    )
    pieces = over_planes(piece)
    xs = over_chips(tokens[0])
    piece, upward = call(
        ffn_piece_kernel,
        "ffn_piece",
        (shape(half, in_lanes), shape(length, width)),
        w_in,
        w_out,
        w_back,
        cotangent[0],
        after=(piece,),
    )
    in_pieces = over_planes(piece)
    gys = over_chips(upward)
    mine = call(
        functools.partial(place_kernel, 2), "qkv_place", shape(PLANES, kept, 3 * local), *pieces
    )
    other = swap_core(mine)

    block = (group * CHIPS + (chip ^ jnp.arange(CHIPS))) * CORES + core
    position = (block[:, None] * length + jnp.arange(length)[None]).astype(f32).reshape(many)
    frequency = 10000.0 ** (-jnp.arange(0, HEAD_DIM, 2).astype(f32) / HEAD_DIM)
    angles = position[:, None] * frequency[None]
    cosine, sine = lax.optimization_barrier((jnp.cos(angles), jnp.sin(angles)))
    cosine = jnp.tile(cosine, (1, 4))
    sine = jnp.tile(sine, (1, 4))
    spans = length // HALF
    ids = jnp.pad(seq_ids[0], (1, 1), constant_values=-1)
    key_ids = jnp.stack(
        [lax.dynamic_slice_in_dim(ids, block[j] * spans, spans + 2, 0) for j in range(CHIPS)]
    )
    key_ids = jnp.repeat(key_ids, HALF, axis=1)
    query_ids = key_ids[:, HALF : HALF + length]
    offset = jnp.arange(extent)[None, :] - HALF - jnp.arange(length)[:, None]
    allowed = (jnp.abs(offset) <= HALF)[None] & (query_ids[:, :, None] == key_ids[:, None, :])
    bias = jnp.where(allowed, 0.0, -1e30).astype(f32)

    low_one, query, kv, wq, gains = call(
        qkv_kernel,
        "qkv",
        (
            shape(many, width),
            shape(CHIPS, length, local),
            shape(CHIPS, length, 2 * local),
            shape(width, 3 * local),
            shape(8, width, dtype=f32),
        ),
        *xs,
        mine,
        other,
        cosine,
        sine,
                flops=2 * many * width * 3 * local,
    )
    kv_other = swap_core(kv)

    def beyond(value):
        pairs = []
        for m in range(seq_count):
            to = m - MEMBERS + 1 if m % CORES == 0 else m + MEMBERS - 1
            if 0 <= to < seq_count:
                pairs.append((m, to))
        return lax.ppermute(value, "seq", pairs)

    rim = ()
    if edges:
        first = lax.dynamic_index_in_dim(kv, chip, 0, False)[:HALF]
        last = lax.dynamic_index_in_dim(kv, chip ^ (CHIPS - 1), 0, False)[length - HALF :]
        rim = (beyond(jnp.where(core == 0, first, last)),)

    attn = call(
        functools.partial(attend_kernel, edges),
        "attend",
        shape(CHIPS, length, local),
        query,
        kv,
        kv_other,
        bias,
        *rim,
                flops=4 * many * extent * local,
    )
    attns = over_chips(attn)
    mine = call(
        functools.partial(place_kernel, 2), "ffn_place", shape(PLANES, half, in_lanes), *in_pieces, after=(attns[1],)
    )
    other = swap_core(mine)
    own, d1, d2, d3, hidden, low_two, hidden_low, grad_expanded, gain_two, wb, wo = call(
        ffn_kernel,
        "ffn",
        (shape(length, width, dtype=f32),)
        + (shape(length, width),) * 3
        + (
            shape(length, width, dtype=f32),
            shape(many, width),
            shape(many, units),
            shape(many, 2 * units),
            shape(8, width, dtype=f32),
            shape(units, width),
            shape(local, width),
        ),
        *attns,
        *xs,
        *gys,
        mine,
        other,
        gains,
                scratch=(pltpu.VMEM((width, 2 * units), bf16), pltpu.VMEM((width, width), bf16)),
        flops=2 * many * width * (width + 5 * units),
    )
    received = [swap_seq(d, CORES * (j + 1)) for j, d in enumerate((d1, d2, d3))]
    keep_ffn, away, mixed_own, mixed1, mixed2, mixed3 = call(
        ffn_grads_kernel,
        "ffn_grads",
        (shape(PLANES, half, ffn_lanes, dtype=f32), shape(PLANES, half, ffn_lanes))
        + (shape(length, width, dtype=f32),)
        + (shape(length, width),) * 3,
        low_two,
        hidden_low,
        grad_expanded,
        *gys,
        wb,
                scratch=(pltpu.VMEM((width, 2 * units), f32), pltpu.VMEM((CORES, units, lanes), f32)),
        flops=2 * many * width * 4 * units,
    )
    got_ffn = swap_core(away)
    dh, dh_low = call(
        dh_kernel, "dh", (shape(length, width, dtype=f32), shape(length, width)), own, *received, gys[0], hidden, gains, after=(away,)
    )
    dhs = over_chips(dh_low)
    sent_ffn = call(
        to_planes_kernel,
        "ffn_to_planes",
        (shape(half, ffn_lanes, dtype=f32),) + (shape(half, ffn_lanes),) * 3,
        keep_ffn,
        got_ffn,
        after=(dh_low,),
            )
    got_ffn = [swap_shard(s, i + 1) for i, s in enumerate(sent_ffn[1:])]

    backs = call(
        functools.partial(attend_back_kernel, edges),
        "attend_back",
        (
            shape(CHIPS, length, local, dtype=f32),
            shape(CHIPS, length, 2 * local, dtype=f32),
            shape(CHIPS, length, 2 * local),
        )
        + ((shape(HALF, 2 * local),) if edges else ()),
        query,
        kv,
        kv_other,
        bias,
        *dhs,
        wo,
        *rim,
        after=(sent_ffn[1],),
                flops=10 * many * extent * local,
    )
    dq, dkv, back = backs[:3]
    back = swap_core(back)
    if edges:
        rim = (beyond(backs[3]),)

    def over_groups(total, kept_type):
        step = MEMBERS
        while step < seq_count:
            total = total + swap_seq(total.astype(bf16), step).astype(f32)
            step *= 2
        return total.astype(kept_type)

    def summed(own, parts, name, after=()):
        out = call(
            sum_kernel, name, shape(*own.shape, dtype=f32 if edges else bf16), own, *parts, after=after
        )
        return over_groups(out, bf16)

    pieces_ffn = over_chips(summed(sent_ffn[0], got_ffn, "ffn_sum", (dq,)))

    keep, away, dqkv = call(
        functools.partial(qkv_grads_kernel, edges),
        "qkv_grads",
        (
            shape(PLANES, half, qkv_lanes, dtype=f32),
            shape(PLANES, half, qkv_lanes),
            shape(many, 3 * local),
        ),
        dq,
        dkv,
        back,
        cosine,
        sine,
        low_one,
        *attns,
        *dhs,
        *rim,
                scratch=(pltpu.VMEM((width, qkv_lanes), f32), pltpu.VMEM((many, local), bf16)),
        flops=2 * many * width * 4 * local,
    )
    got = swap_core(away)
    last_own, o1, o2, o3, gain_sums = call(
        da_kernel,
        "da",
        (shape(2 * length, width, dtype=f32),)
        + (shape(2 * length, width),) * 3
        + (shape(PLANES, EXTRA, qkv_lanes, dtype=f32),),
        dqkv,
        wq,
        *xs,
        mixed_own,
        mixed1,
        mixed2,
        mixed3,
        gain_two,
        flops=2 * many * width * 3 * local,
    )
    received = [swap_seq(o, CORES * (j + 1)) for j, o in enumerate((o1, o2, o3))]
    sent = call(
        to_planes_gains_kernel,
        "qkv_to_planes",
        (shape(kept, qkv_lanes, dtype=f32),) + (shape(kept, qkv_lanes),) * 3,
        keep,
        got,
        gain_sums,
            )
    got = [swap_shard(s, i + 1) for i, s in enumerate(sent[1:])]

    mine = call(
        functools.partial(place_kernel, 0),
        "ffn_gather",
        shape(CHIPS, half, ffn_lanes),
        *pieces_ffn,
        after=(sent[1],),
            )
    owned_in, owned_back = call(
        ffn_owned_kernel,
        "ffn_owned",
        (shape(*w_in.shape, dtype=f32), shape(*w_back.shape, dtype=f32)),
        mine,
        swap_core(mine),
            )
    mixed, grad_tokens = call(
        last_kernel,
        "last",
        (shape(1, length, width), shape(1, length, width)),
        last_own,
        *received,
        xs[0],
        dh,
        hidden,
        gains,
        after=(sent[1],),
    )
    mine = call(
        functools.partial(place_kernel, 0),
        "qkv_gather",
        shape(CHIPS, kept, qkv_lanes),
        *over_chips(summed(sent[0], got, "qkv_sum")),
            )
    owned_qkv, owned_out, gain_sums = call(
        qkv_owned_kernel,
        "qkv_owned",
        (
            shape(*w_qkv.shape, dtype=f32),
            shape(*w_out.shape, dtype=f32),
            shape(EXTRA, local, dtype=f32),
        ),
        mine,
        swap_core(mine),
            )
    return (mixed, grad_tokens, gain_sums[0], owned_qkv, owned_out, gain_sums[1], owned_in, owned_back)


def solution(mesh):
    return jax.shard_map(
        shards,
        mesh=mesh,
        in_specs=(
            P("shard", "seq", None),
            P("shard"),
            P("shard", None),
            P("shard", None),
            P("shard"),
            P("shard", None),
            P("shard", None),
            P("shard", None),
            P("shard", "seq", None),
        ),
        out_specs=(
            P("shard", "seq", None),
            P("shard", "seq", None),
            P("shard"),
            P("shard", None),
            P("shard", None),
            P("shard"),
            P("shard", None),
            P("shard", None),
        ),
        check_vma=False,
    )
```

```python
import functools
import math

import jax
import jax.numpy as jnp
from jax import lax
from jax.experimental import pallas as pl
from jax.experimental.pallas import tpu as pltpu
from jax.sharding import PartitionSpec as P

HEADS = 12
HEAD_DIM = 64
FF = 1152
HALF = 64
CHIPS = 4
CORES = 2
MEMBERS = CHIPS * CORES
PLANES = 4
EXTRA = 16
f32 = jnp.float32
bf16 = jnp.bfloat16
SCALE = HEAD_DIM ** (-0.5)
ROOM = 6 * 1024 * 1024


TIMES = {
    "qkv_piece": 0.5,
    "ffn_piece": 1,
    "qkv_place": 0.8,
    "qkv": 1.6,
    "attend": 2.3,
    "ffn_place": 1.2,
    "ffn": 4.5,
    "ffn_grads": 1.6,
    "dh": 0.4,
    "mixed": 0.6,
    "ffn_split": 1,
    "mixed_sum": 0.4,
    "attend_back": 6.9,
    "qkv_grads": 2.4,
    "da": 1.5,
    "qkv_to_planes": 0.8,
    "qkv_gather": 0.6,
    "last": 0.6,
    "ffn_owned": 2.2,
    "qkv_owned": 1.7,
}


def dot(left, right):
    return lax.dot_general(left, right, (((1,), (0,)), ((), ())), preferred_element_type=f32)


def dot_t(left, right):
    return lax.dot_general(left, right, (((1,), (1,)), ((), ())), preferred_element_type=f32)


def t_dot(left, right):
    return lax.dot_general(left, right, (((0,), (0,)), ((), ())), preferred_element_type=f32)


def swap_seq(value, bits):
    count = lax.axis_size("seq")
    return lax.ppermute(value, "seq", [(i, i ^ bits) for i in range(count)])


def swap_shard(value, bits):
    count = lax.axis_size("shard")
    return lax.ppermute(value, "shard", [(i, i ^ bits) for i in range(count)])


def swap_core(value):
    return swap_seq(value, 1)


def over_chips(value):
    return [value] + [swap_seq(value, CORES * j) for j in range(1, CHIPS)]


def over_planes(value):
    return [value] + [swap_shard(value, i) for i in range(1, PLANES)]


def shape(*dims, dtype=bf16):
    return jax.ShapeDtypeStruct(dims, dtype)


def places():
    me = lax.axis_index("seq")
    return (me % MEMBERS) // CORES, me % CORES, lax.axis_index("shard")


def size_of(value):
    return math.prod(value.shape) * jnp.dtype(value.dtype).itemsize


def call(kernel, name, outs, *operands, after=(), scratch=(), held=0):
    taken = len(operands)
    specs = [pl.BlockSpec(memory_space=pltpu.HBM)] * held
    specs += [pl.BlockSpec(memory_space=pltpu.VMEM)] * (taken - held)
    specs += [pl.BlockSpec(memory_space=pl.ANY)] * len(after)
    us = TIMES.get(name, 0.5)
    held_size = sum(size_of(o) for o in operands[held:])
    held_size += sum(size_of(o) for o in jax.tree.leaves(outs))

    def body(*refs):
        kernel(places(), *refs[:taken], *refs[taken + len(after) :])

    return pl.pallas_call(
        body,
        out_shape=outs,
        in_specs=specs,
        out_specs=jax.tree.map(lambda _: pl.BlockSpec(memory_space=pltpu.VMEM), outs),
        scratch_shapes=list(scratch),
        cost_estimate=pl.CostEstimate(
            flops=int(us * 2e10), bytes_accessed=int(us * 10), transcendentals=0
        ),
        compiler_params=pltpu.CompilerParams(vmem_limit_bytes=2 * held_size + ROOM),
        name=name,
    )(*operands, *after)


def norm_parts(values):
    center = values - jnp.mean(values, axis=-1, keepdims=True)
    factor = lax.rsqrt(jnp.mean(center * center, axis=-1, keepdims=True) + 1e-05)
    return center * factor, factor


def norm_inward(upward, gain, normed, factor):
    scaled = upward * gain
    return factor * (
        scaled
        - jnp.mean(scaled, axis=-1, keepdims=True)
        - normed * jnp.mean(scaled * normed, axis=-1, keepdims=True)
    )


def first_half(shape_of):
    return lax.broadcasted_iota(jnp.int32, shape_of, 1) % HEAD_DIM < HEAD_DIM // 2


def shifted(values):
    return pltpu.roll(values, 96, 1), pltpu.roll(values, 32, 1)


def rows_at(start, size):
    return pl.ds(pl.multiple_of(start, 16), size)


def lanes_at(start, size):
    return pl.ds(pl.multiple_of(start, 128), size)


def extra_rows(first, second, lanes):
    row = lax.broadcasted_iota(jnp.int32, (EXTRA, lanes), 0)
    pad = jnp.zeros((1, lanes - first.shape[1]), f32)
    first = jnp.concatenate([first, pad], axis=1)
    second = jnp.concatenate([second, pad], axis=1)
    return jnp.where(row == 0, first, jnp.where(row == 1, second, 0.0))


def copied(pairs, sems):
    copies = [pltpu.make_async_copy(src, dst, sems.at[i]) for i, (src, dst) in enumerate(pairs)]
    for copy in copies:
        copy.start()
    for copy in copies:
        copy.wait()


def qkv_piece_kernel(where, w_qkv, w_out, gain_one, gain_two, out, rows, part, sems):
    chip, core = where[0], where[1]
    half = w_qkv.shape[0] // CORES
    width = w_qkv.shape[1] // 3
    local = width // CHIPS
    size, lanes = part.shape
    copied(
        (
            (w_qkv.at[rows_at(core * half, half), :], rows),
            (w_out.at[rows_at(chip * size, size), lanes_at(core * lanes, lanes)], part),
        ),
        sems,
    )
    for b in range(CHIPS):

        @pl.when(chip == b)
        def _():
            for p in range(3):
                at = p * width + b * local
                out[:half, p * local : (p + 1) * local] = rows[:, at : at + local]

    out[half : half + EXTRA, :] = extra_rows(
        gain_one[...].astype(f32)[None], gain_two[...].astype(f32)[None], 3 * local
    ).astype(bf16)
    at = half + EXTRA
    out[at : at + 16, :lanes] = part[:16, :]
    out[at + 16 :, :lanes] = part[16:32, :]
    out[at : at + 16, lanes:] = part[32:, :local]
    out[at + 16 :, lanes:] = part[32:, local:]


def ffn_piece_kernel(where, w_in, w_back, out, rows, back, sems):
    chip, core = where[0], where[1]
    half = w_in.shape[0] // CORES
    units = FF // PLANES // CHIPS
    lanes = back.shape[1]
    copied(
        (
            (w_in.at[rows_at(core * half, half), :], rows),
            (w_back.at[:, lanes_at(core * lanes, lanes)], back),
        ),
        sems,
    )
    out[units:, :lanes] = jnp.zeros((half - units, lanes), bf16)
    for b in range(CHIPS):

        @pl.when(chip == b)
        def _():
            for p in range(2):
                for z in range(PLANES):
                    at = p * FF + z * units * CHIPS + b * units
                    to = lanes + (p * PLANES + z) * units
                    out[:, to : to + units] = rows[:, at : at + units]
            out[:units, :lanes] = back[b * units : (b + 1) * units, :]


def place_kernel(slot, where, p0, p1, p2, p3, out):
    for i, ref in enumerate((p0, p1, p2, p3)):
        out[where[slot] ^ i] = ref[...]


def qkv_place_kernel(where, p0, p1, p2, p3, out, packet):
    kept = out.shape[1]
    lanes = packet.shape[2]
    for i, ref in enumerate((p0, p1, p2, p3)):
        z = where[2] ^ i
        out[z] = ref[:kept, :]
        packet[z, :16, :] = ref[kept : kept + 16, :lanes]
        packet[z, 16:32, :] = ref[kept + 16 :, :lanes]
        packet[z, 32:, :] = jnp.concatenate(
            [ref[kept : kept + 16, lanes:], ref[kept + 16 :, lanes:]], axis=1
        )


def up_pair_kernel(where, own, both, out):
    out[0] = own[...]
    out[1] = both[own.shape[0] :, :]


def pair_kernel(where, first, second, out):
    out[0] = first[...]
    out[1] = second[...]


def ffn_place_kernel(where, near, far, p01, p23, out):
    half = near.shape[1]
    p0, p1, p2, p3 = p01.at[0], p01.at[1], p23.at[0], p23.at[1]
    size, lanes = p0.shape[1:]
    for i, ref in enumerate((near.at[0], near.at[1], far.at[0], far.at[1])):
        z = where[2] ^ i
        out[z, :, :lanes] = ref[:, :lanes]
        out[z, :, 3 * lanes :] = ref[:, lanes:]
    for i, ref in enumerate((p0, p1, p2, p3)):
        b = where[0] ^ i
        at = rows_at((b % 2) * size, size)

        for half_at in range(2):

            @pl.when(b // 2 == half_at)
            def _():
                for z in range(PLANES):
                    out[z, at, (half_at + 1) * lanes : (half_at + 2) * lanes] = ref[z]


def qkv_kernel(where, x0, x1, x2, x3, mine, other, cos, sin, a_out, q_out, kv_out, w_out, g_out):
    rows = x0.shape[0]
    half = mine.shape[1] - EXTRA
    local = mine.shape[2] // 3
    share = CORES * half
    core = where[1]
    for z in range(PLANES):
        w_out[rows_at(z * share + core * half, half), :] = mine[z, :half, :]
        w_out[rows_at(z * share + (1 - core) * half, half), :] = other[z, :half, :]
        tail = mine[z, half:, :share].astype(f32)
        g_out[:, z * share : (z + 1) * share] = tail[:8]
    gain = g_out[0:1, :]
    for j, ref in enumerate((x0, x1, x2, x3)):
        normed, _ = norm_parts(ref[:rows, :].astype(f32))
        a_out[j * rows : (j + 1) * rows, :] = (normed * gain).astype(bf16)
    out = dot(a_out[...], w_out[...])
    front = first_half((CHIPS * rows, 128))
    parts = []
    for at in range(0, 2 * local, 128):
        u = out[:, at : at + 128]
        up, down = shifted(u)
        parts.append((u * cos[...] + jnp.where(front, -up, down) * sin[...]).astype(bf16))
    qk = jnp.concatenate(parts, axis=1)
    value = out[:, 2 * local :].astype(bf16)
    for j in range(CHIPS):
        at = slice(j * rows, (j + 1) * rows)
        q_out[j] = qk[at, :local]
        kv_out[j, :, :local] = qk[at, local:]
        kv_out[j, :, local:] = value[at]


def extended(where, j, kv, other, rim):
    chip, core = where[0], where[1]
    length = kv.shape[1]
    b = chip ^ j
    below = jnp.where(core == 0, jnp.maximum(b - 1, 0), b) ^ chip
    above = jnp.where(core == 0, b, jnp.minimum(b + 1, CHIPS - 1)) ^ chip
    before = other[below, length - HALF :, :]
    after = other[above, :HALF, :]
    if rim is not None:
        before = jnp.where((core == 0) & (b == 0), rim[...], before)
        after = jnp.where((core == 1) & (b == CHIPS - 1), rim[...], after)
    return jnp.concatenate([before, kv[j], after], axis=0)


def probs_of(q, k, bias):
    logits = dot_t(q, k) * SCALE + bias
    highest = jnp.max(logits, axis=-1, keepdims=True)
    exponent = jnp.exp(logits - highest)
    return exponent / jnp.sum(exponent, axis=-1, keepdims=True)


def attend_kernel(edges, where, q, kv, other, bias, *rest):
    rim, out = rest if edges else (None, rest[0])
    local = q.shape[-1]
    for j in range(CHIPS):
        ext = extended(where, j, kv, other, rim)
        parts = []
        for h in range(local // HEAD_DIM):
            lanes = slice(h * HEAD_DIM, (h + 1) * HEAD_DIM)
            prob = probs_of(q[j, :, lanes], ext[:, lanes], bias[j]).astype(bf16)
            parts.append(dot(prob, ext[:, local + h * HEAD_DIM : local + (h + 1) * HEAD_DIM]))
        out[j] = jnp.concatenate(parts, axis=1).astype(bf16)


def ffn_kernel(
    where, t0, t1, t2, t3, x0, x1, x2, x3, y02, y13, mine, other, gains,
    own_out, d1_out, d2_out, d3_out, hid_out, a_out, m_out, dgu_out, gain_out, wb_out, wc_out,
    wi, wo,
):
    chip, core = where[0], where[1]
    rows = x0.shape[0]
    width = x0.shape[1]
    half = mine.shape[1]
    share = CORES * half
    units = FF // CHIPS
    part = units // PLANES
    lanes = width // CORES
    local = width // CHIPS
    for z in range(PLANES):
        for k, ref in ((core, mine), (1 - core, other)):
            wi[rows_at(z * share + k * half, half), :] = ref[z, :, 3 * lanes :]
            for p in range(CORES):
                at = slice(z * share + p * half, z * share + (p + 1) * half)
                wo[at, lanes_at(k * lanes, lanes)] = ref[z, :, (p + 1) * lanes : (p + 2) * lanes]
    own_back = jnp.concatenate([mine[z, :part, :lanes] for z in range(PLANES)], axis=0)
    other_back = jnp.concatenate([other[z, :part, :lanes] for z in range(PLANES)], axis=0)
    wb_out[:, :lanes] = jnp.where(core == 0, own_back, other_back)
    wb_out[:, lanes:] = jnp.where(core == 0, other_back, own_back)
    wc_out[...] = wo[rows_at(chip * local, local), :]
    xs = (x0, x1, x2, x3)
    gain = gains[1:2, :]
    outward = [
        (ref, wo[rows_at((chip ^ i) * local, local), :]) for i, ref in enumerate((t0, t1, t2, t3))
    ]
    normed = []
    for j in range(CHIPS):
        hidden = xs[j][:rows, :].astype(f32)
        for i, (ref, weight) in enumerate(outward):
            hidden = hidden + dot(ref[j ^ i], weight)
        if j == 0:
            hid_out[...] = hidden
        norm, _ = norm_parts(hidden)
        normed.append(norm)
        a_out[j * rows : (j + 1) * rows, :] = (norm * gain).astype(bf16)
    total = jnp.zeros((1, width), f32)
    for j in range(CHIPS):
        at = slice(j * rows, (j + 1) * rows)
        gu = dot(a_out[at, :], wi[...])
        entering, gating = gu[:, :units], gu[:, units:]
        rise = 0.5 * (1.0 + lax.erf(entering * (0.5**0.5)))
        slope = rise + entering * jnp.exp(-0.5 * entering * entering) * 0.3989422804014327
        act = entering * rise
        m_out[at, :] = (act * gating).astype(bf16)
        dm = dot_t((y02, y13)[j % 2][j // 2], wb_out[...])
        dgu = jnp.concatenate([dm * gating * slope, dm * act], axis=1).astype(bf16)
        dgu_out[at, :] = dgu
        da = dot_t(dgu, wi[...])
        total = total + jnp.sum(da * normed[j], axis=0, keepdims=True)
        if j == 0:
            own_out[...] = da
        else:
            (d1_out, d2_out, d3_out)[j - 1][...] = da.astype(bf16)
    gain_out[...] = jnp.broadcast_to(total, gain_out.shape)


def mixed_kernel(where, m, wb, own, m1, m2, m3):
    rows = own.shape[0]
    own[...] = dot(m[:rows, :], wb[...])
    for j, ref in enumerate((m1, m2, m3)):
        ref[...] = dot(m[(j + 1) * rows : (j + 2) * rows, :], wb[...]).astype(bf16)


def mixed_sum_kernel(where, own, r1, r2, r3, hidden, out):
    total = own[...] + r1[...].astype(f32) + r2[...].astype(f32) + r3[...].astype(f32)
    out[0] = (hidden[...] + total).astype(bf16)


def ffn_grads_kernel(where, a, m, dgu, y02, y13, keep, away, gin, gb):
    core = where[1]
    half = keep.shape[1]
    share = CORES * half
    units = m.shape[1]
    part = units // PLANES
    lanes = y02.shape[2] // CORES
    gin[...] = t_dot(a[...], dgu[...])
    upward = jnp.concatenate([y02[0], y13[0], y02[1], y13[1]], axis=0)
    back = t_dot(m[...], upward)
    first, second = back[:, :lanes], back[:, lanes:]
    gb[0] = jnp.where(core == 0, first, second)
    gb[1] = jnp.where(core == 0, second, first)
    for z in range(PLANES):
        at = slice(z * part, (z + 1) * part)
        blank = jnp.zeros((half - part, lanes), f32)
        keep[z, :, : 2 * units] = gin[rows_at(z * share + core * half, half), :]
        keep[z, :, 2 * units :] = jnp.concatenate([gb[0, at, :], blank], axis=0)
        away[z, :, : 2 * units] = gin[rows_at(z * share + (1 - core) * half, half), :].astype(bf16)
        away[z, :, 2 * units :] = jnp.concatenate([gb[1, at, :], blank], axis=0).astype(bf16)


def dh_kernel(where, own, r1, r2, r3, y02, hidden, gains, dh_out, low_out):
    total = own[...] + r1[...].astype(f32) + r2[...].astype(f32) + r3[...].astype(f32)
    normed, factor = norm_parts(hidden[...])
    dh = y02[0].astype(f32) + norm_inward(total, gains[1:2, :], normed, factor)
    dh_out[...] = dh
    low_out[...] = dh.astype(bf16)


def attend_back_kernel(edges, where, q, kv, other, bias, h0, h1, h2, h3, w_out, *rest):
    rim, rest = (rest[0], rest[1:]) if edges else (None, rest)
    dq_out, dkv_out, back_out = rest[:3]
    chip, core = where[0], where[1]
    local = q.shape[-1]
    length = q.shape[1]
    back_out[...] = jnp.zeros_like(back_out)
    for j, dh in enumerate((h0, h1, h2, h3)):
        dctx = dot_t(dh[...], w_out[...]).astype(bf16)
        ext = extended(where, j, kv, other, rim)
        dqs, dks, dvs = [], [], []
        for h in range(local // HEAD_DIM):
            lanes = slice(h * HEAD_DIM, (h + 1) * HEAD_DIM)
            qh = q[j, :, lanes]
            kh = ext[:, lanes]
            vh = ext[:, local + h * HEAD_DIM : local + (h + 1) * HEAD_DIM]
            dch = dctx[:, lanes]
            prob = probs_of(qh, kh, bias[j])
            dprob = dot_t(dch, vh)
            inner = jnp.sum(prob * dprob, axis=-1, keepdims=True)
            dscore = (prob * (dprob - inner) * SCALE).astype(bf16)
            dqs.append(dot(dscore, kh))
            dks.append(t_dot(dscore, qh))
            dvs.append(t_dot(prob.astype(bf16), dch))
        dq_out[j] = jnp.concatenate(dqs, axis=1)
        grads = jnp.concatenate(dks + dvs, axis=1)
        dkv_out[j] = grads[HALF : HALF + length]
        before = grads[:HALF].astype(bf16)
        after = grads[HALF + length :].astype(bf16)
        b = chip ^ j
        below = jnp.where(core == 0, b - 1, b)
        above = jnp.where(core == 0, b, b + 1)

        @pl.when(below >= 0)
        def _():
            back_out[jnp.maximum(below, 0) ^ chip, length - HALF :, :] = before

        @pl.when(above < CHIPS)
        def _():
            back_out[jnp.minimum(above, CHIPS - 1) ^ chip, :HALF, :] = after

        if edges:
            rim_out = rest[3]

            @pl.when(below < 0)
            def _():
                rim_out[...] = before

            @pl.when(above >= CHIPS)
            def _():
                rim_out[...] = after


def qkv_grads_kernel(edges, where, dq, dkv, back, cos, sin, a, t0, t1, t2, t3, h0, h1, h2, h3, *rest):
    rim, rest = (rest[0], rest[1:]) if edges else (None, rest)
    keep, away, d_out, acc, cols = rest
    chip, core = where[0], where[1]
    length = dq.shape[1]
    local = dq.shape[2]
    width = a.shape[1]
    front = first_half((length, 128))
    for j in range(CHIPS):
        at = slice(j * length, (j + 1) * length)
        gkv = dkv[j] + back[j].astype(f32)
        if edges:
            b = chip ^ j
            blank = jnp.zeros((length - HALF, 2 * local), f32)
            value = rim[...].astype(f32)
            gkv = gkv + jnp.where(
                (core == 0) & (b == 0), jnp.concatenate([value, blank], axis=0), 0.0
    )
            gkv = gkv + jnp.where(
                (core == 1) & (b == CHIPS - 1), jnp.concatenate([blank, value], axis=0), 0.0
    )
        g = jnp.concatenate([dq[j], gkv[:, :local]], axis=1)
        for lane in range(0, 2 * local, 128):
            u = g[:, lane : lane + 128]
            up, down = shifted(u * sin[at, :])
            d_out[at, lane : lane + 128] = (
                u * cos[at, :] + jnp.where(front, up, -down)
            ).astype(bf16)
        d_out[at, 2 * local :] = gkv[:, local:].astype(bf16)
    acc[:, : 3 * local] = t_dot(a[...], d_out[...])
    for b in range(CHIPS):

        @pl.when(chip == b)
        def _():
            for j, ref in enumerate((h0, h1, h2, h3)):
                cols[j * length : (j + 1) * length, :] = ref[:, b * local : (b + 1) * local]

    for i, ref in enumerate((t0, t1, t2, t3)):
        rows = jnp.concatenate([ref[j ^ i] for j in range(CHIPS)], axis=0)
        acc[rows_at((chip ^ i) * local, local), 3 * local :] = t_dot(rows, cols[...])
    half = keep.shape[1]
    share = CORES * half
    for z in range(PLANES):
        keep[z] = acc[rows_at(z * share + core * half, half), :]
        away[z] = acc[rows_at(z * share + (1 - core) * half, half), :].astype(bf16)


def da_kernel(where, d, w, x0, x1, x2, x3, gain_two, own_out, o1, o2, o3, gain_out):
    rows = x0.shape[0]
    total = jnp.zeros((1, w.shape[0]), f32)
    for j, ref in enumerate((x0, x1, x2, x3)):
        da = dot_t(d[j * rows : (j + 1) * rows, :], w[...])
        normed, _ = norm_parts(ref[:rows, :].astype(f32))
        total = total + jnp.sum(da * normed, axis=0, keepdims=True)
        if j == 0:
            own_out[...] = da
        else:
            (o1, o2, o3)[j - 1][...] = da.astype(bf16)
    share = w.shape[0] // PLANES
    for z in range(PLANES):
        at = slice(z * share, (z + 1) * share)
        gain_out[z] = extra_rows(total[:, at], gain_two[0:1, at], gain_out.shape[2])


def copy_kernel(where, value, out):
    out[...] = value[...]


def ffn_split_kernel(where, keep, got, near, far):
    for i in range(PLANES):
        at = where[2] ^ i
        total = keep[at] + got[at].astype(f32)
        if i < 2:
            near[i] = total
        else:
            far[i - 2] = total.astype(bf16)


def ffn_near_kernel(where, near, got, own, sent):
    own[...] = near[0] + got[0].astype(f32)
    sent[...] = (near[1] + got[1].astype(f32)).astype(bf16)


def ffn_total_kernel(where, own, got, out):
    out[...] = (own[...] + got[...].astype(f32)).astype(out.dtype)


def to_planes_gains_kernel(where, keep, got, gains, d1, d2, d3, own, o1, o2, o3, e1, e2, e3):
    for ref, out in ((d1, e1), (d2, e2), (d3, e3)):
        out[...] = ref[...]
    plane = where[2]
    half = keep.shape[1]
    own[:half, :] = keep[plane] + got[plane].astype(f32)
    own[half:, :] = gains[plane]
    for i, ref in enumerate((o1, o2, o3)):
        at = plane ^ (i + 1)
        ref[:half, :] = (keep[at] + got[at].astype(f32)).astype(bf16)
        ref[half:, :] = gains[at].astype(bf16)


def sum_kernel(where, own, r1, r2, r3, out):
    total = own[...] + r1[...].astype(f32) + r2[...].astype(f32) + r3[...].astype(f32)
    out[...] = total.astype(out.dtype)


def last_kernel(where, own, r1, r2, r3, x0, dh, gains, grad_out):
    total = own[...] + r1[...].astype(f32) + r2[...].astype(f32) + r3[...].astype(f32)
    normed, factor = norm_parts(x0[...].astype(f32))
    grad = dh[...] + norm_inward(total, gains[0:1, :], normed, factor)
    grad_out[0] = grad.astype(bf16)


def ffn_owned_kernel(where, mine, other, in_out, back_out):
    core = where[1]
    half = mine.shape[1]
    units = FF // CHIPS
    part = units // PLANES
    lanes = mine.shape[2] - 2 * units
    for k, ref in ((core, mine), (1 - core, other)):
        rows = rows_at(k * half, half)
        for p in range(2):
            for z in range(PLANES):
                at = (p * PLANES + z) * part
                for b in range(CHIPS):
                    to = p * FF + (z * CHIPS + b) * part
                    in_out[rows, to : to + part] = ref[b, :, at : at + part].astype(f32)
    for b in range(CHIPS):
        own = mine[b, :part, 2 * units :].astype(f32)
        got = other[b, :part, 2 * units :].astype(f32)
        back_out[b * part : (b + 1) * part, :lanes] = jnp.where(core == 0, own, got)
        back_out[b * part : (b + 1) * part, lanes:] = jnp.where(core == 0, got, own)


def qkv_owned_kernel(where, mine, other, qkv_out, w_out, one_out, two_out):
    core = where[1]
    half = mine.shape[1] - EXTRA
    local = w_out.shape[1] // CHIPS
    total = jnp.zeros((EXTRA, local), f32)
    for k, ref in ((core, mine), (1 - core, other)):
        rows = rows_at(k * half, half)
        for b in range(CHIPS):
            for p in range(3):
                to = (p * CHIPS + b) * local
                qkv_out[rows, to : to + local] = ref[b, :half, p * local : (p + 1) * local].astype(f32)
            w_out[rows, b * local : (b + 1) * local] = ref[b, :half, 3 * local :].astype(f32)
            total = total + ref[b, half:, :local].astype(f32)
    one_out[...] = total[0]
    two_out[...] = total[1]


def shards(tokens, norm_gain, w_qkv, w_out, ffn_gain, w_in, w_back, seq_ids, cotangent):
    length, width = tokens.shape[1:]
    me = lax.axis_index("seq")
    seq_count = lax.axis_size("seq")
    edges = seq_count > MEMBERS
    group = me // MEMBERS
    chip = (me % MEMBERS) // CORES
    core = me % CORES
    local = width // CHIPS
    units = FF // CHIPS
    many = CHIPS * length
    half = width // PLANES // CORES
    lanes = width // CORES
    extent = length + 2 * HALF
    kept = half + EXTRA
    in_lanes = 2 * units + width + lanes
    in_sent = lanes + 2 * units
    ffn_lanes = 2 * units + lanes
    qkv_lanes = 4 * local

    out_rows = w_out.shape[0] // CHIPS
    piece = call(
        qkv_piece_kernel,
        "qkv_piece",
        shape(kept + 32, 3 * local),
        w_qkv,
        w_out,
        norm_gain,
        ffn_gain,
        held=2,
        scratch=(
            pltpu.VMEM((half, 3 * width), bf16),
            pltpu.VMEM((out_rows, lanes), bf16),
            pltpu.SemaphoreType.DMA((2,)),
        ),
    )
    pieces = over_planes(piece)
    both = jnp.concatenate([tokens[0], cotangent[0]], axis=0)
    both_near = swap_seq(both, 2 * CORES)
    xs = [tokens[0], swap_seq(tokens[0], CORES), both_near, swap_seq(tokens[0], 3 * CORES)]
    piece = call(
        ffn_piece_kernel,
        "ffn_piece",
        shape(half, in_sent),
        w_in,
        w_back,
        held=2,
        scratch=(
            pltpu.VMEM((half, 2 * FF), bf16),
            pltpu.VMEM((w_back.shape[0], lanes), bf16),
            pltpu.SemaphoreType.DMA((2,)),
        ),
        after=(piece,),
    )
    in_near = swap_shard(piece, 1)
    mine, out_own = call(
        qkv_place_kernel,
        "qkv_place",
        (
            shape(PLANES, kept, 3 * local),
            shape(PLANES, out_rows, lanes),
        ),
        *pieces,
    )
    out_near = swap_seq(out_own, CORES)
    other = swap_core(mine)

    block = (group * CHIPS + (chip ^ jnp.arange(CHIPS))) * CORES + core
    position = (block[:, None] * length + jnp.arange(length)[None]).astype(f32).reshape(many)
    frequency = 10000.0 ** (-jnp.arange(0, HEAD_DIM, 2).astype(f32) / HEAD_DIM)
    angles = position[:, None] * jnp.tile(frequency, 4)[None]
    cosine, sine = jnp.cos(angles), jnp.sin(angles)
    spans = length // HALF
    ids = jnp.pad(seq_ids[0], (1, 1), constant_values=-1)
    key_ids = jnp.stack(
        [lax.dynamic_slice_in_dim(ids, block[j] * spans, spans + 2, 0) for j in range(CHIPS)]
    )
    key_ids = jnp.repeat(key_ids, HALF, axis=1)
    query_ids = key_ids[:, HALF : HALF + length]
    offset = jnp.arange(extent)[None, :] - HALF - jnp.arange(length)[:, None]
    allowed = (jnp.abs(offset) <= HALF)[None] & (query_ids[:, :, None] == key_ids[:, None, :])
    bias = jnp.where(allowed, 0.0, -1e30).astype(f32)

    low_one, query, kv, wq, gains = call(
        qkv_kernel,
        "qkv",
        (
            shape(many, width),
            shape(CHIPS, length, local),
            shape(CHIPS, length, 2 * local),
            shape(width, 3 * local),
            shape(8, width, dtype=f32),
        ),
        *xs,
        mine,
        other,
        cosine,
        sine,
    )
    kv_other = swap_core(kv)
    in_pair = call(
        pair_kernel, "in_pair", shape(2, half, in_sent), piece, in_near, after=(gains,)
    )
    in_far = swap_shard(in_pair, 2)

    def beyond(value):
        pairs = []
        for m in range(seq_count):
            to = m - MEMBERS + 1 if m % CORES == 0 else m + MEMBERS - 1
            if 0 <= to < seq_count:
                pairs.append((m, to))
        return lax.ppermute(value, "seq", pairs)

    rim = ()
    if edges:
        first = lax.dynamic_index_in_dim(kv, chip, 0, False)[:HALF]
        last = lax.dynamic_index_in_dim(kv, chip ^ (CHIPS - 1), 0, False)[length - HALF :]
        rim = (beyond(jnp.where(core == 0, first, last)),)

    out_pair = call(pair_kernel, "out_pair", shape(2, *out_own.shape), out_own, out_near, after=(in_pair,))
    out_far = swap_seq(out_pair, 2 * CORES)
    up_pair = call(up_pair_kernel, "up_pair", shape(2, length, width), cotangent[0], both_near, after=(gains,))
    gys = (up_pair, swap_seq(up_pair, CORES))
    attn = call(
        functools.partial(attend_kernel, edges),
        "attend",
        shape(CHIPS, length, local),
        query,
        kv,
        kv_other,
        bias,
        *rim,
        after=(gys[1],),
    )
    attns = over_chips(attn)
    in_mine = call(
        ffn_place_kernel,
        "ffn_place",
        shape(PLANES, half, in_lanes),
        in_pair,
        in_far,
        out_pair,
        out_far,
        after=tuple(attns[1:]),
    )
    in_other = swap_core(in_mine)
    own, d1, d2, d3, hidden, low_two, hidden_low, grad_expanded, gain_two, wb, wo = call(
        ffn_kernel,
        "ffn",
        (shape(length, width, dtype=f32),)
        + (shape(length, width),) * 3
        + (
            shape(length, width, dtype=f32),
            shape(many, width),
            shape(many, units),
            shape(many, 2 * units),
            shape(8, width, dtype=f32),
            shape(units, width),
            shape(local, width),
        ),
        *attns,
        *xs,
        *gys,
        in_mine,
        in_other,
        gains,
        scratch=(pltpu.VMEM((width, 2 * units), bf16), pltpu.VMEM((width, width), bf16)),
    )
    received = [swap_seq(d, CORES * (j + 1)) for j, d in enumerate((d1, d2, d3))]
    keep_ffn, away = call(
        ffn_grads_kernel,
        "ffn_grads",
        (shape(PLANES, half, ffn_lanes, dtype=f32), shape(PLANES, half, ffn_lanes)),
        low_two,
        hidden_low,
        grad_expanded,
        *gys,
        scratch=(pltpu.VMEM((width, 2 * units), f32), pltpu.VMEM((CORES, units, lanes), f32)),
    )
    got_ffn = swap_core(away)
    near, far = call(
        ffn_split_kernel,
        "ffn_split",
        (shape(2, half, ffn_lanes, dtype=f32), shape(2, half, ffn_lanes)),
        keep_ffn,
        got_ffn,
    )
    got_far = swap_shard(far, 2)
    dh, dh_low = call(
        dh_kernel, "dh", (shape(length, width, dtype=f32), shape(length, width)), own, *received, gys[0], hidden, gains, after=(far,)
    )
    dhs = over_chips(dh_low)
    partial_mixed = call(
        mixed_kernel,
        "mixed",
        (shape(length, width, dtype=f32),) + (shape(length, width),) * 3,
        hidden_low,
        wb,
        after=(dh_low,),
    )
    got_mixed = [swap_seq(o, CORES * (j + 1)) for j, o in enumerate(partial_mixed[1:])]

    backs = call(
        functools.partial(attend_back_kernel, edges),
        "attend_back",
        (
            shape(CHIPS, length, local, dtype=f32),
            shape(CHIPS, length, 2 * local, dtype=f32),
            shape(CHIPS, length, 2 * local),
        )
        + ((shape(HALF, 2 * local),) if edges else ()),
        query,
        kv,
        kv_other,
        bias,
        *dhs,
        wo,
        *rim,
        after=(far,),
    )
    dq, dkv, back = backs[:3]
    back = swap_core(back)
    if edges:
        rim = (beyond(backs[3]),)

    def over_groups(total, kept_type):
        step = MEMBERS
        while step < seq_count:
            total = total + swap_seq(total.astype(bf16), step).astype(f32)
            step *= 2
        return total.astype(kept_type)

    def summed(own, parts, name, after=()):
        out = call(
            sum_kernel, name, shape(*own.shape, dtype=f32 if edges else bf16), own, *parts, after=after
        )
        return over_groups(out, bf16)

    mixed = call(
        mixed_sum_kernel, "mixed_sum", shape(1, length, width), partial_mixed[0], *got_mixed, hidden, after=(dq,)
    )

    keep, away, dqkv = call(
        functools.partial(qkv_grads_kernel, edges),
        "qkv_grads",
        (
            shape(PLANES, half, qkv_lanes, dtype=f32),
            shape(PLANES, half, qkv_lanes),
            shape(many, 3 * local),
        ),
        dq,
        dkv,
        back,
        cosine,
        sine,
        low_one,
        *attns,
        *dhs,
        *rim,
        scratch=(pltpu.VMEM((width, qkv_lanes), f32), pltpu.VMEM((many, local), bf16)),
    )
    own_ffn, sent_near = call(
        ffn_near_kernel,
        "ffn_near",
        (shape(half, ffn_lanes, dtype=f32), shape(half, ffn_lanes)),
        near,
        got_far,
        after=(dq,),
    )
    total = call(
        ffn_total_kernel,
        "ffn_total",
        shape(half, ffn_lanes, dtype=f32 if edges else bf16),
        own_ffn,
        swap_shard(sent_near, 1),
        after=(away,),
    )
    pieces_ffn = over_chips(over_groups(total, bf16))
    got = swap_core(away)
    last_own, o1, o2, o3, gain_sums = call(
        da_kernel,
        "da",
        (shape(length, width, dtype=f32),)
        + (shape(length, width),) * 3
        + (shape(PLANES, EXTRA, qkv_lanes, dtype=f32),),
        dqkv,
        wq,
        *xs,
        gain_two,
        after=(mixed,),
    )
    sent = call(
        to_planes_gains_kernel,
        "qkv_to_planes",
        (shape(kept, qkv_lanes, dtype=f32),)
        + (shape(kept, qkv_lanes),) * 3
        + (shape(length, width),) * 3,
        keep,
        got,
        gain_sums,
        o1,
        o2,
        o3,
    )
    got = [swap_shard(s, i + 1) for i, s in enumerate(sent[1:4])]
    received = [swap_seq(o, CORES * (j + 1)) for j, o in enumerate(sent[4:])]

    mine = call(
        functools.partial(place_kernel, 0),
        "ffn_gather",
        shape(CHIPS, half, ffn_lanes),
        *pieces_ffn,
        after=(sent[1],),
    )
    owned_in, owned_back = call(
        ffn_owned_kernel,
        "ffn_owned",
        (shape(*w_in.shape, dtype=f32), shape(*w_back.shape, dtype=f32)),
        mine,
        swap_core(mine),
    )
    grad_tokens = call(
        last_kernel,
        "last",
        shape(1, length, width),
        last_own,
        *received,
        xs[0],
        dh,
        gains,
        after=(sent[1],),
    )
    mine = call(
        functools.partial(place_kernel, 0),
        "qkv_gather",
        shape(CHIPS, kept, qkv_lanes),
        *over_chips(summed(sent[0], got, "qkv_sum")),
        after=(grad_tokens, owned_back),
    )
    owned_qkv, owned_out, grad_gain_one, grad_gain_two = call(
        qkv_owned_kernel,
        "qkv_owned",
        (
            shape(*w_qkv.shape, dtype=f32),
            shape(*w_out.shape, dtype=f32),
            shape(local, dtype=f32),
            shape(local, dtype=f32),
        ),
        mine,
        swap_core(mine),
    )
    return (mixed, grad_tokens, grad_gain_one, owned_qkv, owned_out, grad_gain_two, owned_in, owned_back)


def solution(mesh):
    return jax.shard_map(
        shards,
        mesh=mesh,
        in_specs=(
            P("shard", "seq", None),
            P("shard"),
            P("shard", None),
            P("shard", None),
            P("shard"),
            P("shard", None),
            P("shard", None),
            P("shard", None),
            P("shard", "seq", None),
        ),
        out_specs=(
            P("shard", "seq", None),
            P("shard", "seq", None),
            P("shard"),
            P("shard", None),
            P("shard", None),
            P("shard"),
            P("shard", None),
            P("shard", None),
        ),
        check_vma=False,
    )
```

```python
import functools
import math

import jax
import jax.numpy as jnp
from jax import lax
from jax.experimental import pallas as pl
from jax.experimental.pallas import tpu as pltpu
from jax.sharding import PartitionSpec as P

HEADS = 12
HEAD_DIM = 64
FF = 1152
HALF = 64
CHIPS = 4
CORES = 2
MEMBERS = CHIPS * CORES
PLANES = 4
EXTRA = 16
f32 = jnp.float32
bf16 = jnp.bfloat16
SCALE = HEAD_DIM ** (-0.5)
ROOM = 6 * 1024 * 1024


TIMES = {
    "qkv_piece": 0.5,
    "ffn_piece": 1,
    "qkv_place": 0.8,
    "qkv": 1.6,
    "attend": 2.3,
    "ffn_place": 1.2,
    "ffn": 4.5,
    "ffn_grads": 1.6,
    "dh": 0.4,
    "mixed": 0.6,
    "ffn_split": 1,
    "mixed_sum": 0.4,
    "attend_back": 6.9,
    "qkv_grads": 2.4,
    "da": 1.5,
    "qkv_to_planes": 0.8,
    "qkv_gather": 0.6,
    "last_packet": 0.5,
    "ffn_total": 0.4,
    "ffn_gather": 0.5,
    "qkv_sum": 0.4,
    "last": 0.6,
    "ffn_owned": 2.2,
    "qkv_owned": 1.7,
}


def dot(left, right):
    return lax.dot_general(left, right, (((1,), (0,)), ((), ())), preferred_element_type=f32)


def dot_t(left, right):
    return lax.dot_general(left, right, (((1,), (1,)), ((), ())), preferred_element_type=f32)


def t_dot(left, right):
    return lax.dot_general(left, right, (((0,), (0,)), ((), ())), preferred_element_type=f32)


def swap_seq(value, bits):
    count = lax.axis_size("seq")
    return lax.ppermute(value, "seq", [(i, i ^ bits) for i in range(count)])


def swap_shard(value, bits):
    count = lax.axis_size("shard")
    return lax.ppermute(value, "shard", [(i, i ^ bits) for i in range(count)])


def swap_core(value):
    return swap_seq(value, 1)


def over_chips(value):
    return [value] + [swap_seq(value, CORES * j) for j in range(1, CHIPS)]


def over_planes(value):
    return [value] + [swap_shard(value, i) for i in range(1, PLANES)]


def shape(*dims, dtype=bf16):
    return jax.ShapeDtypeStruct(dims, dtype)


def places():
    me = lax.axis_index("seq")
    return (me % MEMBERS) // CORES, me % CORES, lax.axis_index("shard")


def size_of(value):
    return math.prod(value.shape) * jnp.dtype(value.dtype).itemsize


def call(kernel, name, outs, *operands, after=(), scratch=(), held=0):
    taken = len(operands)
    specs = [pl.BlockSpec(memory_space=pltpu.HBM)] * held
    specs += [pl.BlockSpec(memory_space=pltpu.VMEM)] * (taken - held)
    specs += [pl.BlockSpec(memory_space=pl.ANY)] * len(after)
    us = TIMES.get(name, 0.5)
    held_size = sum(size_of(o) for o in operands[held:])
    held_size += sum(size_of(o) for o in jax.tree.leaves(outs))

    def body(*refs):
        kernel(places(), *refs[:taken], *refs[taken + len(after) :])

    return pl.pallas_call(
        body,
        out_shape=outs,
        in_specs=specs,
        out_specs=jax.tree.map(lambda _: pl.BlockSpec(memory_space=pltpu.VMEM), outs),
        scratch_shapes=list(scratch),
        cost_estimate=pl.CostEstimate(
            flops=int(us * 2e10), bytes_accessed=int(us * 10), transcendentals=0
        ),
        compiler_params=pltpu.CompilerParams(vmem_limit_bytes=2 * held_size + ROOM),
        name=name,
    )(*operands, *after)


def norm_parts(values):
    center = values - jnp.mean(values, axis=-1, keepdims=True)
    factor = lax.rsqrt(jnp.mean(center * center, axis=-1, keepdims=True) + 1e-05)
    return center * factor, factor


def norm_inward(upward, gain, normed, factor):
    scaled = upward * gain
    return factor * (
        scaled
        - jnp.mean(scaled, axis=-1, keepdims=True)
        - normed * jnp.mean(scaled * normed, axis=-1, keepdims=True)
    )


def first_half(shape_of):
    return lax.broadcasted_iota(jnp.int32, shape_of, 1) % HEAD_DIM < HEAD_DIM // 2


def shifted(values):
    return pltpu.roll(values, 96, 1), pltpu.roll(values, 32, 1)


def rows_at(start, size):
    return pl.ds(pl.multiple_of(start, 16), size)


def lanes_at(start, size):
    return pl.ds(pl.multiple_of(start, 128), size)


def extra_rows(first, second, lanes):
    row = lax.broadcasted_iota(jnp.int32, (EXTRA, lanes), 0)
    pad = jnp.zeros((1, lanes - first.shape[1]), f32)
    first = jnp.concatenate([first, pad], axis=1)
    second = jnp.concatenate([second, pad], axis=1)
    return jnp.where(row == 0, first, jnp.where(row == 1, second, 0.0))


def copied(pairs, sems):
    copies = [pltpu.make_async_copy(src, dst, sems.at[i]) for i, (src, dst) in enumerate(pairs)]
    for copy in copies:
        copy.start()
    for copy in copies:
        copy.wait()


def qkv_piece_kernel(where, w_qkv, part, gains, out, rows, sems):
    chip, core = where[0], where[1]
    half = w_qkv.shape[0] // CORES
    width = w_qkv.shape[1] // 3
    local = width // CHIPS
    size, lanes = part.shape
    copied(((w_qkv.at[rows_at(core * half, half), :], rows),), sems)
    for b in range(CHIPS):

        @pl.when(chip == b)
        def _():
            for p in range(3):
                at = p * width + b * local
                out[:half, p * local : (p + 1) * local] = rows[:, at : at + local]

    both = gains[...].astype(f32)
    out[half : half + EXTRA, :] = extra_rows(both[0:1, :], both[1:2, :], 3 * local).astype(bf16)
    at = half + EXTRA
    out[at : at + 16, :lanes] = part[:16, :]
    out[at + 16 :, :lanes] = part[16:32, :]
    out[at : at + 16, lanes:] = part[32:, :local]
    out[at + 16 :, lanes:] = part[32:, local:]


def ffn_piece_kernel(where, w_in, w_back, out, rows, back, sems):
    chip, core = where[0], where[1]
    half = w_in.shape[0] // CORES
    units = FF // PLANES // CHIPS
    lanes = back.shape[1]
    copied(
        (
            (w_in.at[rows_at(core * half, half), :], rows),
            (w_back.at[:, lanes_at(core * lanes, lanes)], back),
        ),
        sems,
    )
    out[units:, :lanes] = jnp.zeros((half - units, lanes), bf16)
    for b in range(CHIPS):

        @pl.when(chip == b)
        def _():
            for p in range(2):
                for z in range(PLANES):
                    at = p * FF + z * units * CHIPS + b * units
                    to = lanes + (p * PLANES + z) * units
                    out[:, to : to + units] = rows[:, at : at + units]
            out[:units, :lanes] = back[b * units : (b + 1) * units, :]


def place_kernel(slot, where, p0, p1, p2, p3, out):
    for i, ref in enumerate((p0, p1, p2, p3)):
        out[where[slot] ^ i] = ref[...]


def qkv_place_kernel(where, p0, p1, p2, p3, out, packet):
    kept = out.shape[1]
    lanes = packet.shape[2]
    for i, ref in enumerate((p0, p1, p2, p3)):
        z = where[2] ^ i
        out[z] = ref[:kept, :]
        packet[z, :16, :] = ref[kept : kept + 16, :lanes]
        packet[z, 16:32, :] = ref[kept + 16 :, :lanes]
        packet[z, 32:, :] = jnp.concatenate(
            [ref[kept : kept + 16, lanes:], ref[kept + 16 :, lanes:]], axis=1
        )


def up_pair_kernel(where, own, both, out):
    out[0] = own[...]
    out[1] = both[own.shape[0] :, :]


def last_packet_kernel(where, total, *refs):
    half, lanes = total.shape
    rows, width = refs[0].shape
    spare = lanes - width
    for ref, out in zip(refs[: len(refs) // 2], refs[len(refs) // 2 :]):
        out[:rows, :] = ref[...]
        out[rows : rows + half, :] = total[:, :width]
        for i in range(half // 32):
            at = slice(i * spare, (i + 1) * spare)
            out[rows + half :, at] = total[i * 32 : (i + 1) * 32, width:]
        blank = width - half // 32 * spare
        out[rows + half :, width - blank :] = jnp.zeros((32, blank), bf16)


def ffn_gather_kernel(where, total, r1, r2, r3, out):
    half, lanes = total.shape
    width = r1.shape[1]
    spare = lanes - width
    rows = r1.shape[0] - half - 32
    out[where[0]] = total[...]
    for j, ref in enumerate((r1, r2, r3)):
        at = where[0] ^ (j + 1)
        out[at, :, :width] = ref[rows : rows + half, :]
        for i in range(half // 32):
            piece = ref[rows + half :, i * spare : (i + 1) * spare]
            out[at, i * 32 : (i + 1) * 32, width:] = piece


def pair_kernel(where, first, second, out):
    out[0] = first[...]
    out[1] = second[...]


def ffn_place_kernel(where, near, far, p01, p23, out):
    half = near.shape[1]
    p0, p1, p2, p3 = p01.at[0], p01.at[1], p23.at[0], p23.at[1]
    size, lanes = p0.shape[1:]
    for i, ref in enumerate((near.at[0], near.at[1], far.at[0], far.at[1])):
        z = where[2] ^ i
        out[z, :, :lanes] = ref[:, :lanes]
        out[z, :, 3 * lanes :] = ref[:, lanes:]
    for i, ref in enumerate((p0, p1, p2, p3)):
        b = where[0] ^ i
        at = rows_at((b % 2) * size, size)

        for half_at in range(2):

            @pl.when(b // 2 == half_at)
            def _():
                for z in range(PLANES):
                    out[z, at, (half_at + 1) * lanes : (half_at + 2) * lanes] = ref[z]


def qkv_kernel(where, x0, x1, x2, x3, mine, other, cos, sin, a_out, q_out, kv_out, w_out, g_out):
    rows = x0.shape[0]
    half = mine.shape[1] - EXTRA
    local = mine.shape[2] // 3
    share = CORES * half
    core = where[1]
    for z in range(PLANES):
        w_out[rows_at(z * share + core * half, half), :] = mine[z, :half, :]
        w_out[rows_at(z * share + (1 - core) * half, half), :] = other[z, :half, :]
        tail = mine[z, half:, :share].astype(f32)
        g_out[:, z * share : (z + 1) * share] = tail[:8]
    gain = g_out[0:1, :]
    for j, ref in enumerate((x0, x1, x2, x3)):
        normed, _ = norm_parts(ref[:rows, :].astype(f32))
        a_out[j * rows : (j + 1) * rows, :] = (normed * gain).astype(bf16)
    out = dot(a_out[...], w_out[...])
    front = first_half((CHIPS * rows, 128))
    parts = []
    for at in range(0, 2 * local, 128):
        u = out[:, at : at + 128]
        up, down = shifted(u)
        parts.append((u * cos[...] + jnp.where(front, -up, down) * sin[...]).astype(bf16))
    qk = jnp.concatenate(parts, axis=1)
    value = out[:, 2 * local :].astype(bf16)
    for j in range(CHIPS):
        at = slice(j * rows, (j + 1) * rows)
        q_out[j] = qk[at, :local]
        kv_out[j, :, :local] = qk[at, local:]
        kv_out[j, :, local:] = value[at]


def extended(where, j, kv, other, rim):
    chip, core = where[0], where[1]
    length = kv.shape[1]
    b = chip ^ j
    below = jnp.where(core == 0, jnp.maximum(b - 1, 0), b) ^ chip
    above = jnp.where(core == 0, b, jnp.minimum(b + 1, CHIPS - 1)) ^ chip
    before = other[below, length - HALF :, :]
    after = other[above, :HALF, :]
    if rim is not None:
        before = jnp.where((core == 0) & (b == 0), rim[...], before)
        after = jnp.where((core == 1) & (b == CHIPS - 1), rim[...], after)
    return jnp.concatenate([before, kv[j], after], axis=0)


def probs_of(q, k, bias):
    logits = dot_t(q, k) * SCALE + bias
    highest = jnp.max(logits, axis=-1, keepdims=True)
    exponent = jnp.exp(logits - highest)
    return exponent / jnp.sum(exponent, axis=-1, keepdims=True)


def attend_kernel(edges, where, q, kv, other, bias, *rest):
    rim, out = rest if edges else (None, rest[0])
    local = q.shape[-1]
    for j in range(CHIPS):
        ext = extended(where, j, kv, other, rim)
        parts = []
        for h in range(local // HEAD_DIM):
            lanes = slice(h * HEAD_DIM, (h + 1) * HEAD_DIM)
            prob = probs_of(q[j, :, lanes], ext[:, lanes], bias[j]).astype(bf16)
            parts.append(dot(prob, ext[:, local + h * HEAD_DIM : local + (h + 1) * HEAD_DIM]))
        out[j] = jnp.concatenate(parts, axis=1).astype(bf16)


def ffn_kernel(
    where, t0, t1, t2, t3, x0, x1, x2, x3, y02, y13, mine, other, gains,
    own_out, d1_out, d2_out, d3_out, hid_out, a_out, m_out, dgu_out, gain_out, wb_out, wc_out,
    wi, wo,
):
    chip, core = where[0], where[1]
    rows = x0.shape[0]
    width = x0.shape[1]
    half = mine.shape[1]
    share = CORES * half
    units = FF // CHIPS
    part = units // PLANES
    lanes = width // CORES
    local = width // CHIPS
    for z in range(PLANES):
        for k, ref in ((core, mine), (1 - core, other)):
            wi[rows_at(z * share + k * half, half), :] = ref[z, :, 3 * lanes :]
            for p in range(CORES):
                at = slice(z * share + p * half, z * share + (p + 1) * half)
                wo[at, lanes_at(k * lanes, lanes)] = ref[z, :, (p + 1) * lanes : (p + 2) * lanes]
    own_back = jnp.concatenate([mine[z, :part, :lanes] for z in range(PLANES)], axis=0)
    other_back = jnp.concatenate([other[z, :part, :lanes] for z in range(PLANES)], axis=0)
    wb_out[:, :lanes] = jnp.where(core == 0, own_back, other_back)
    wb_out[:, lanes:] = jnp.where(core == 0, other_back, own_back)
    wc_out[...] = wo[rows_at(chip * local, local), :]
    xs = (x0, x1, x2, x3)
    gain = gains[1:2, :]
    outward = [
        (ref, wo[rows_at((chip ^ i) * local, local), :]) for i, ref in enumerate((t0, t1, t2, t3))
    ]
    normed = []
    for j in range(CHIPS):
        hidden = xs[j][:rows, :].astype(f32)
        for i, (ref, weight) in enumerate(outward):
            hidden = hidden + dot(ref[j ^ i], weight)
        if j == 0:
            hid_out[...] = hidden
        norm, _ = norm_parts(hidden)
        normed.append(norm)
        a_out[j * rows : (j + 1) * rows, :] = (norm * gain).astype(bf16)
    total = jnp.zeros((1, width), f32)
    for j in range(CHIPS):
        at = slice(j * rows, (j + 1) * rows)
        gu = dot(a_out[at, :], wi[...])
        entering, gating = gu[:, :units], gu[:, units:]
        rise = 0.5 * (1.0 + lax.erf(entering * (0.5**0.5)))
        slope = rise + entering * jnp.exp(-0.5 * entering * entering) * 0.3989422804014327
        act = entering * rise
        m_out[at, :] = (act * gating).astype(bf16)
        dm = dot_t((y02, y13)[j % 2][j // 2], wb_out[...])
        dgu = jnp.concatenate([dm * gating * slope, dm * act], axis=1).astype(bf16)
        dgu_out[at, :] = dgu
        da = dot_t(dgu, wi[...])
        total = total + jnp.sum(da * normed[j], axis=0, keepdims=True)
        if j == 0:
            own_out[...] = da
        else:
            (d1_out, d2_out, d3_out)[j - 1][...] = da.astype(bf16)
    gain_out[...] = jnp.broadcast_to(total, gain_out.shape)


def mixed_kernel(where, m, wb, own, m1, m2, m3):
    rows = own.shape[0]
    own[...] = dot(m[:rows, :], wb[...])
    for j, ref in enumerate((m1, m2, m3)):
        ref[...] = dot(m[(j + 1) * rows : (j + 2) * rows, :], wb[...]).astype(bf16)


def mixed_sum_kernel(where, own, r1, r2, r3, hidden, out):
    total = own[...] + r1[...].astype(f32) + r2[...].astype(f32) + r3[...].astype(f32)
    out[0] = (hidden[...] + total).astype(bf16)


def ffn_grads_kernel(where, a, m, dgu, y02, y13, keep, away, gin, gb):
    core = where[1]
    half = keep.shape[1]
    share = CORES * half
    units = m.shape[1]
    part = units // PLANES
    lanes = y02.shape[2] // CORES
    gin[...] = t_dot(a[...], dgu[...])
    upward = jnp.concatenate([y02[0], y13[0], y02[1], y13[1]], axis=0)
    back = t_dot(m[...], upward)
    first, second = back[:, :lanes], back[:, lanes:]
    gb[0] = jnp.where(core == 0, first, second)
    gb[1] = jnp.where(core == 0, second, first)
    for z in range(PLANES):
        at = slice(z * part, (z + 1) * part)
        blank = jnp.zeros((half - part, lanes), f32)
        keep[z, :, : 2 * units] = gin[rows_at(z * share + core * half, half), :]
        keep[z, :, 2 * units :] = jnp.concatenate([gb[0, at, :], blank], axis=0)
        away[z, :, : 2 * units] = gin[rows_at(z * share + (1 - core) * half, half), :].astype(bf16)
        away[z, :, 2 * units :] = jnp.concatenate([gb[1, at, :], blank], axis=0).astype(bf16)


def dh_kernel(where, own, r1, r2, r3, y02, hidden, gains, dh_out, low_out):
    total = own[...] + r1[...].astype(f32) + r2[...].astype(f32) + r3[...].astype(f32)
    normed, factor = norm_parts(hidden[...])
    dh = y02[0].astype(f32) + norm_inward(total, gains[1:2, :], normed, factor)
    dh_out[...] = dh
    low_out[...] = dh.astype(bf16)


def attend_back_kernel(edges, where, q, kv, other, bias, h0, h1, h2, h3, w_out, *rest):
    rim, rest = (rest[0], rest[1:]) if edges else (None, rest)
    dq_out, dkv_out, back_out = rest[:3]
    chip, core = where[0], where[1]
    local = q.shape[-1]
    length = q.shape[1]
    back_out[...] = jnp.zeros_like(back_out)
    for j, dh in enumerate((h0, h1, h2, h3)):
        dctx = dot_t(dh[...], w_out[...]).astype(bf16)
        ext = extended(where, j, kv, other, rim)
        dqs, dks, dvs = [], [], []
        for h in range(local // HEAD_DIM):
            lanes = slice(h * HEAD_DIM, (h + 1) * HEAD_DIM)
            qh = q[j, :, lanes]
            kh = ext[:, lanes]
            vh = ext[:, local + h * HEAD_DIM : local + (h + 1) * HEAD_DIM]
            dch = dctx[:, lanes]
            prob = probs_of(qh, kh, bias[j])
            dprob = dot_t(dch, vh)
            inner = jnp.sum(prob * dprob, axis=-1, keepdims=True)
            dscore = (prob * (dprob - inner) * SCALE).astype(bf16)
            dqs.append(dot(dscore, kh))
            dks.append(t_dot(dscore, qh))
            dvs.append(t_dot(prob.astype(bf16), dch))
        dq_out[j] = jnp.concatenate(dqs, axis=1)
        grads = jnp.concatenate(dks + dvs, axis=1)
        dkv_out[j] = grads[HALF : HALF + length]
        before = grads[:HALF].astype(bf16)
        after = grads[HALF + length :].astype(bf16)
        b = chip ^ j
        below = jnp.where(core == 0, b - 1, b)
        above = jnp.where(core == 0, b, b + 1)

        @pl.when(below >= 0)
        def _():
            back_out[jnp.maximum(below, 0) ^ chip, length - HALF :, :] = before

        @pl.when(above < CHIPS)
        def _():
            back_out[jnp.minimum(above, CHIPS - 1) ^ chip, :HALF, :] = after

        if edges:
            rim_out = rest[3]

            @pl.when(below < 0)
            def _():
                rim_out[...] = before

            @pl.when(above >= CHIPS)
            def _():
                rim_out[...] = after


def qkv_grads_kernel(edges, where, dq, dkv, back, cos, sin, a, t0, t1, t2, t3, h0, h1, h2, h3, *rest):
    rim, rest = (rest[0], rest[1:]) if edges else (None, rest)
    keep, away, d_out, acc, cols = rest
    chip, core = where[0], where[1]
    length = dq.shape[1]
    local = dq.shape[2]
    width = a.shape[1]
    front = first_half((length, 128))
    for j in range(CHIPS):
        at = slice(j * length, (j + 1) * length)
        gkv = dkv[j] + back[j].astype(f32)
        if edges:
            b = chip ^ j
            blank = jnp.zeros((length - HALF, 2 * local), f32)
            value = rim[...].astype(f32)
            gkv = gkv + jnp.where(
                (core == 0) & (b == 0), jnp.concatenate([value, blank], axis=0), 0.0
    )
            gkv = gkv + jnp.where(
                (core == 1) & (b == CHIPS - 1), jnp.concatenate([blank, value], axis=0), 0.0
    )
        g = jnp.concatenate([dq[j], gkv[:, :local]], axis=1)
        for lane in range(0, 2 * local, 128):
            u = g[:, lane : lane + 128]
            up, down = shifted(u * sin[at, :])
            d_out[at, lane : lane + 128] = (
                u * cos[at, :] + jnp.where(front, up, -down)
            ).astype(bf16)
        d_out[at, 2 * local :] = gkv[:, local:].astype(bf16)
    acc[:, : 3 * local] = t_dot(a[...], d_out[...])
    for b in range(CHIPS):

        @pl.when(chip == b)
        def _():
            for j, ref in enumerate((h0, h1, h2, h3)):
                cols[j * length : (j + 1) * length, :] = ref[:, b * local : (b + 1) * local]

    for i, ref in enumerate((t0, t1, t2, t3)):
        rows = jnp.concatenate([ref[j ^ i] for j in range(CHIPS)], axis=0)
        acc[rows_at((chip ^ i) * local, local), 3 * local :] = t_dot(rows, cols[...])
    half = keep.shape[1]
    share = CORES * half
    for z in range(PLANES):
        keep[z] = acc[rows_at(z * share + core * half, half), :]
        away[z] = acc[rows_at(z * share + (1 - core) * half, half), :].astype(bf16)


def da_kernel(where, d, w, x0, x1, x2, x3, gain_two, own_out, o1, o2, o3, gain_out):
    rows = x0.shape[0]
    total = jnp.zeros((1, w.shape[0]), f32)
    for j, ref in enumerate((x0, x1, x2, x3)):
        da = dot_t(d[j * rows : (j + 1) * rows, :], w[...])
        normed, _ = norm_parts(ref[:rows, :].astype(f32))
        total = total + jnp.sum(da * normed, axis=0, keepdims=True)
        if j == 0:
            own_out[...] = da
        else:
            (o1, o2, o3)[j - 1][...] = da.astype(bf16)
    share = w.shape[0] // PLANES
    for z in range(PLANES):
        at = slice(z * share, (z + 1) * share)
        gain_out[z] = extra_rows(total[:, at], gain_two[0:1, at], gain_out.shape[2])


def copy_kernel(where, value, out):
    out[...] = value[...]


def ffn_split_kernel(where, keep, got, near, far):
    for i in range(PLANES):
        at = where[2] ^ i
        total = keep[at] + got[at].astype(f32)
        if i < 2:
            near[i] = total
        else:
            far[i - 2] = total.astype(bf16)


def ffn_near_kernel(where, near, got, own, sent):
    own[...] = near[0] + got[0].astype(f32)
    sent[...] = (near[1] + got[1].astype(f32)).astype(bf16)


def ffn_total_kernel(where, own, got, out):
    out[...] = (own[...] + got[...].astype(f32)).astype(out.dtype)


def to_planes_gains_kernel(where, keep, got, gains, own, o1, o2, o3):
    plane = where[2]
    half = keep.shape[1]
    own[:half, :] = keep[plane] + got[plane].astype(f32)
    own[half:, :] = gains[plane]
    for i, ref in enumerate((o1, o2, o3)):
        at = plane ^ (i + 1)
        ref[:half, :] = (keep[at] + got[at].astype(f32)).astype(bf16)
        ref[half:, :] = gains[at].astype(bf16)


def sum_kernel(where, own, r1, r2, r3, out):
    total = own[...] + r1[...].astype(f32) + r2[...].astype(f32) + r3[...].astype(f32)
    out[...] = total.astype(out.dtype)


def last_kernel(where, own, r1, r2, r3, x0, dh, gains, grad_out):
    total = own[...]
    for ref in (r1, r2, r3):
        total = total + ref[: own.shape[0], :].astype(f32)
    normed, factor = norm_parts(x0[...].astype(f32))
    grad = dh[...] + norm_inward(total, gains[0:1, :], normed, factor)
    grad_out[0] = grad.astype(bf16)


def ffn_owned_kernel(where, mine, other, in_out, back_out):
    core = where[1]
    half = mine.shape[1]
    units = FF // CHIPS
    part = units // PLANES
    lanes = mine.shape[2] - 2 * units
    for k, ref in ((core, mine), (1 - core, other)):
        rows = rows_at(k * half, half)
        for p in range(2):
            for z in range(PLANES):
                at = (p * PLANES + z) * part
                for b in range(CHIPS):
                    to = p * FF + (z * CHIPS + b) * part
                    in_out[rows, to : to + part] = ref[b, :, at : at + part].astype(f32)
    for b in range(CHIPS):
        own = mine[b, :part, 2 * units :].astype(f32)
        got = other[b, :part, 2 * units :].astype(f32)
        back_out[b * part : (b + 1) * part, :lanes] = jnp.where(core == 0, own, got)
        back_out[b * part : (b + 1) * part, lanes:] = jnp.where(core == 0, got, own)


def qkv_owned_kernel(where, mine, other, qkv_out, w_out, one_out, two_out):
    core = where[1]
    half = mine.shape[1] - EXTRA
    local = w_out.shape[1] // CHIPS
    total = jnp.zeros((EXTRA, local), f32)
    for k, ref in ((core, mine), (1 - core, other)):
        rows = rows_at(k * half, half)
        for b in range(CHIPS):
            for p in range(3):
                to = (p * CHIPS + b) * local
                qkv_out[rows, to : to + local] = ref[b, :half, p * local : (p + 1) * local].astype(f32)
            w_out[rows, b * local : (b + 1) * local] = ref[b, :half, 3 * local :].astype(f32)
            total = total + ref[b, half:, :local].astype(f32)
    one_out[...] = total[0]
    two_out[...] = total[1]


def shards(tokens, norm_gain, w_qkv, w_out, ffn_gain, w_in, w_back, seq_ids, cotangent):
    length, width = tokens.shape[1:]
    me = lax.axis_index("seq")
    seq_count = lax.axis_size("seq")
    edges = seq_count > MEMBERS
    group = me // MEMBERS
    chip = (me % MEMBERS) // CORES
    core = me % CORES
    local = width // CHIPS
    units = FF // CHIPS
    many = CHIPS * length
    half = width // PLANES // CORES
    lanes = width // CORES
    extent = length + 2 * HALF
    kept = half + EXTRA
    in_lanes = 2 * units + width + lanes
    in_sent = lanes + 2 * units
    ffn_lanes = 2 * units + lanes
    qkv_lanes = 4 * local

    out_rows = w_out.shape[0] // CHIPS
    piece = call(
        qkv_piece_kernel,
        "qkv_piece",
        shape(kept + 32, 3 * local),
        w_qkv,
        lax.dynamic_slice(w_out, (chip * out_rows, core * lanes), (out_rows, lanes)),
        jnp.stack([norm_gain, ffn_gain]),
        held=1,
        scratch=(pltpu.VMEM((half, 3 * width), bf16), pltpu.SemaphoreType.DMA((1,))),
    )
    pieces = over_planes(piece)
    both = jnp.concatenate([tokens[0], cotangent[0]], axis=0)
    both_near = swap_seq(both, 2 * CORES)
    xs = [tokens[0], swap_seq(tokens[0], CORES), both_near, swap_seq(tokens[0], 3 * CORES)]
    mine, out_own = call(
        qkv_place_kernel,
        "qkv_place",
        (
            shape(PLANES, kept, 3 * local),
            shape(PLANES, out_rows, lanes),
        ),
        *pieces,
    )
    piece = call(
        ffn_piece_kernel,
        "ffn_piece",
        shape(half, in_sent),
        w_in,
        w_back,
        held=2,
        scratch=(
            pltpu.VMEM((half, 2 * FF), bf16),
            pltpu.VMEM((w_back.shape[0], lanes), bf16),
            pltpu.SemaphoreType.DMA((2,)),
        ),
        after=(mine,),
    )
    in_near = swap_shard(piece, 1)
    out_near = swap_seq(out_own, CORES)
    other = swap_core(mine)

    block = (group * CHIPS + (chip ^ jnp.arange(CHIPS))) * CORES + core
    position = (block[:, None] * length + jnp.arange(length)[None]).astype(f32).reshape(many)
    frequency = 10000.0 ** (-jnp.arange(0, HEAD_DIM, 2).astype(f32) / HEAD_DIM)
    angles = position[:, None] * jnp.tile(frequency, 4)[None]
    cosine, sine = jnp.cos(angles), jnp.sin(angles)
    spans = length // HALF
    ids = jnp.pad(seq_ids[0], (1, 1), constant_values=-1)
    key_ids = jnp.stack(
        [lax.dynamic_slice_in_dim(ids, block[j] * spans, spans + 2, 0) for j in range(CHIPS)]
    )
    key_ids = jnp.repeat(key_ids, HALF, axis=1)
    query_ids = key_ids[:, HALF : HALF + length]
    offset = jnp.arange(extent)[None, :] - HALF - jnp.arange(length)[:, None]
    allowed = (jnp.abs(offset) <= HALF)[None] & (query_ids[:, :, None] == key_ids[:, None, :])
    bias = jnp.where(allowed, 0.0, -1e30).astype(f32)

    low_one, query, kv, wq, gains = call(
        qkv_kernel,
        "qkv",
        (
            shape(many, width),
            shape(CHIPS, length, local),
            shape(CHIPS, length, 2 * local),
            shape(width, 3 * local),
            shape(8, width, dtype=f32),
        ),
        *xs,
        mine,
        other,
        cosine,
        sine,
    )
    kv_other = swap_core(kv)

    def beyond(value):
        pairs = []
        for m in range(seq_count):
            to = m - MEMBERS + 1 if m % CORES == 0 else m + MEMBERS - 1
            if 0 <= to < seq_count:
                pairs.append((m, to))
        return lax.ppermute(value, "seq", pairs)

    rim = ()
    if edges:
        first = lax.dynamic_index_in_dim(kv, chip, 0, False)[:HALF]
        last = lax.dynamic_index_in_dim(kv, chip ^ (CHIPS - 1), 0, False)[length - HALF :]
        rim = (beyond(jnp.where(core == 0, first, last)),)

    out_pair = call(pair_kernel, "out_pair", shape(2, *out_own.shape), out_own, out_near, after=(gains,))
    out_far = swap_seq(out_pair, 2 * CORES)
    in_pair = call(
        pair_kernel, "in_pair", shape(2, half, in_sent), piece, in_near, after=(out_pair,)
    )
    in_far = swap_shard(in_pair, 2)
    up_pair = call(up_pair_kernel, "up_pair", shape(2, length, width), cotangent[0], both_near, after=(gains,))
    gys = (up_pair, swap_seq(up_pair, CORES))
    attn = call(
        functools.partial(attend_kernel, edges),
        "attend",
        shape(CHIPS, length, local),
        query,
        kv,
        kv_other,
        bias,
        *rim,
    )
    last_attn = call(copy_kernel, "attn_copy", shape(*attn.shape), attn, after=(gys[1],))
    attns = [attn, swap_seq(attn, CORES), swap_seq(attn, 2 * CORES), swap_seq(last_attn, 3 * CORES)]
    in_mine = call(
        ffn_place_kernel,
        "ffn_place",
        shape(PLANES, half, in_lanes),
        in_pair,
        in_far,
        out_pair,
        out_far,
        after=tuple(attns[1:]),
    )
    in_other = swap_core(in_mine)
    own, d1, d2, d3, hidden, low_two, hidden_low, grad_expanded, gain_two, wb, wo = call(
        ffn_kernel,
        "ffn",
        (shape(length, width, dtype=f32),)
        + (shape(length, width),) * 3
        + (
            shape(length, width, dtype=f32),
            shape(many, width),
            shape(many, units),
            shape(many, 2 * units),
            shape(8, width, dtype=f32),
            shape(units, width),
            shape(local, width),
        ),
        *attns,
        *xs,
        *gys,
        in_mine,
        in_other,
        gains,
        scratch=(pltpu.VMEM((width, 2 * units), bf16), pltpu.VMEM((width, width), bf16)),
    )
    received = [swap_seq(d, CORES * (j + 1)) for j, d in enumerate((d1, d2, d3))]
    keep_ffn, away = call(
        ffn_grads_kernel,
        "ffn_grads",
        (shape(PLANES, half, ffn_lanes, dtype=f32), shape(PLANES, half, ffn_lanes)),
        low_two,
        hidden_low,
        grad_expanded,
        *gys,
        scratch=(pltpu.VMEM((width, 2 * units), f32), pltpu.VMEM((CORES, units, lanes), f32)),
    )
    got_ffn = swap_core(away)
    near, far = call(
        ffn_split_kernel,
        "ffn_split",
        (shape(2, half, ffn_lanes, dtype=f32), shape(2, half, ffn_lanes)),
        keep_ffn,
        got_ffn,
    )
    got_far = swap_shard(far, 2)
    dh, dh_low = call(
        dh_kernel, "dh", (shape(length, width, dtype=f32), shape(length, width)), own, *received, gys[0], hidden, gains, after=(far,)
    )
    dhs = over_chips(dh_low)
    partial_mixed = call(
        mixed_kernel,
        "mixed",
        (shape(length, width, dtype=f32),) + (shape(length, width),) * 3,
        hidden_low,
        wb,
        after=(dh_low,),
    )
    got_mixed = [swap_seq(o, CORES * (j + 1)) for j, o in enumerate(partial_mixed[1:])]

    backs = call(
        functools.partial(attend_back_kernel, edges),
        "attend_back",
        (
            shape(CHIPS, length, local, dtype=f32),
            shape(CHIPS, length, 2 * local, dtype=f32),
            shape(CHIPS, length, 2 * local),
        )
        + ((shape(HALF, 2 * local),) if edges else ()),
        query,
        kv,
        kv_other,
        bias,
        *dhs,
        wo,
        *rim,
        after=(far,),
    )
    dq, dkv, back = backs[:3]
    back = swap_core(back)
    if edges:
        rim = (beyond(backs[3]),)

    def over_groups(total, kept_type):
        step = MEMBERS
        while step < seq_count:
            total = total + swap_seq(total.astype(bf16), step).astype(f32)
            step *= 2
        return total.astype(kept_type)

    def summed(own, parts, name, after=()):
        out = call(
            sum_kernel, name, shape(*own.shape, dtype=f32 if edges else bf16), own, *parts, after=after
        )
        return over_groups(out, bf16)

    mixed = call(
        mixed_sum_kernel, "mixed_sum", shape(1, length, width), partial_mixed[0], *got_mixed, hidden, after=(dq,)
    )

    keep, away, dqkv = call(
        functools.partial(qkv_grads_kernel, edges),
        "qkv_grads",
        (
            shape(PLANES, half, qkv_lanes, dtype=f32),
            shape(PLANES, half, qkv_lanes),
            shape(many, 3 * local),
        ),
        dq,
        dkv,
        back,
        cosine,
        sine,
        low_one,
        *attns,
        *dhs,
        *rim,
        scratch=(pltpu.VMEM((width, qkv_lanes), f32), pltpu.VMEM((many, local), bf16)),
    )
    got = swap_core(away)
    own_ffn, sent_near = call(
        ffn_near_kernel,
        "ffn_near",
        (shape(half, ffn_lanes, dtype=f32), shape(half, ffn_lanes)),
        near,
        got_far,
        after=(dq,),
    )
    total = call(
        ffn_total_kernel,
        "ffn_total",
        shape(half, ffn_lanes, dtype=f32 if edges else bf16),
        own_ffn,
        swap_shard(sent_near, 1),
        after=(got,),
    )
    total = over_groups(total, bf16)
    last_own, o1, o2, o3, gain_sums = call(
        da_kernel,
        "da",
        (shape(length, width, dtype=f32),)
        + (shape(length, width),) * 3
        + (shape(PLANES, EXTRA, qkv_lanes, dtype=f32),),
        dqkv,
        wq,
        *xs,
        gain_two,
        after=(mixed,),
    )
    sent = call(
        to_planes_gains_kernel,
        "qkv_to_planes",
        (shape(kept, qkv_lanes, dtype=f32),)
        + (shape(kept, qkv_lanes),) * 3,
        keep,
        got,
        gain_sums,
    )
    got = [swap_shard(s, i + 1) for i, s in enumerate(sent[1:4])]
    packet = shape(length + half + 32, width)
    packets = call(last_packet_kernel, "last_packet", (packet,) * 2, total, o1, o2, after=(sent[1],))
    packets += call(last_packet_kernel, "third_packet", (packet,), total, o3, after=(got[0],))
    received = [swap_seq(o, CORES * (j + 1)) for j, o in enumerate(packets)]

    mine = call(
        ffn_gather_kernel,
        "ffn_gather",
        shape(CHIPS, half, ffn_lanes),
        total,
        *received,
    )
    owned_in, owned_back = call(
        ffn_owned_kernel,
        "ffn_owned",
        (shape(*w_in.shape, dtype=f32), shape(*w_back.shape, dtype=f32)),
        mine,
        swap_core(mine),
    )
    grad_tokens = call(
        last_kernel,
        "last",
        shape(1, length, width),
        last_own,
        *received,
        xs[0],
        dh,
        gains,
        after=(sent[1],),
    )
    mine = call(
        functools.partial(place_kernel, 0),
        "qkv_gather",
        shape(CHIPS, kept, qkv_lanes),
        *over_chips(summed(sent[0], got, "qkv_sum")),
        after=(grad_tokens, owned_back),
    )
    owned_qkv, owned_out, grad_gain_one, grad_gain_two = call(
        qkv_owned_kernel,
        "qkv_owned",
        (
            shape(*w_qkv.shape, dtype=f32),
            shape(*w_out.shape, dtype=f32),
            shape(local, dtype=f32),
            shape(local, dtype=f32),
        ),
        mine,
        swap_core(mine),
    )
    return (mixed, grad_tokens, grad_gain_one, owned_qkv, owned_out, grad_gain_two, owned_in, owned_back)


def solution(mesh):
    return jax.shard_map(
        shards,
        mesh=mesh,
        in_specs=(
            P("shard", "seq", None),
            P("shard"),
            P("shard", None),
            P("shard", None),
            P("shard"),
            P("shard", None),
            P("shard", None),
            P("shard", None),
            P("shard", "seq", None),
        ),
        out_specs=(
            P("shard", "seq", None),
            P("shard", "seq", None),
            P("shard"),
            P("shard", None),
            P("shard", None),
            P("shard"),
            P("shard", None),
            P("shard", None),
        ),
        check_vma=False,
    )
```

```python
import functools
import math

import jax
import jax.numpy as jnp
from jax import lax
from jax.experimental import pallas as pl
from jax.experimental.pallas import tpu as pltpu
from jax.sharding import PartitionSpec as P

HEADS = 12
HEAD_DIM = 64
FF = 1152
HALF = 64
CHIPS = 4
CORES = 2
MEMBERS = CHIPS * CORES
PLANES = 4
EXTRA = 16
f32 = jnp.float32
bf16 = jnp.bfloat16
SCALE = HEAD_DIM ** (-0.5)
ROOM = 6 * 1024 * 1024


TIMES = {
    "qkv_piece": 0.5,
    "ffn_piece": 1,
    "qkv_place": 0.8,
    "qkv": 3.2,
    "attend": 2.3,
    "ffn_place": 1.2,
    "ffn": 4.5,
    "ffn_grads": 1.6,
    "dh": 0.4,
    "mixed": 0.6,
    "ffn_split": 1,
    "mixed_sum": 0.4,
    "attend_back": 6.9,
    "qkv_grads": 2.4,
    "da": 1.5,
    "qkv_to_planes": 0.8,
    "qkv_gather": 0.6,
    "last_packet": 0.5,
    "ffn_total": 0.4,
    "ffn_gather": 0.5,
    "qkv_sum": 0.4,
    "last": 0.6,
    "ffn_owned": 2.2,
    "qkv_owned": 1.7,
}


def dot(left, right):
    return lax.dot_general(left, right, (((1,), (0,)), ((), ())), preferred_element_type=f32)


def dot_t(left, right):
    return lax.dot_general(left, right, (((1,), (1,)), ((), ())), preferred_element_type=f32)


def t_dot(left, right):
    return lax.dot_general(left, right, (((0,), (0,)), ((), ())), preferred_element_type=f32)


def swap_seq(value, bits):
    count = lax.axis_size("seq")
    return lax.ppermute(value, "seq", [(i, i ^ bits) for i in range(count)])


def swap_shard(value, bits):
    count = lax.axis_size("shard")
    return lax.ppermute(value, "shard", [(i, i ^ bits) for i in range(count)])


def swap_core(value):
    return swap_seq(value, 1)


def over_chips(value):
    return [value] + [swap_seq(value, CORES * j) for j in range(CHIPS - 1, 0, -1)][::-1]


def over_planes(value):
    return [value] + [swap_shard(value, i) for i in range(1, PLANES)]


def shape(*dims, dtype=bf16):
    return jax.ShapeDtypeStruct(dims, dtype)


def places():
    me = lax.axis_index("seq")
    return (me % MEMBERS) // CORES, me % CORES, lax.axis_index("shard")


def size_of(value):
    return math.prod(value.shape) * jnp.dtype(value.dtype).itemsize


def call(kernel, name, outs, *operands, after=(), scratch=(), held=0):
    taken = len(operands)
    specs = [pl.BlockSpec(memory_space=pltpu.HBM)] * held
    specs += [pl.BlockSpec(memory_space=pltpu.VMEM)] * (taken - held)
    specs += [pl.BlockSpec(memory_space=pl.ANY)] * len(after)
    us = TIMES.get(name, 0.5)
    held_size = sum(size_of(o) for o in operands[held:])
    held_size += sum(size_of(o) for o in jax.tree.leaves(outs))

    def body(*refs):
        kernel(places(), *refs[:taken], *refs[taken + len(after) :])

    return pl.pallas_call(
        body,
        out_shape=outs,
        in_specs=specs,
        out_specs=jax.tree.map(lambda _: pl.BlockSpec(memory_space=pltpu.VMEM), outs),
        scratch_shapes=list(scratch),
        cost_estimate=pl.CostEstimate(
            flops=int(us * 2e10), bytes_accessed=int(us * 10), transcendentals=0
        ),
        compiler_params=pltpu.CompilerParams(vmem_limit_bytes=2 * held_size + ROOM),
        name=name,
    )(*operands, *after)


def norm_parts(values):
    center = values - jnp.mean(values, axis=-1, keepdims=True)
    factor = lax.rsqrt(jnp.mean(center * center, axis=-1, keepdims=True) + 1e-05)
    return center * factor, factor


def norm_inward(upward, gain, normed, factor):
    scaled = upward * gain
    return factor * (
        scaled
        - jnp.mean(scaled, axis=-1, keepdims=True)
        - normed * jnp.mean(scaled * normed, axis=-1, keepdims=True)
    )


def first_half(shape_of):
    return lax.broadcasted_iota(jnp.int32, shape_of, 1) % HEAD_DIM < HEAD_DIM // 2


def shifted(values):
    return pltpu.roll(values, 96, 1), pltpu.roll(values, 32, 1)


def rows_at(start, size):
    return pl.ds(pl.multiple_of(start, 16), size)


def lanes_at(start, size):
    return pl.ds(pl.multiple_of(start, 128), size)


def extra_rows(first, second, lanes):
    row = lax.broadcasted_iota(jnp.int32, (EXTRA, lanes), 0)
    pad = jnp.zeros((1, lanes - first.shape[1]), f32)
    first = jnp.concatenate([first, pad], axis=1)
    second = jnp.concatenate([second, pad], axis=1)
    return jnp.where(row == 0, first, jnp.where(row == 1, second, 0.0))


def copied(pairs, sems):
    copies = [pltpu.make_async_copy(src, dst, sems.at[i]) for i, (src, dst) in enumerate(pairs)]
    for copy in copies:
        copy.start()
    for copy in copies:
        copy.wait()


def qkv_piece_kernel(where, w_qkv, part, gains, out, rows, sems):
    chip, core = where[0], where[1]
    half = w_qkv.shape[0] // CORES
    width = w_qkv.shape[1] // 3
    local = width // CHIPS
    size, lanes = part.shape
    copied(((w_qkv.at[rows_at(core * half, half), :], rows),), sems)
    for b in range(CHIPS):

        @pl.when(chip == b)
        def _():
            for p in range(3):
                at = p * width + b * local
                out[:half, p * local : (p + 1) * local] = rows[:, at : at + local]

    both = gains[...].astype(f32)[None]
    share = both.shape[1] // 2
    out[half:, :] = extra_rows(both[:, :share], both[:, share:], out.shape[1]).astype(bf16)
    out[:size, 3 * local :] = part[:, :local]
    out[size:half, 3 * local :] = part[:, local:]


def ffn_piece_kernel(where, w_in, w_back, out, rows, back, sems):
    chip, core = where[0], where[1]
    half = w_in.shape[0] // CORES
    units = FF // PLANES // CHIPS
    lanes = back.shape[1]
    copied(
        (
            (w_in.at[rows_at(core * half, half), :], rows),
            (w_back.at[:, lanes_at(core * lanes, lanes)], back),
        ),
        sems,
    )
    spare = half - units
    side = units * lanes // half
    rest = lanes - side
    at_back = 2 * PLANES * units
    for b in range(CHIPS):

        @pl.when(chip == b)
        def _():
            for p in range(2):
                for z in range(PLANES):
                    at = p * FF + z * units * CHIPS + b * units
                    to = (p * PLANES + z) * units
                    out[:, to : to + units] = rows[:, at : at + units]
            own = back[b * units : (b + 1) * units, :]
            out[:units, at_back:] = own[:, :side]
            for i in range(units // spare):
                to = at_back + i * rest
                out[units:, to : to + rest] = own[i * spare : (i + 1) * spare, side:]


def unpacked(block, units):
    spare = block.shape[0] - units
    rest = block.shape[1] // (units // spare)
    last = [block[units:, i * rest : (i + 1) * rest] for i in range(units // spare)]
    return jnp.concatenate([block[:units], jnp.concatenate(last, axis=0)], axis=1)


def place_kernel(slot, where, p0, p1, p2, p3, out):
    for i, ref in enumerate((p0, p1, p2, p3)):
        out[where[slot] ^ i] = ref[...]


def qkv_place_kernel(where, p0, p1, p2, p3, out, packet):
    lanes = out.shape[2]
    size = packet.shape[1]
    for i, ref in enumerate((p0, p1, p2, p3)):
        z = where[2] ^ i
        out[z] = ref[:, :lanes]
        packet[z] = jnp.concatenate([ref[:size, lanes:], ref[size : 2 * size, lanes:]], axis=1)


def up_pair_kernel(where, own, both, out):
    out[0] = own[...]
    out[1] = both[own.shape[0] :, :]


def last_packet_kernel(where, total, *refs):
    half, lanes = total.shape
    rows, width = refs[0].shape
    spare = lanes - width
    for ref, out in zip(refs[: len(refs) // 2], refs[len(refs) // 2 :]):
        out[:rows, :] = ref[...]
        out[rows : rows + half, :] = total[:, :width]
        for i in range(half // 32):
            at = slice(i * spare, (i + 1) * spare)
            out[rows + half :, at] = total[i * 32 : (i + 1) * 32, width:]
        blank = width - half // 32 * spare
        out[rows + half :, width - blank :] = jnp.zeros((32, blank), bf16)


def ffn_gather_kernel(where, total, r1, r2, r3, out):
    half, lanes = total.shape
    width = r1.shape[1]
    spare = lanes - width
    rows = r1.shape[0] - half - 32
    out[where[0]] = total[...]
    for j, ref in enumerate((r1, r2, r3)):
        at = where[0] ^ (j + 1)
        out[at, :, :width] = ref[rows : rows + half, :]
        for i in range(half // 32):
            piece = ref[rows + half :, i * spare : (i + 1) * spare]
            out[at, i * 32 : (i + 1) * 32, width:] = piece


def pair_kernel(where, first, second, out):
    out[0] = first[...]
    out[1] = second[...]


def ffn_place_kernel(where, near, far, p01, p23, out):
    half = near.shape[1]
    p0, p1, p2, p3 = p01.at[0], p01.at[1], p23.at[0], p23.at[1]
    size, lanes = p0.shape[1:]
    for i, ref in enumerate((near.at[0], near.at[1], far.at[0], far.at[1])):
        z = where[2] ^ i
        out[z, :, 2 * lanes :] = ref[...]
    for i, ref in enumerate((p0, p1, p2, p3)):
        b = where[0] ^ i
        at = rows_at((b % 2) * size, size)

        for half_at in range(2):

            @pl.when(b // 2 == half_at)
            def _():
                for z in range(PLANES):
                    out[z, at, half_at * lanes : (half_at + 1) * lanes] = ref[z]


def qkv_kernel(where, x0, x1, x2, x3, mine, other, cos, sin, a_out, q_out, kv_out, w_out, g_out):
    rows = x0.shape[0]
    half = mine.shape[1] - EXTRA
    local = mine.shape[2] // 3
    share = CORES * half
    core = where[1]
    for z in range(PLANES):
        w_out[rows_at(z * share + core * half, half), :] = mine[z, :half, :]
        w_out[rows_at(z * share + (1 - core) * half, half), :] = other[z, :half, :]
        tail = mine[z, half:, :share].astype(f32)
        g_out[:, z * share : (z + 1) * share] = tail[:8]
    gain = g_out[0:1, :]
    for j, ref in enumerate((x0, x1, x2, x3)):
        normed, _ = norm_parts(ref[:rows, :].astype(f32))
        a_out[j * rows : (j + 1) * rows, :] = (normed * gain).astype(bf16)
    out = dot(a_out[...], w_out[...])
    front = first_half((CHIPS * rows, 128))
    parts = []
    for at in range(0, 2 * local, 128):
        u = out[:, at : at + 128]
        up, down = shifted(u)
        parts.append((u * cos[...] + jnp.where(front, -up, down) * sin[...]).astype(bf16))
    qk = jnp.concatenate(parts, axis=1)
    value = out[:, 2 * local :].astype(bf16)
    for j in range(CHIPS):
        at = slice(j * rows, (j + 1) * rows)
        q_out[j] = qk[at, :local]
        kv_out[j, :, :local] = qk[at, local:]
        kv_out[j, :, local:] = value[at]


def block_of(pairs, j, local):
    return pairs[j // 2, :, j % 2 * local : (j % 2 + 1) * local]


def extended(where, j, kv, other, rim):
    chip, core = where[0], where[1]
    length = kv.shape[1]
    b = chip ^ j
    below = jnp.where(core == 0, jnp.maximum(b - 1, 0), b) ^ chip
    above = jnp.where(core == 0, b, jnp.minimum(b + 1, CHIPS - 1)) ^ chip
    before = other[below, length - HALF :, :]
    after = other[above, :HALF, :]
    if rim is not None:
        before = jnp.where((core == 0) & (b == 0), rim[...], before)
        after = jnp.where((core == 1) & (b == CHIPS - 1), rim[...], after)
    return jnp.concatenate([before, kv[j], after], axis=0)


def probs_of(q, k, bias):
    logits = dot_t(q, k) * SCALE + bias
    highest = jnp.max(logits, axis=-1, keepdims=True)
    exponent = jnp.exp(logits - highest)
    return exponent / jnp.sum(exponent, axis=-1, keepdims=True)


def attend_kernel(edges, where, q, kv, other, bias, *rest):
    rim, out, kept = rest if edges else (None, *rest)
    local = q.shape[-1]
    extent = bias.shape[-1]
    for j in range(CHIPS):
        ext = extended(where, j, kv, other, rim)
        parts = []
        for h in range(local // HEAD_DIM):
            lanes = slice(h * HEAD_DIM, (h + 1) * HEAD_DIM)
            prob = probs_of(q[j, :, lanes], ext[:, lanes], bias[j]).astype(bf16)
            kept[j, :, h * extent : (h + 1) * extent] = prob
            parts.append(dot(prob, ext[:, local + h * HEAD_DIM : local + (h + 1) * HEAD_DIM]))
        out[j // 2, :, j % 2 * local : (j % 2 + 1) * local] = jnp.concatenate(parts, axis=1).astype(bf16)


def ffn_kernel(
    where, t0, t1, t2, t3, x0, x1, x2, x3, y02, y13, mine, other, gains,
    own_out, d1_out, d2_out, d3_out, hid_out, a_out, m_out, dgu_out, gain_out, wb_out, wc_out,
    wi, wo,
):
    chip, core = where[0], where[1]
    rows = x0.shape[0]
    width = x0.shape[1]
    half = mine.shape[1]
    share = CORES * half
    units = FF // CHIPS
    part = units // PLANES
    lanes = width // CORES
    local = width // CHIPS
    for z in range(PLANES):
        for k, ref in ((core, mine), (1 - core, other)):
            wi[rows_at(z * share + k * half, half), :] = ref[z, :, width : width + 2 * units]
            for p in range(CORES):
                at = slice(z * share + p * half, z * share + (p + 1) * half)
                wo[at, lanes_at(k * lanes, lanes)] = ref[z, :, p * lanes : (p + 1) * lanes]
    own_back, other_back = [
        jnp.concatenate(
            [unpacked(ref[z, :, width + 2 * units :], part) for z in range(PLANES)], axis=0
        )
        for ref in (mine, other)
    ]
    wb_out[:, :lanes] = jnp.where(core == 0, own_back, other_back)
    wb_out[:, lanes:] = jnp.where(core == 0, other_back, own_back)
    wc_out[...] = wo[rows_at(chip * local, local), :]
    xs = (x0, x1, x2, x3)
    gain = gains[1:2, :]
    outward = [
        (ref, wo[rows_at((chip ^ i) * local, local), :]) for i, ref in enumerate((t0, t1, t2, t3))
    ]
    normed = []
    for j in range(CHIPS):
        hidden = xs[j][:rows, :].astype(f32)
        for i, (ref, weight) in enumerate(outward):
            hidden = hidden + dot(block_of(ref, j ^ i, local), weight)
        if j == 0:
            hid_out[...] = hidden
        norm, _ = norm_parts(hidden)
        normed.append(norm)
        a_out[j * rows : (j + 1) * rows, :] = (norm * gain).astype(bf16)
    total = jnp.zeros((1, width), f32)
    for j in range(CHIPS):
        at = slice(j * rows, (j + 1) * rows)
        gu = dot(a_out[at, :], wi[...])
        entering, gating = gu[:, :units], gu[:, units:]
        rise = 0.5 * (1.0 + lax.erf(entering * (0.5**0.5)))
        slope = rise + entering * jnp.exp(-0.5 * entering * entering) * 0.3989422804014327
        act = entering * rise
        m_out[at, :] = (act * gating).astype(bf16)
        dm = dot_t((y02, y13)[j % 2][j // 2], wb_out[...])
        dgu = jnp.concatenate([dm * gating * slope, dm * act], axis=1).astype(bf16)
        dgu_out[at, :] = dgu
        da = dot_t(dgu, wi[...])
        total = total + jnp.sum(da * normed[j], axis=0, keepdims=True)
        if j == 0:
            own_out[...] = da
        else:
            (d1_out, d2_out, d3_out)[j - 1][...] = da.astype(bf16)
    gain_out[...] = jnp.broadcast_to(total, gain_out.shape)


def mixed_kernel(where, m, wb, own, m1, m2, m3):
    rows = own.shape[0]
    own[...] = dot(m[:rows, :], wb[...])
    for j, ref in enumerate((m1, m2, m3)):
        ref[...] = dot(m[(j + 1) * rows : (j + 2) * rows, :], wb[...]).astype(bf16)


def mixed_sum_kernel(where, own, r1, r2, r3, hidden, out):
    total = own[...] + r1[...].astype(f32) + r2[...].astype(f32) + r3[...].astype(f32)
    out[0] = (hidden[...] + total).astype(bf16)


def ffn_grads_kernel(where, a, m, dgu, y02, y13, keep, away, gin, gb):
    core = where[1]
    half = keep.shape[1]
    share = CORES * half
    units = m.shape[1]
    part = units // PLANES
    lanes = y02.shape[2] // CORES
    gin[...] = t_dot(a[...], dgu[...])
    upward = jnp.concatenate([y02[0], y13[0], y02[1], y13[1]], axis=0)
    back = t_dot(m[...], upward)
    first, second = back[:, :lanes], back[:, lanes:]
    gb[0] = jnp.where(core == 0, first, second)
    gb[1] = jnp.where(core == 0, second, first)
    for z in range(PLANES):
        at = slice(z * part, (z + 1) * part)
        blank = jnp.zeros((half - part, lanes), f32)
        keep[z, :, : 2 * units] = gin[rows_at(z * share + core * half, half), :]
        keep[z, :, 2 * units :] = jnp.concatenate([gb[0, at, :], blank], axis=0)
        away[z, :, : 2 * units] = gin[rows_at(z * share + (1 - core) * half, half), :].astype(bf16)
        away[z, :, 2 * units :] = jnp.concatenate([gb[1, at, :], blank], axis=0).astype(bf16)


def dh_kernel(where, own, r1, r2, r3, y02, hidden, gains, dh_out, low_out):
    total = own[...] + r1[...].astype(f32) + r2[...].astype(f32) + r3[...].astype(f32)
    normed, factor = norm_parts(hidden[...])
    dh = y02[0].astype(f32) + norm_inward(total, gains[1:2, :], normed, factor)
    dh_out[...] = dh
    low_out[...] = dh.astype(bf16)


def attend_back_kernel(edges, where, q, kv, other, probs, h0, h1, h2, h3, w_out, *rest):
    rim, rest = (rest[0], rest[1:]) if edges else (None, rest)
    dq_out, dkv_out, back_out = rest[:3]
    chip, core = where[0], where[1]
    local = q.shape[-1]
    length = q.shape[1]
    extent = length + 2 * HALF
    back_out[...] = jnp.zeros_like(back_out)
    for j, dh in enumerate((h0, h1, h2, h3)):
        dctx = dot_t(dh[...], w_out[...]).astype(bf16)
        ext = extended(where, j, kv, other, rim)
        dqs, dks, dvs = [], [], []
        for h in range(local // HEAD_DIM):
            lanes = slice(h * HEAD_DIM, (h + 1) * HEAD_DIM)
            qh = q[j, :, lanes]
            kh = ext[:, lanes]
            vh = ext[:, local + h * HEAD_DIM : local + (h + 1) * HEAD_DIM]
            dch = dctx[:, lanes]
            low = probs[j, :, h * extent : (h + 1) * extent]
            prob = low.astype(f32)
            dprob = dot_t(dch, vh)
            inner = jnp.sum(prob * dprob, axis=-1, keepdims=True)
            dscore = (prob * (dprob - inner) * SCALE).astype(bf16)
            dqs.append(dot(dscore, kh))
            dks.append(t_dot(dscore, qh))
            dvs.append(t_dot(low, dch))
        dq_out[j] = jnp.concatenate(dqs, axis=1)
        grads = jnp.concatenate(dks + dvs, axis=1)
        dkv_out[j] = grads[HALF : HALF + length]
        before = grads[:HALF].astype(bf16)
        after = grads[HALF + length :].astype(bf16)
        b = chip ^ j
        below = jnp.where(core == 0, b - 1, b)
        above = jnp.where(core == 0, b, b + 1)

        @pl.when(below >= 0)
        def _():
            back_out[jnp.maximum(below, 0) ^ chip, length - HALF :, :] = before

        @pl.when(above < CHIPS)
        def _():
            back_out[jnp.minimum(above, CHIPS - 1) ^ chip, :HALF, :] = after

        if edges:
            rim_out = rest[3]

            @pl.when(below < 0)
            def _():
                rim_out[...] = before

            @pl.when(above >= CHIPS)
            def _():
                rim_out[...] = after


def qkv_grads_kernel(edges, where, dq, dkv, back, cos, sin, a, t0, t1, t2, t3, h0, h1, h2, h3, *rest):
    rim, rest = (rest[0], rest[1:]) if edges else (None, rest)
    keep, away, d_out, acc, cols = rest
    chip, core = where[0], where[1]
    length = dq.shape[1]
    local = dq.shape[2]
    width = a.shape[1]
    front = first_half((length, 128))
    for j in range(CHIPS):
        at = slice(j * length, (j + 1) * length)
        gkv = dkv[j] + back[j].astype(f32)
        if edges:
            b = chip ^ j
            blank = jnp.zeros((length - HALF, 2 * local), f32)
            value = rim[...].astype(f32)
            gkv = gkv + jnp.where(
                (core == 0) & (b == 0), jnp.concatenate([value, blank], axis=0), 0.0
    )
            gkv = gkv + jnp.where(
                (core == 1) & (b == CHIPS - 1), jnp.concatenate([blank, value], axis=0), 0.0
    )
        g = jnp.concatenate([dq[j], gkv[:, :local]], axis=1)
        for lane in range(0, 2 * local, 128):
            u = g[:, lane : lane + 128]
            up, down = shifted(u * sin[at, :])
            d_out[at, lane : lane + 128] = (
                u * cos[at, :] + jnp.where(front, up, -down)
            ).astype(bf16)
        d_out[at, 2 * local :] = gkv[:, local:].astype(bf16)
    acc[:, : 3 * local] = t_dot(a[...], d_out[...])
    for b in range(CHIPS):

        @pl.when(chip == b)
        def _():
            for j, ref in enumerate((h0, h1, h2, h3)):
                cols[j * length : (j + 1) * length, :] = ref[:, b * local : (b + 1) * local]

    for i, ref in enumerate((t0, t1, t2, t3)):
        rows = jnp.concatenate([block_of(ref, j ^ i, local) for j in range(CHIPS)], axis=0)
        acc[rows_at((chip ^ i) * local, local), 3 * local :] = t_dot(rows, cols[...])
    half = keep.shape[1]
    share = CORES * half
    for z in range(PLANES):
        keep[z] = acc[rows_at(z * share + core * half, half), :]
        away[z] = acc[rows_at(z * share + (1 - core) * half, half), :].astype(bf16)


def da_kernel(where, d, w, x0, x1, x2, x3, gain_two, own_out, o1, o2, o3, gain_out):
    rows = x0.shape[0]
    total = jnp.zeros((1, w.shape[0]), f32)
    for j, ref in enumerate((x0, x1, x2, x3)):
        da = dot_t(d[j * rows : (j + 1) * rows, :], w[...])
        normed, _ = norm_parts(ref[:rows, :].astype(f32))
        total = total + jnp.sum(da * normed, axis=0, keepdims=True)
        if j == 0:
            own_out[...] = da
        else:
            (o1, o2, o3)[j - 1][...] = da.astype(bf16)
    share = w.shape[0] // PLANES
    for z in range(PLANES):
        at = slice(z * share, (z + 1) * share)
        gain_out[z] = extra_rows(total[:, at], gain_two[0:1, at], gain_out.shape[2])


def copy_kernel(where, value, out):
    out[...] = value[...]


def ffn_split_kernel(where, keep, got, near, far):
    for i in range(PLANES):
        at = where[2] ^ i
        total = keep[at] + got[at].astype(f32)
        if i < 2:
            near[i] = total
        else:
            far[i - 2] = total.astype(bf16)


def ffn_near_kernel(where, near, got, own, sent):
    own[...] = near[0] + got[0].astype(f32)
    sent[...] = (near[1] + got[1].astype(f32)).astype(bf16)


def ffn_total_kernel(where, own, got, out):
    out[...] = (own[...] + got[...].astype(f32)).astype(out.dtype)


def to_planes_gains_kernel(where, keep, got, gains, own, o1, o2, o3):
    plane = where[2]
    half = keep.shape[1]
    own[:half, :] = keep[plane] + got[plane].astype(f32)
    own[half:, :] = gains[plane]
    for i, ref in enumerate((o1, o2, o3)):
        at = plane ^ (i + 1)
        ref[:half, :] = (keep[at] + got[at].astype(f32)).astype(bf16)
        ref[half:, :] = gains[at].astype(bf16)


def sum_kernel(where, own, r1, r2, r3, out):
    total = own[...] + r1[...].astype(f32) + r2[...].astype(f32) + r3[...].astype(f32)
    out[...] = total.astype(out.dtype)


def last_kernel(where, own, r1, r2, r3, x0, dh, gains, grad_out):
    total = own[...]
    for ref in (r1, r2, r3):
        total = total + ref[: own.shape[0], :].astype(f32)
    normed, factor = norm_parts(x0[...].astype(f32))
    grad = dh[...] + norm_inward(total, gains[0:1, :], normed, factor)
    grad_out[0] = grad.astype(bf16)


def ffn_owned_kernel(where, mine, other, in_out, back_out):
    core = where[1]
    half = mine.shape[1]
    units = FF // CHIPS
    part = units // PLANES
    lanes = mine.shape[2] - 2 * units
    for k, ref in ((core, mine), (1 - core, other)):
        rows = rows_at(k * half, half)
        for p in range(2):
            for z in range(PLANES):
                at = (p * PLANES + z) * part
                for b in range(CHIPS):
                    to = p * FF + (z * CHIPS + b) * part
                    in_out[rows, to : to + part] = ref[b, :, at : at + part].astype(f32)
    for b in range(CHIPS):
        own = mine[b, :part, 2 * units :].astype(f32)
        got = other[b, :part, 2 * units :].astype(f32)
        back_out[b * part : (b + 1) * part, :lanes] = jnp.where(core == 0, own, got)
        back_out[b * part : (b + 1) * part, lanes:] = jnp.where(core == 0, got, own)


def qkv_owned_kernel(where, mine, other, qkv_out, w_out, one_out, two_out):
    core = where[1]
    half = mine.shape[1] - EXTRA
    local = w_out.shape[1] // CHIPS
    total = jnp.zeros((EXTRA, local), f32)
    for k, ref in ((core, mine), (1 - core, other)):
        rows = rows_at(k * half, half)
        for b in range(CHIPS):
            for p in range(3):
                to = (p * CHIPS + b) * local
                qkv_out[rows, to : to + local] = ref[b, :half, p * local : (p + 1) * local].astype(f32)
            w_out[rows, b * local : (b + 1) * local] = ref[b, :half, 3 * local :].astype(f32)
            total = total + ref[b, half:, :local].astype(f32)
    one_out[...] = total[0]
    two_out[...] = total[1]


def shards(tokens, norm_gain, w_qkv, w_out, ffn_gain, w_in, w_back, seq_ids, cotangent):
    length, width = tokens.shape[1:]
    me = lax.axis_index("seq")
    seq_count = lax.axis_size("seq")
    edges = seq_count > MEMBERS
    group = me // MEMBERS
    chip = (me % MEMBERS) // CORES
    core = me % CORES
    local = width // CHIPS
    units = FF // CHIPS
    many = CHIPS * length
    half = width // PLANES // CORES
    lanes = width // CORES
    extent = length + 2 * HALF
    kept = half + EXTRA
    in_sent = 2 * units + units // PLANES * lanes // half
    in_lanes = width + in_sent
    ffn_lanes = 2 * units + lanes
    qkv_lanes = 4 * local

    out_rows = w_out.shape[0] // CHIPS
    piece = call(
        qkv_piece_kernel,
        "qkv_piece",
        shape(kept, 4 * local),
        w_qkv,
        lax.dynamic_slice(w_out, (chip * out_rows, core * lanes), (out_rows, lanes)),
        jnp.concatenate([norm_gain, ffn_gain]),
        held=1,
        scratch=(pltpu.VMEM((half, 3 * width), bf16), pltpu.SemaphoreType.DMA((1,))),
    )
    pieces = over_planes(piece)
    both = jnp.concatenate([tokens[0], cotangent[0]], axis=0)
    both_near = swap_seq(both, 2 * CORES)
    xs = [tokens[0], swap_seq(tokens[0], CORES), both_near, swap_seq(tokens[0], 3 * CORES)]
    mine, out_own = call(
        qkv_place_kernel,
        "qkv_place",
        (
            shape(PLANES, kept, 3 * local),
            shape(PLANES, out_rows, lanes),
        ),
        *pieces,
    )
    piece = call(
        ffn_piece_kernel,
        "ffn_piece",
        shape(half, in_sent),
        w_in,
        w_back,
        held=2,
        scratch=(
            pltpu.VMEM((half, 2 * FF), bf16),
            pltpu.VMEM((w_back.shape[0], lanes), bf16),
            pltpu.SemaphoreType.DMA((2,)),
        ),
        after=(mine,),
    )
    in_near = swap_shard(piece, 1)
    out_near = swap_seq(out_own, CORES)
    other = swap_core(mine)

    block = (group * CHIPS + (chip ^ jnp.arange(CHIPS))) * CORES + core
    position = (block[:, None] * length + jnp.arange(length)[None]).astype(f32).reshape(many)
    frequency = 10000.0 ** (-jnp.arange(0, HEAD_DIM, 2).astype(f32) / HEAD_DIM)
    angles = position[:, None] * jnp.tile(frequency, 4)[None]
    cosine, sine = jnp.cos(angles), jnp.sin(angles)
    spans = length // HALF
    ids = jnp.pad(seq_ids[0], (1, 1), constant_values=-1)
    key_ids = jnp.stack(
        [lax.dynamic_slice_in_dim(ids, block[j] * spans, spans + 2, 0) for j in range(CHIPS)]
    )
    key_ids = jnp.repeat(key_ids, HALF, axis=1)
    query_ids = key_ids[:, HALF : HALF + length]
    offset = jnp.arange(extent)[None, :] - HALF - jnp.arange(length)[:, None]
    allowed = (jnp.abs(offset) <= HALF)[None] & (query_ids[:, :, None] == key_ids[:, None, :])
    bias = jnp.where(allowed, 0.0, -1e30).astype(f32)

    low_one, query, kv, wq, gains = call(
        qkv_kernel,
        "qkv",
        (
            shape(many, width),
            shape(CHIPS, length, local),
            shape(CHIPS, length, 2 * local),
            shape(width, 3 * local),
            shape(8, width, dtype=f32),
        ),
        *xs,
        mine,
        other,
        cosine,
        sine,
    )
    kv_other = swap_core(kv)

    def beyond(value):
        pairs = []
        for m in range(seq_count):
            to = m - MEMBERS + 1 if m % CORES == 0 else m + MEMBERS - 1
            if 0 <= to < seq_count:
                pairs.append((m, to))
        return lax.ppermute(value, "seq", pairs)

    rim = ()
    if edges:
        first = lax.dynamic_index_in_dim(kv, chip, 0, False)[:HALF]
        last = lax.dynamic_index_in_dim(kv, chip ^ (CHIPS - 1), 0, False)[length - HALF :]
        rim = (beyond(jnp.where(core == 0, first, last)),)

    up_pair = call(up_pair_kernel, "up_pair", shape(2, length, width), cotangent[0], both_near, after=(gains,))
    gys = (up_pair, swap_seq(up_pair, CORES))
    out_pair = call(pair_kernel, "out_pair", shape(2, *out_own.shape), out_own, out_near, after=(up_pair,))
    out_far = swap_seq(out_pair, 2 * CORES)
    in_pair = call(
        pair_kernel, "in_pair", shape(2, half, in_sent), piece, in_near, after=(out_pair,)
    )
    in_far = swap_shard(in_pair, 2)
    attn, probs = call(
        functools.partial(attend_kernel, edges),
        "attend",
        (shape(2, length, 2 * local), shape(CHIPS, length, local // HEAD_DIM * extent)),
        query,
        kv,
        kv_other,
        bias,
        *rim,
    )
    last_attn = call(copy_kernel, "attn_copy", shape(*attn.shape), attn, after=(gys[1],))
    attns = [attn, swap_seq(attn, CORES), swap_seq(attn, 2 * CORES), swap_seq(last_attn, 3 * CORES)]
    in_mine = call(
        ffn_place_kernel,
        "ffn_place",
        shape(PLANES, half, in_lanes),
        in_pair,
        in_far,
        out_pair,
        out_far,
        after=tuple(attns[1:]),
    )
    in_other = swap_core(in_mine)
    own, d1, d2, d3, hidden, low_two, hidden_low, grad_expanded, gain_two, wb, wo = call(
        ffn_kernel,
        "ffn",
        (shape(length, width, dtype=f32),)
        + (shape(length, width),) * 3
        + (
            shape(length, width, dtype=f32),
            shape(many, width),
            shape(many, units),
            shape(many, 2 * units),
            shape(8, width, dtype=f32),
            shape(units, width),
            shape(local, width),
        ),
        *attns,
        *xs,
        *gys,
        in_mine,
        in_other,
        gains,
        scratch=(pltpu.VMEM((width, 2 * units), bf16), pltpu.VMEM((width, width), bf16)),
    )
    received = [swap_seq(d, CORES * (j + 1)) for j, d in enumerate((d1, d2, d3))]
    keep_ffn, away = call(
        ffn_grads_kernel,
        "ffn_grads",
        (shape(PLANES, half, ffn_lanes, dtype=f32), shape(PLANES, half, ffn_lanes)),
        low_two,
        hidden_low,
        grad_expanded,
        *gys,
        scratch=(pltpu.VMEM((width, 2 * units), f32), pltpu.VMEM((CORES, units, lanes), f32)),
    )
    got_ffn = swap_core(away)
    near, far = call(
        ffn_split_kernel,
        "ffn_split",
        (shape(2, half, ffn_lanes, dtype=f32), shape(2, half, ffn_lanes)),
        keep_ffn,
        got_ffn,
    )
    got_far = swap_shard(far, 2)
    dh, dh_low = call(
        dh_kernel, "dh", (shape(length, width, dtype=f32), shape(length, width)), own, *received, gys[0], hidden, gains, after=(far,)
    )
    dhs = over_chips(dh_low)
    partial_mixed = call(
        mixed_kernel,
        "mixed",
        (shape(length, width, dtype=f32),) + (shape(length, width),) * 3,
        hidden_low,
        wb,
        after=(dh_low,),
    )
    got_mixed = [swap_seq(o, CORES * (j + 1)) for j, o in enumerate(partial_mixed[1:])]

    backs = call(
        functools.partial(attend_back_kernel, edges),
        "attend_back",
        (
            shape(CHIPS, length, local, dtype=f32),
            shape(CHIPS, length, 2 * local, dtype=f32),
            shape(CHIPS, length, 2 * local),
        )
        + ((shape(HALF, 2 * local),) if edges else ()),
        query,
        kv,
        kv_other,
        probs,
        *dhs,
        wo,
        *rim,
        after=(far,),
    )
    dq, dkv, back = backs[:3]
    back = swap_core(back)
    if edges:
        rim = (beyond(backs[3]),)

    def over_groups(total, kept_type):
        step = MEMBERS
        while step < seq_count:
            total = total + swap_seq(total.astype(bf16), step).astype(f32)
            step *= 2
        return total.astype(kept_type)

    def summed(own, parts, name, after=()):
        out = call(
            sum_kernel, name, shape(*own.shape, dtype=f32 if edges else bf16), own, *parts, after=after
        )
        return over_groups(out, bf16)

    mixed = call(
        mixed_sum_kernel, "mixed_sum", shape(1, length, width), partial_mixed[0], *got_mixed, hidden, after=(away,)
    )

    keep, away, dqkv = call(
        functools.partial(qkv_grads_kernel, edges),
        "qkv_grads",
        (
            shape(PLANES, half, qkv_lanes, dtype=f32),
            shape(PLANES, half, qkv_lanes),
            shape(many, 3 * local),
        ),
        dq,
        dkv,
        back,
        cosine,
        sine,
        low_one,
        *attns,
        *dhs,
        *rim,
        scratch=(pltpu.VMEM((width, qkv_lanes), f32), pltpu.VMEM((many, local), bf16)),
    )
    got = swap_core(away)
    own_ffn, sent_near = call(
        ffn_near_kernel,
        "ffn_near",
        (shape(half, ffn_lanes, dtype=f32), shape(half, ffn_lanes)),
        near,
        got_far,
        after=(away,),
    )
    total = call(
        ffn_total_kernel,
        "ffn_total",
        shape(half, ffn_lanes, dtype=f32 if edges else bf16),
        own_ffn,
        swap_shard(sent_near, 1),
        after=(got,),
    )
    total = over_groups(total, bf16)
    last_own, o1, o2, o3, gain_sums = call(
        da_kernel,
        "da",
        (shape(length, width, dtype=f32),)
        + (shape(length, width),) * 3
        + (shape(PLANES, EXTRA, qkv_lanes, dtype=f32),),
        dqkv,
        wq,
        *xs,
        gain_two,
        after=(mixed,),
    )
    sent = call(
        to_planes_gains_kernel,
        "qkv_to_planes",
        (shape(kept, qkv_lanes, dtype=f32),)
        + (shape(kept, qkv_lanes),) * 3,
        keep,
        got,
        gain_sums,
    )
    got = [swap_shard(s, i + 1) for i, s in enumerate(sent[1:4])]
    packet = shape(length + half + 32, width)
    packets = call(last_packet_kernel, "last_packet", (packet,) * 2, total, o1, o2, after=(sent[1],))
    packets += call(last_packet_kernel, "third_packet", (packet,), total, o3, after=(got[0],))
    received = [swap_seq(o, CORES * (j + 1)) for j, o in enumerate(packets)]

    mine = call(
        ffn_gather_kernel,
        "ffn_gather",
        shape(CHIPS, half, ffn_lanes),
        total,
        *received,
    )
    owned_in, owned_back = call(
        ffn_owned_kernel,
        "ffn_owned",
        (shape(*w_in.shape, dtype=f32), shape(*w_back.shape, dtype=f32)),
        mine,
        swap_core(mine),
    )
    grad_tokens = call(
        last_kernel,
        "last",
        shape(1, length, width),
        last_own,
        *received,
        xs[0],
        dh,
        gains,
        after=(sent[1],),
    )
    mine = call(
        functools.partial(place_kernel, 0),
        "qkv_gather",
        shape(CHIPS, kept, qkv_lanes),
        *over_chips(summed(sent[0], got, "qkv_sum")),
        after=(grad_tokens, owned_back),
    )
    owned_qkv, owned_out, grad_gain_one, grad_gain_two = call(
        qkv_owned_kernel,
        "qkv_owned",
        (
            shape(*w_qkv.shape, dtype=f32),
            shape(*w_out.shape, dtype=f32),
            shape(local, dtype=f32),
            shape(local, dtype=f32),
        ),
        mine,
        swap_core(mine),
    )
    return (mixed, grad_tokens, grad_gain_one, owned_qkv, owned_out, grad_gain_two, owned_in, owned_back)


def solution(mesh):
    return jax.shard_map(
        shards,
        mesh=mesh,
        in_specs=(
            P("shard", "seq", None),
            P("shard"),
            P("shard", None),
            P("shard", None),
            P("shard"),
            P("shard", None),
            P("shard", None),
            P("shard", None),
            P("shard", "seq", None),
        ),
        out_specs=(
            P("shard", "seq", None),
            P("shard", "seq", None),
            P("shard"),
            P("shard", None),
            P("shard", None),
            P("shard"),
            P("shard", None),
            P("shard", None),
        ),
        check_vma=False,
    )
```

```python
import functools
import math

import jax
import jax.numpy as jnp
from jax import lax
from jax.experimental import pallas as pl
from jax.experimental.pallas import tpu as pltpu
from jax.sharding import PartitionSpec as P

HEADS = 12
HEAD_DIM = 64
FF = 1152
HALF = 64
CHIPS = 4
CORES = 2
MEMBERS = CHIPS * CORES
PLANES = 4
EXTRA = 8
f32 = jnp.float32
bf16 = jnp.bfloat16
SCALE = HEAD_DIM ** (-0.5)
ROOM = 6 * 1024 * 1024


TIMES = {
    "qkv_piece": 0.5,
    "ffn_piece": 1,
    "qkv_place": 0.8,
    "qkv": 3.2,
    "attend": 2.3,
    "ffn_place": 1.2,
    "ffn": 4.5,
    "ffn_grads": 1.6,
    "dh": 0.4,
    "mixed": 0.6,
    "ffn_split": 1,
    "mixed_sum": 0.4,
    "attend_back": 6.9,
    "qkv_grads": 2.4,
    "da": 1.5,
    "qkv_to_planes": 0.8,
    "qkv_gather": 0.6,
    "last_packet": 0.5,
    "ffn_total": 0.4,
    "ffn_gather": 0.5,
    "qkv_sum": 0.4,
    "last": 0.6,
    "ffn_owned": 2.2,
    "qkv_owned": 1.7,
}


def dot(left, right):
    return lax.dot_general(left, right, (((1,), (0,)), ((), ())), preferred_element_type=f32)


def dot_t(left, right):
    return lax.dot_general(left, right, (((1,), (1,)), ((), ())), preferred_element_type=f32)


def t_dot(left, right):
    return lax.dot_general(left, right, (((0,), (0,)), ((), ())), preferred_element_type=f32)


def swap_seq(value, bits):
    count = lax.axis_size("seq")
    return lax.ppermute(value, "seq", [(i, i ^ bits) for i in range(count)])


def swap_shard(value, bits):
    count = lax.axis_size("shard")
    return lax.ppermute(value, "shard", [(i, i ^ bits) for i in range(count)])


def swap_core(value):
    return swap_seq(value, 1)


def over_chips(value):
    return [value] + [swap_seq(value, CORES * j) for j in range(CHIPS - 1, 0, -1)][::-1]


def over_planes(value):
    return [value] + [swap_shard(value, i) for i in range(1, PLANES)]


def shape(*dims, dtype=bf16):
    return jax.ShapeDtypeStruct(dims, dtype)


def places():
    me = lax.axis_index("seq")
    return (me % MEMBERS) // CORES, me % CORES, lax.axis_index("shard")


def size_of(value):
    return math.prod(value.shape) * jnp.dtype(value.dtype).itemsize


def call(kernel, name, outs, *operands, after=(), scratch=(), held=0):
    taken = len(operands)
    specs = [pl.BlockSpec(memory_space=pltpu.HBM)] * held
    specs += [pl.BlockSpec(memory_space=pltpu.VMEM)] * (taken - held)
    specs += [pl.BlockSpec(memory_space=pl.ANY)] * len(after)
    us = TIMES.get(name, 0.5)
    held_size = sum(size_of(o) for o in operands[held:])
    held_size += sum(size_of(o) for o in jax.tree.leaves(outs))

    def body(*refs):
        kernel(places(), *refs[:taken], *refs[taken + len(after) :])

    return pl.pallas_call(
        body,
        out_shape=outs,
        in_specs=specs,
        out_specs=jax.tree.map(lambda _: pl.BlockSpec(memory_space=pltpu.VMEM), outs),
        scratch_shapes=list(scratch),
        cost_estimate=pl.CostEstimate(
            flops=int(us * 2e10), bytes_accessed=int(us * 10), transcendentals=0
        ),
        compiler_params=pltpu.CompilerParams(vmem_limit_bytes=2 * held_size + ROOM),
        name=name,
    )(*operands, *after)


def norm_parts(values):
    center = values - jnp.mean(values, axis=-1, keepdims=True)
    factor = lax.rsqrt(jnp.mean(center * center, axis=-1, keepdims=True) + 1e-05)
    return center * factor, factor


def norm_inward(upward, gain, normed, factor):
    scaled = upward * gain
    return factor * (
        scaled
        - jnp.mean(scaled, axis=-1, keepdims=True)
        - normed * jnp.mean(scaled * normed, axis=-1, keepdims=True)
    )


def first_half(shape_of):
    return lax.broadcasted_iota(jnp.int32, shape_of, 1) % HEAD_DIM < HEAD_DIM // 2


def shifted(values):
    return pltpu.roll(values, 96, 1), pltpu.roll(values, 32, 1)


def rows_at(start, size):
    return pl.ds(pl.multiple_of(start, 16), size)


def lanes_at(start, size):
    return pl.ds(pl.multiple_of(start, 128), size)


def extra_rows(first, second, lanes):
    row = lax.broadcasted_iota(jnp.int32, (EXTRA, lanes), 0)
    pad = jnp.zeros((1, lanes - first.shape[1]), f32)
    first = jnp.concatenate([first, pad], axis=1)
    second = jnp.concatenate([second, pad], axis=1)
    return jnp.where(row == 0, first, jnp.where(row == 1, second, 0.0))


def copied(pairs, sems):
    copies = [pltpu.make_async_copy(src, dst, sems.at[i]) for i, (src, dst) in enumerate(pairs)]
    for copy in copies:
        copy.start()
    for copy in copies:
        copy.wait()


def qkv_piece_kernel(where, w_qkv, part, gains, out, rows, sems):
    chip, core = where[0], where[1]
    half = w_qkv.shape[0] // CORES
    width = w_qkv.shape[1] // 3
    local = width // CHIPS
    size, lanes = part.shape
    copied(((w_qkv.at[rows_at(core * half, half), :], rows),), sems)
    for b in range(CHIPS):

        @pl.when(chip == b)
        def _():
            for p in range(3):
                at = p * width + b * local
                out[:half, p * local : (p + 1) * local] = rows[:, at : at + local]

    both = gains[...].astype(f32)[None]
    share = both.shape[1] // 2
    out[half:, :] = extra_rows(both[:, :share], both[:, share:], out.shape[1]).astype(bf16)
    out[:size, 3 * local :] = part[:, :local]
    out[size:half, 3 * local :] = part[:, local:]


def ffn_piece_kernel(where, w_in, w_back, out, rows, back, sems):
    chip, core = where[0], where[1]
    half = w_in.shape[0] // CORES
    units = FF // PLANES // CHIPS
    lanes = back.shape[1]
    copied(
        (
            (w_in.at[rows_at(core * half, half), :], rows),
            (w_back.at[:, lanes_at(core * lanes, lanes)], back),
        ),
        sems,
    )
    spare = half - units
    side = units * lanes // half
    rest = lanes - side
    at_back = 2 * PLANES * units
    for b in range(CHIPS):

        @pl.when(chip == b)
        def _():
            for p in range(2):
                for z in range(PLANES):
                    at = p * FF + z * units * CHIPS + b * units
                    to = (p * PLANES + z) * units
                    out[:, to : to + units] = rows[:, at : at + units]
            own = back[b * units : (b + 1) * units, :]
            out[:units, at_back:] = own[:, :side]
            for i in range(units // spare):
                to = at_back + i * rest
                out[units:, to : to + rest] = own[i * spare : (i + 1) * spare, side:]


def unpacked(block, units):
    spare = block.shape[0] - units
    rest = block.shape[1] // (units // spare)
    last = [block[units:, i * rest : (i + 1) * rest] for i in range(units // spare)]
    return jnp.concatenate([block[:units], jnp.concatenate(last, axis=0)], axis=1)


def place_kernel(slot, where, p0, p1, p2, p3, out):
    for i, ref in enumerate((p0, p1, p2, p3)):
        out[where[slot] ^ i] = ref[...]


def qkv_place_kernel(where, p0, p1, p2, p3, out, packet):
    lanes = out.shape[2]
    size = packet.shape[1]
    for i, ref in enumerate((p0, p1, p2, p3)):
        z = where[2] ^ i
        out[z] = ref[:, :lanes]
        packet[z] = jnp.concatenate([ref[:size, lanes:], ref[size : 2 * size, lanes:]], axis=1)


def up_pair_kernel(where, own, both, out):
    out[0] = own[...]
    out[1] = both[own.shape[0] :, :]


def last_packet_kernel(where, total, *refs):
    half, lanes = total.shape
    rows, width = refs[0].shape
    spare = lanes - width
    for ref, out in zip(refs[: len(refs) // 2], refs[len(refs) // 2 :]):
        out[:rows, :] = ref[...]
        out[rows : rows + half, :] = total[:, :width]
        for i in range(half // 32):
            at = slice(i * spare, (i + 1) * spare)
            out[rows + half :, at] = total[i * 32 : (i + 1) * 32, width:]
        blank = width - half // 32 * spare
        out[rows + half :, width - blank :] = jnp.zeros((32, blank), bf16)


def ffn_gather_kernel(where, total, r1, r2, r3, out):
    half, lanes = total.shape
    width = r1.shape[1]
    spare = lanes - width
    rows = r1.shape[0] - half - 32
    out[where[0]] = total[...]
    for j, ref in enumerate((r1, r2, r3)):
        at = where[0] ^ (j + 1)
        out[at, :, :width] = ref[rows : rows + half, :]
        for i in range(half // 32):
            piece = ref[rows + half :, i * spare : (i + 1) * spare]
            out[at, i * 32 : (i + 1) * 32, width:] = piece


def pair_kernel(where, first, second, out):
    out[0] = first[...]
    out[1] = second[...]


def ffn_place_kernel(where, near, far, p01, p23, out):
    half = near.shape[1]
    p0, p1, p2, p3 = p01.at[0], p01.at[1], p23.at[0], p23.at[1]
    size, lanes = p0.shape[1:]
    for i, ref in enumerate((near.at[0], near.at[1], far.at[0], far.at[1])):
        z = where[2] ^ i
        out[z, :, 2 * lanes :] = ref[...]
    for i, ref in enumerate((p0, p1, p2, p3)):
        b = where[0] ^ i
        at = rows_at((b % 2) * size, size)

        for half_at in range(2):

            @pl.when(b // 2 == half_at)
            def _():
                for z in range(PLANES):
                    out[z, at, half_at * lanes : (half_at + 1) * lanes] = ref[z]


def qkv_kernel(where, x0, x1, x2, x3, mine, other, cos, sin, a_out, q_out, kv_out, w_out, g_out):
    rows = x0.shape[0]
    half = mine.shape[1] - EXTRA
    local = mine.shape[2] // 3
    share = CORES * half
    core = where[1]
    for z in range(PLANES):
        w_out[rows_at(z * share + core * half, half), :] = mine[z, :half, :]
        w_out[rows_at(z * share + (1 - core) * half, half), :] = other[z, :half, :]
        tail = mine[z, half:, :share].astype(f32)
        g_out[:, z * share : (z + 1) * share] = tail[:8]
    gain = g_out[0:1, :]
    for j, ref in enumerate((x0, x1, x2, x3)):
        normed, _ = norm_parts(ref[:rows, :].astype(f32))
        a_out[j * rows : (j + 1) * rows, :] = (normed * gain).astype(bf16)
    out = dot(a_out[...], w_out[...])
    front = first_half((CHIPS * rows, 128))
    parts = []
    for at in range(0, 2 * local, 128):
        u = out[:, at : at + 128]
        up, down = shifted(u)
        parts.append((u * cos[...] + jnp.where(front, -up, down) * sin[...]).astype(bf16))
    qk = jnp.concatenate(parts, axis=1)
    value = out[:, 2 * local :].astype(bf16)
    for j in range(CHIPS):
        at = slice(j * rows, (j + 1) * rows)
        q_out[j] = qk[at, :local]
        kv_out[j, :, :local] = qk[at, local:]
        kv_out[j, :, local:] = value[at]


def block_of(pairs, j, local):
    return pairs[j // 2, :, j % 2 * local : (j % 2 + 1) * local]


def extended(where, j, kv, other, rim):
    chip, core = where[0], where[1]
    length = kv.shape[1]
    b = chip ^ j
    below = jnp.where(core == 0, jnp.maximum(b - 1, 0), b) ^ chip
    above = jnp.where(core == 0, b, jnp.minimum(b + 1, CHIPS - 1)) ^ chip
    before = other[below, length - HALF :, :]
    after = other[above, :HALF, :]
    if rim is not None:
        before = jnp.where((core == 0) & (b == 0), rim[...], before)
        after = jnp.where((core == 1) & (b == CHIPS - 1), rim[...], after)
    return jnp.concatenate([before, kv[j], after], axis=0)


def probs_of(q, k, bias):
    logits = dot_t(q, k) * SCALE + bias
    highest = jnp.max(logits, axis=-1, keepdims=True)
    exponent = jnp.exp(logits - highest)
    return exponent / jnp.sum(exponent, axis=-1, keepdims=True)


def attend_kernel(edges, where, q, kv, other, bias, *rest):
    rim, out, kept = rest if edges else (None, *rest)
    local = q.shape[-1]
    extent = bias.shape[-1]
    for j in range(CHIPS):
        ext = extended(where, j, kv, other, rim)
        parts = []
        for h in range(local // HEAD_DIM):
            lanes = slice(h * HEAD_DIM, (h + 1) * HEAD_DIM)
            prob = probs_of(q[j, :, lanes], ext[:, lanes], bias[j]).astype(bf16)
            kept[j, :, h * extent : (h + 1) * extent] = prob
            parts.append(dot(prob, ext[:, local + h * HEAD_DIM : local + (h + 1) * HEAD_DIM]))
        out[j // 2, :, j % 2 * local : (j % 2 + 1) * local] = jnp.concatenate(parts, axis=1).astype(bf16)


def ffn_kernel(
    where, t0, t1, t2, t3, x0, x1, x2, x3, y02, y13, mine, other, gains,
    own_out, d1_out, d2_out, d3_out, hid_out, a_out, m_out, dgu_out, gain_out, wb_out, wc_out,
    wi, wo,
):
    chip, core = where[0], where[1]
    rows = x0.shape[0]
    width = x0.shape[1]
    half = mine.shape[1]
    share = CORES * half
    units = FF // CHIPS
    part = units // PLANES
    lanes = width // CORES
    local = width // CHIPS
    for z in range(PLANES):
        for k, ref in ((core, mine), (1 - core, other)):
            wi[rows_at(z * share + k * half, half), :] = ref[z, :, width : width + 2 * units]
            for p in range(CORES):
                at = slice(z * share + p * half, z * share + (p + 1) * half)
                wo[at, lanes_at(k * lanes, lanes)] = ref[z, :, p * lanes : (p + 1) * lanes]
    own_back, other_back = [
        jnp.concatenate(
            [unpacked(ref[z, :, width + 2 * units :], part) for z in range(PLANES)], axis=0
        )
        for ref in (mine, other)
    ]
    wb_out[:, :lanes] = jnp.where(core == 0, own_back, other_back)
    wb_out[:, lanes:] = jnp.where(core == 0, other_back, own_back)
    wc_out[...] = wo[rows_at(chip * local, local), :]
    xs = (x0, x1, x2, x3)
    gain = gains[1:2, :]
    outward = [
        (ref, wo[rows_at((chip ^ i) * local, local), :]) for i, ref in enumerate((t0, t1, t2, t3))
    ]
    normed = []
    for j in range(CHIPS):
        hidden = xs[j][:rows, :].astype(f32)
        for i, (ref, weight) in enumerate(outward):
            hidden = hidden + dot(block_of(ref, j ^ i, local), weight)
        if j == 0:
            hid_out[...] = hidden
        norm, _ = norm_parts(hidden)
        normed.append(norm)
        a_out[j * rows : (j + 1) * rows, :] = (norm * gain).astype(bf16)
    total = jnp.zeros((1, width), f32)
    for j in range(CHIPS):
        at = slice(j * rows, (j + 1) * rows)
        gu = dot(a_out[at, :], wi[...])
        entering, gating = gu[:, :units], gu[:, units:]
        rise = 0.5 * (1.0 + lax.erf(entering * (0.5**0.5)))
        slope = rise + entering * jnp.exp(-0.5 * entering * entering) * 0.3989422804014327
        act = entering * rise
        m_out[at, :] = (act * gating).astype(bf16)
        dm = dot_t((y02, y13)[j % 2][j // 2], wb_out[...])
        dgu = jnp.concatenate([dm * gating * slope, dm * act], axis=1).astype(bf16)
        dgu_out[at, :] = dgu
        da = dot_t(dgu, wi[...])
        total = total + jnp.sum(da * normed[j], axis=0, keepdims=True)
        if j == 0:
            own_out[...] = da
        else:
            (d1_out, d2_out, d3_out)[j - 1][...] = da.astype(bf16)
    gain_out[...] = jnp.broadcast_to(total, gain_out.shape)


def mixed_kernel(where, m, wb, own, m1, m2, m3):
    rows = own.shape[0]
    own[...] = dot(m[:rows, :], wb[...])
    for j, ref in enumerate((m1, m2, m3)):
        ref[...] = dot(m[(j + 1) * rows : (j + 2) * rows, :], wb[...]).astype(bf16)


def mixed_sum_kernel(where, own, r1, r2, r3, hidden, out):
    total = own[...] + r1[...].astype(f32) + r2[...].astype(f32) + r3[...].astype(f32)
    out[0] = (hidden[...] + total).astype(bf16)


def ffn_grads_kernel(where, a, m, dgu, y02, y13, keep, away, gin, gb):
    core = where[1]
    half = keep.shape[1]
    share = CORES * half
    units = m.shape[1]
    part = units // PLANES
    lanes = y02.shape[2] // CORES
    gin[...] = t_dot(a[...], dgu[...])
    upward = jnp.concatenate([y02[0], y13[0], y02[1], y13[1]], axis=0)
    back = t_dot(m[...], upward)
    first, second = back[:, :lanes], back[:, lanes:]
    gb[0] = jnp.where(core == 0, first, second)
    gb[1] = jnp.where(core == 0, second, first)
    for z in range(PLANES):
        at = slice(z * part, (z + 1) * part)
        blank = jnp.zeros((half - part, lanes), f32)
        keep[z, :, : 2 * units] = gin[rows_at(z * share + core * half, half), :]
        keep[z, :, 2 * units :] = jnp.concatenate([gb[0, at, :], blank], axis=0)
        away[z, :, : 2 * units] = gin[rows_at(z * share + (1 - core) * half, half), :].astype(bf16)
        away[z, :, 2 * units :] = jnp.concatenate([gb[1, at, :], blank], axis=0).astype(bf16)


def dh_kernel(where, own, r1, r2, r3, y02, hidden, gains, dh_out, low_out):
    total = own[...] + r1[...].astype(f32) + r2[...].astype(f32) + r3[...].astype(f32)
    normed, factor = norm_parts(hidden[...])
    dh = y02[0].astype(f32) + norm_inward(total, gains[1:2, :], normed, factor)
    dh_out[...] = dh
    low_out[...] = dh.astype(bf16)


def attend_back_kernel(edges, where, q, kv, other, probs, h0, h1, h2, h3, w_out, *rest):
    rim, rest = (rest[0], rest[1:]) if edges else (None, rest)
    dq_out, dkv_out, back_out = rest[:3]
    chip, core = where[0], where[1]
    local = q.shape[-1]
    length = q.shape[1]
    extent = length + 2 * HALF
    back_out[...] = jnp.zeros_like(back_out)
    for j, dh in enumerate((h0, h1, h2, h3)):
        dctx = dot_t(dh[...], w_out[...]).astype(bf16)
        ext = extended(where, j, kv, other, rim)
        dqs, dks, dvs = [], [], []
        for h in range(local // HEAD_DIM):
            lanes = slice(h * HEAD_DIM, (h + 1) * HEAD_DIM)
            qh = q[j, :, lanes]
            kh = ext[:, lanes]
            vh = ext[:, local + h * HEAD_DIM : local + (h + 1) * HEAD_DIM]
            dch = dctx[:, lanes]
            low = probs[j, :, h * extent : (h + 1) * extent]
            prob = low.astype(f32)
            dprob = dot_t(dch, vh)
            inner = jnp.sum(prob * dprob, axis=-1, keepdims=True)
            dscore = (prob * (dprob - inner) * SCALE).astype(bf16)
            dqs.append(dot(dscore, kh))
            dks.append(t_dot(dscore, qh))
            dvs.append(t_dot(low, dch))
        dq_out[j] = jnp.concatenate(dqs, axis=1)
        grads = jnp.concatenate(dks + dvs, axis=1)
        dkv_out[j] = grads[HALF : HALF + length]
        before = grads[:HALF].astype(bf16)
        after = grads[HALF + length :].astype(bf16)
        b = chip ^ j
        below = jnp.where(core == 0, b - 1, b)
        above = jnp.where(core == 0, b, b + 1)

        @pl.when(below >= 0)
        def _():
            back_out[jnp.maximum(below, 0) ^ chip, length - HALF :, :] = before

        @pl.when(above < CHIPS)
        def _():
            back_out[jnp.minimum(above, CHIPS - 1) ^ chip, :HALF, :] = after

        if edges:
            rim_out = rest[3]

            @pl.when(below < 0)
            def _():
                rim_out[...] = before

            @pl.when(above >= CHIPS)
            def _():
                rim_out[...] = after


def qkv_grads_kernel(edges, where, dq, dkv, back, cos, sin, a, t0, t1, t2, t3, h0, h1, h2, h3, *rest):
    rim, rest = (rest[0], rest[1:]) if edges else (None, rest)
    keep, away, d_out, acc, cols = rest
    chip, core = where[0], where[1]
    length = dq.shape[1]
    local = dq.shape[2]
    width = a.shape[1]
    front = first_half((length, 128))
    for j in range(CHIPS):
        at = slice(j * length, (j + 1) * length)
        gkv = dkv[j] + back[j].astype(f32)
        if edges:
            b = chip ^ j
            blank = jnp.zeros((length - HALF, 2 * local), f32)
            value = rim[...].astype(f32)
            gkv = gkv + jnp.where(
                (core == 0) & (b == 0), jnp.concatenate([value, blank], axis=0), 0.0
    )
            gkv = gkv + jnp.where(
                (core == 1) & (b == CHIPS - 1), jnp.concatenate([blank, value], axis=0), 0.0
    )
        g = jnp.concatenate([dq[j], gkv[:, :local]], axis=1)
        for lane in range(0, 2 * local, 128):
            u = g[:, lane : lane + 128]
            up, down = shifted(u * sin[at, :])
            d_out[at, lane : lane + 128] = (
                u * cos[at, :] + jnp.where(front, up, -down)
            ).astype(bf16)
        d_out[at, 2 * local :] = gkv[:, local:].astype(bf16)
    acc[:, : 3 * local] = t_dot(a[...], d_out[...])
    for b in range(CHIPS):

        @pl.when(chip == b)
        def _():
            for j, ref in enumerate((h0, h1, h2, h3)):
                cols[j * length : (j + 1) * length, :] = ref[:, b * local : (b + 1) * local]

    for i, ref in enumerate((t0, t1, t2, t3)):
        rows = jnp.concatenate([block_of(ref, j ^ i, local) for j in range(CHIPS)], axis=0)
        acc[rows_at((chip ^ i) * local, local), 3 * local :] = t_dot(rows, cols[...])
    half = keep.shape[1]
    share = CORES * half
    for z in range(PLANES):
        keep[z] = acc[rows_at(z * share + core * half, half), :]
        away[z] = acc[rows_at(z * share + (1 - core) * half, half), :].astype(bf16)


def da_kernel(where, d, w, x0, x1, x2, x3, gain_two, own_out, o1, o2, o3, gain_out):
    rows = x0.shape[0]
    total = jnp.zeros((1, w.shape[0]), f32)
    for j, ref in enumerate((x0, x1, x2, x3)):
        da = dot_t(d[j * rows : (j + 1) * rows, :], w[...])
        normed, _ = norm_parts(ref[:rows, :].astype(f32))
        total = total + jnp.sum(da * normed, axis=0, keepdims=True)
        if j == 0:
            own_out[...] = da
        else:
            (o1, o2, o3)[j - 1][...] = da.astype(bf16)
    share = w.shape[0] // PLANES
    for z in range(PLANES):
        at = slice(z * share, (z + 1) * share)
        gain_out[z] = extra_rows(total[:, at], gain_two[0:1, at], gain_out.shape[2])


def copy_kernel(where, value, out):
    out[...] = value[...]


def ffn_split_kernel(where, keep, got, near, far):
    for i in range(PLANES):
        at = where[2] ^ i
        total = keep[at] + got[at].astype(f32)
        if i % 2 == 0:
            near[i // 2] = total
        else:
            far[i // 2] = total.astype(bf16)


def ffn_near_kernel(where, near, got, own, sent):
    own[...] = near[0] + got[0].astype(f32)
    sent[...] = (near[1] + got[1].astype(f32)).astype(bf16)


def ffn_total_kernel(where, own, got, out):
    out[...] = (own[...] + got[...].astype(f32)).astype(out.dtype)


def to_near_plane_kernel(where, keep, got, gains, out):
    half = keep.shape[1]
    at = where[2] ^ 1
    out[:half, :] = (keep[at] + got[at].astype(f32)).astype(bf16)
    out[half:, :] = gains[at].astype(bf16)


def to_planes_gains_kernel(where, keep, got, gains, own, o2, o3):
    plane = where[2]
    half = keep.shape[1]
    own[:half, :] = keep[plane] + got[plane].astype(f32)
    own[half:, :] = gains[plane]
    for i, ref in enumerate((o2, o3)):
        at = plane ^ (i + 2)
        ref[:half, :] = (keep[at] + got[at].astype(f32)).astype(bf16)
        ref[half:, :] = gains[at].astype(bf16)


def sum_kernel(where, own, r1, r2, r3, out):
    total = own[...] + r1[...].astype(f32) + r2[...].astype(f32) + r3[...].astype(f32)
    out[...] = total.astype(out.dtype)


def last_kernel(where, own, r1, r2, r3, x0, dh, gains, grad_out):
    total = own[...]
    for ref in (r1, r2, r3):
        total = total + ref[: own.shape[0], :].astype(f32)
    normed, factor = norm_parts(x0[...].astype(f32))
    grad = dh[...] + norm_inward(total, gains[0:1, :], normed, factor)
    grad_out[0] = grad.astype(bf16)


def ffn_owned_kernel(where, mine, other, in_out, back_out):
    core = where[1]
    half = mine.shape[1]
    units = FF // CHIPS
    part = units // PLANES
    lanes = mine.shape[2] - 2 * units
    for k, ref in ((core, mine), (1 - core, other)):
        rows = rows_at(k * half, half)
        for p in range(2):
            for z in range(PLANES):
                at = (p * PLANES + z) * part
                for b in range(CHIPS):
                    to = p * FF + (z * CHIPS + b) * part
                    in_out[rows, to : to + part] = ref[b, :, at : at + part].astype(f32)
    for b in range(CHIPS):
        own = mine[b, :part, 2 * units :].astype(f32)
        got = other[b, :part, 2 * units :].astype(f32)
        back_out[b * part : (b + 1) * part, :lanes] = jnp.where(core == 0, own, got)
        back_out[b * part : (b + 1) * part, lanes:] = jnp.where(core == 0, got, own)


def qkv_owned_kernel(where, mine, other, qkv_out, w_out, one_out, two_out):
    core = where[1]
    half = mine.shape[1] - EXTRA
    local = w_out.shape[1] // CHIPS
    total = jnp.zeros((EXTRA, local), f32)
    for k, ref in ((core, mine), (1 - core, other)):
        rows = rows_at(k * half, half)
        for b in range(CHIPS):
            for p in range(3):
                to = (p * CHIPS + b) * local
                qkv_out[rows, to : to + local] = ref[b, :half, p * local : (p + 1) * local].astype(f32)
            w_out[rows, b * local : (b + 1) * local] = ref[b, :half, 3 * local :].astype(f32)
            total = total + ref[b, half:, :local].astype(f32)
    one_out[...] = total[0]
    two_out[...] = total[1]


def shards(tokens, norm_gain, w_qkv, w_out, ffn_gain, w_in, w_back, seq_ids, cotangent):
    length, width = tokens.shape[1:]
    me = lax.axis_index("seq")
    seq_count = lax.axis_size("seq")
    edges = seq_count > MEMBERS
    group = me // MEMBERS
    chip = (me % MEMBERS) // CORES
    core = me % CORES
    local = width // CHIPS
    units = FF // CHIPS
    many = CHIPS * length
    half = width // PLANES // CORES
    lanes = width // CORES
    extent = length + 2 * HALF
    kept = half + EXTRA
    in_sent = 2 * units + units // PLANES * lanes // half
    in_lanes = width + in_sent
    ffn_lanes = 2 * units + lanes
    qkv_lanes = 4 * local

    out_rows = w_out.shape[0] // CHIPS
    piece = call(
        qkv_piece_kernel,
        "qkv_piece",
        shape(kept, 4 * local),
        w_qkv,
        lax.dynamic_slice(w_out, (chip * out_rows, core * lanes), (out_rows, lanes)),
        jnp.concatenate([norm_gain, ffn_gain]),
        held=1,
        scratch=(pltpu.VMEM((half, 3 * width), bf16), pltpu.SemaphoreType.DMA((1,))),
    )
    pieces = over_planes(piece)
    both = jnp.concatenate([tokens[0], cotangent[0]], axis=0)
    both_near = swap_seq(both, 2 * CORES)
    xs = [tokens[0], swap_seq(tokens[0], CORES), both_near, swap_seq(tokens[0], 3 * CORES)]
    mine, out_own = call(
        qkv_place_kernel,
        "qkv_place",
        (
            shape(PLANES, kept, 3 * local),
            shape(PLANES, out_rows, lanes),
        ),
        *pieces,
    )
    piece = call(
        ffn_piece_kernel,
        "ffn_piece",
        shape(half, in_sent),
        w_in,
        w_back,
        held=2,
        scratch=(
            pltpu.VMEM((half, 2 * FF), bf16),
            pltpu.VMEM((w_back.shape[0], lanes), bf16),
            pltpu.SemaphoreType.DMA((2,)),
        ),
        after=(mine,),
    )
    in_near = swap_shard(piece, 1)
    out_near = swap_seq(out_own, CORES)
    other = swap_core(mine)

    block = (group * CHIPS + (chip ^ jnp.arange(CHIPS))) * CORES + core
    position = (block[:, None] * length + jnp.arange(length)[None]).astype(f32).reshape(many)
    frequency = 10000.0 ** (-jnp.arange(0, HEAD_DIM, 2).astype(f32) / HEAD_DIM)
    angles = position[:, None] * jnp.tile(frequency, 4)[None]
    cosine, sine = jnp.cos(angles), jnp.sin(angles)
    spans = length // HALF
    ids = jnp.pad(seq_ids[0], (1, 1), constant_values=-1)
    key_ids = jnp.stack(
        [lax.dynamic_slice_in_dim(ids, block[j] * spans, spans + 2, 0) for j in range(CHIPS)]
    )
    key_ids = jnp.repeat(key_ids, HALF, axis=1)
    query_ids = key_ids[:, HALF : HALF + length]
    offset = jnp.arange(extent)[None, :] - HALF - jnp.arange(length)[:, None]
    allowed = (jnp.abs(offset) <= HALF)[None] & (query_ids[:, :, None] == key_ids[:, None, :])
    bias = jnp.where(allowed, 0.0, -1e30).astype(f32)

    low_one, query, kv, wq, gains = call(
        qkv_kernel,
        "qkv",
        (
            shape(many, width),
            shape(CHIPS, length, local),
            shape(CHIPS, length, 2 * local),
            shape(width, 3 * local),
            shape(8, width, dtype=f32),
        ),
        *xs,
        mine,
        other,
        cosine,
        sine,
    )
    kv_other = swap_core(kv)

    def beyond(value):
        pairs = []
        for m in range(seq_count):
            to = m - MEMBERS + 1 if m % CORES == 0 else m + MEMBERS - 1
            if 0 <= to < seq_count:
                pairs.append((m, to))
        return lax.ppermute(value, "seq", pairs)

    rim = ()
    if edges:
        first = lax.dynamic_index_in_dim(kv, chip, 0, False)[:HALF]
        last = lax.dynamic_index_in_dim(kv, chip ^ (CHIPS - 1), 0, False)[length - HALF :]
        rim = (beyond(jnp.where(core == 0, first, last)),)

    up_pair = call(up_pair_kernel, "up_pair", shape(2, length, width), cotangent[0], both_near, after=(gains,))
    gys = (up_pair, swap_seq(up_pair, CORES))
    out_pair = call(pair_kernel, "out_pair", shape(2, *out_own.shape), out_own, out_near, after=(up_pair,))
    out_far = swap_seq(out_pair, 2 * CORES)
    in_pair = call(
        pair_kernel, "in_pair", shape(2, half, in_sent), piece, in_near, after=(out_pair,)
    )
    in_far = swap_shard(in_pair, 2)
    attn, probs = call(
        functools.partial(attend_kernel, edges),
        "attend",
        (shape(2, length, 2 * local), shape(CHIPS, length, local // HEAD_DIM * extent)),
        query,
        kv,
        kv_other,
        bias,
        *rim,
    )
    last_attn = call(copy_kernel, "attn_copy", shape(*attn.shape), attn, after=(gys[1],))
    attns = [attn, swap_seq(attn, CORES), swap_seq(attn, 2 * CORES), swap_seq(last_attn, 3 * CORES)]
    in_mine = call(
        ffn_place_kernel,
        "ffn_place",
        shape(PLANES, half, in_lanes),
        in_pair,
        in_far,
        out_pair,
        out_far,
        after=tuple(attns[1:]),
    )
    in_other = swap_core(in_mine)
    own, d1, d2, d3, hidden, low_two, hidden_low, grad_expanded, gain_two, wb, wo = call(
        ffn_kernel,
        "ffn",
        (shape(length, width, dtype=f32),)
        + (shape(length, width),) * 3
        + (
            shape(length, width, dtype=f32),
            shape(many, width),
            shape(many, units),
            shape(many, 2 * units),
            shape(8, width, dtype=f32),
            shape(units, width),
            shape(local, width),
        ),
        *attns,
        *xs,
        *gys,
        in_mine,
        in_other,
        gains,
        scratch=(pltpu.VMEM((width, 2 * units), bf16), pltpu.VMEM((width, width), bf16)),
    )
    received = [swap_seq(d, CORES * (j + 1)) for j, d in enumerate((d1, d2, d3))]
    keep_ffn, away = call(
        ffn_grads_kernel,
        "ffn_grads",
        (shape(PLANES, half, ffn_lanes, dtype=f32), shape(PLANES, half, ffn_lanes)),
        low_two,
        hidden_low,
        grad_expanded,
        *gys,
        scratch=(pltpu.VMEM((width, 2 * units), f32), pltpu.VMEM((CORES, units, lanes), f32)),
    )
    got_ffn = swap_core(away)
    near, far = call(
        ffn_split_kernel,
        "ffn_split",
        (shape(2, half, ffn_lanes, dtype=f32), shape(2, half, ffn_lanes)),
        keep_ffn,
        got_ffn,
    )
    got_far = swap_shard(far, 1)
    dh, dh_low = call(
        dh_kernel, "dh", (shape(length, width, dtype=f32), shape(length, width)), own, *received, gys[0], hidden, gains, after=(far,)
    )
    dhs = over_chips(dh_low)
    partial_mixed = call(
        mixed_kernel,
        "mixed",
        (shape(length, width, dtype=f32),) + (shape(length, width),) * 3,
        hidden_low,
        wb,
        after=(dh_low,),
    )
    got_mixed = [swap_seq(o, CORES * (j + 1)) for j, o in enumerate(partial_mixed[1:])]

    backs = call(
        functools.partial(attend_back_kernel, edges),
        "attend_back",
        (
            shape(CHIPS, length, local, dtype=f32),
            shape(CHIPS, length, 2 * local, dtype=f32),
            shape(CHIPS, length, 2 * local),
        )
        + ((shape(HALF, 2 * local),) if edges else ()),
        query,
        kv,
        kv_other,
        probs,
        *dhs,
        wo,
        *rim,
        after=(far,),
    )
    dq, dkv, back = backs[:3]
    back = swap_core(back)
    if edges:
        rim = (beyond(backs[3]),)

    def over_groups(total, kept_type):
        step = MEMBERS
        while step < seq_count:
            total = total + swap_seq(total.astype(bf16), step).astype(f32)
            step *= 2
        return total.astype(kept_type)

    def summed(own, parts, name, after=()):
        out = call(
            sum_kernel, name, shape(*own.shape, dtype=f32 if edges else bf16), own, *parts, after=after
        )
        return over_groups(out, bf16)

    mixed = call(
        mixed_sum_kernel, "mixed_sum", shape(1, length, width), partial_mixed[0], *got_mixed, hidden, after=(away,)
    )

    keep, away, dqkv = call(
        functools.partial(qkv_grads_kernel, edges),
        "qkv_grads",
        (
            shape(PLANES, half, qkv_lanes, dtype=f32),
            shape(PLANES, half, qkv_lanes),
            shape(many, 3 * local),
        ),
        dq,
        dkv,
        back,
        cosine,
        sine,
        low_one,
        *attns,
        *dhs,
        *rim,
        scratch=(pltpu.VMEM((width, qkv_lanes), f32), pltpu.VMEM((many, local), bf16)),
    )
    got = swap_core(away)
    own_ffn, sent_near = call(
        ffn_near_kernel,
        "ffn_near",
        (shape(half, ffn_lanes, dtype=f32), shape(half, ffn_lanes)),
        near,
        got_far,
        after=(dq,),
    )
    total = call(
        ffn_total_kernel,
        "ffn_total",
        shape(half, ffn_lanes, dtype=f32 if edges else bf16),
        own_ffn,
        swap_shard(sent_near, 2),
        after=(got,),
    )
    total = over_groups(total, bf16)
    last_own, o1, o2, o3, gain_sums = call(
        da_kernel,
        "da",
        (shape(length, width, dtype=f32),)
        + (shape(length, width),) * 3
        + (shape(PLANES, EXTRA, qkv_lanes, dtype=f32),),
        dqkv,
        wq,
        *xs,
        gain_two,
        after=(mixed,),
    )
    to_near = call(
        to_near_plane_kernel, "qkv_to_near", shape(kept, qkv_lanes), keep, got, gain_sums
    )
    from_near = swap_shard(to_near, 1)
    sent = call(
        to_planes_gains_kernel,
        "qkv_to_planes",
        (shape(kept, qkv_lanes, dtype=f32),)
        + (shape(kept, qkv_lanes),) * 2,
        keep,
        got,
        gain_sums,
        after=(to_near,),
    )
    got = [from_near] + [swap_shard(s, i + 2) for i, s in enumerate(sent[1:3])]
    packet = shape(length + half + 32, width)
    packets = call(last_packet_kernel, "last_packet", (packet,) * 2, total, o1, o2, after=(sent[1],))
    packets += call(last_packet_kernel, "third_packet", (packet,), total, o3, after=(got[0],))
    received = [swap_seq(o, CORES * (j + 1)) for j, o in enumerate(packets)]

    mine = call(
        ffn_gather_kernel,
        "ffn_gather",
        shape(CHIPS, half, ffn_lanes),
        total,
        *received,
    )
    owned_in, owned_back = call(
        ffn_owned_kernel,
        "ffn_owned",
        (shape(*w_in.shape, dtype=f32), shape(*w_back.shape, dtype=f32)),
        mine,
        swap_core(mine),
    )
    grad_tokens = call(
        last_kernel,
        "last",
        shape(1, length, width),
        last_own,
        *received,
        xs[0],
        dh,
        gains,
        after=(sent[1],),
    )
    mine = call(
        functools.partial(place_kernel, 0),
        "qkv_gather",
        shape(CHIPS, kept, qkv_lanes),
        *over_chips(summed(sent[0], got, "qkv_sum")),
        after=(grad_tokens, owned_back),
    )
    owned_qkv, owned_out, grad_gain_one, grad_gain_two = call(
        qkv_owned_kernel,
        "qkv_owned",
        (
            shape(*w_qkv.shape, dtype=f32),
            shape(*w_out.shape, dtype=f32),
            shape(local, dtype=f32),
            shape(local, dtype=f32),
        ),
        mine,
        swap_core(mine),
    )
    return (mixed, grad_tokens, grad_gain_one, owned_qkv, owned_out, grad_gain_two, owned_in, owned_back)


def solution(mesh):
    return jax.shard_map(
        shards,
        mesh=mesh,
        in_specs=(
            P("shard", "seq", None),
            P("shard"),
            P("shard", None),
            P("shard", None),
            P("shard"),
            P("shard", None),
            P("shard", None),
            P("shard", None),
            P("shard", "seq", None),
        ),
        out_specs=(
            P("shard", "seq", None),
            P("shard", "seq", None),
            P("shard"),
            P("shard", None),
            P("shard", None),
            P("shard"),
            P("shard", None),
            P("shard", None),
        ),
        check_vma=False,
    )
```

```python
import functools
import math

import jax
import jax.numpy as jnp
from jax import lax
from jax.experimental import pallas as pl
from jax.experimental.pallas import tpu as pltpu
from jax.sharding import PartitionSpec as P

HEADS = 12
HEAD_DIM = 64
FF = 1152
HALF = 64
CHIPS = 4
CORES = 2
MEMBERS = CHIPS * CORES
PLANES = 4
EXTRA = 8
f32 = jnp.float32
bf16 = jnp.bfloat16
SCALE = HEAD_DIM ** (-0.5)
ROOM = 6 * 1024 * 1024


TIMES = {
    "qkv_piece": 0.5,
    "ffn_piece": 1,
    "qkv_place": 0.8,
    "qkv": 0.096,
    "attend": 2.3,
    "ffn_place": 1.2,
    "ffn": 4.5,
    "ffn_grads": 1.6,
    "dh": 0.4,
    "mixed": 0.6,
    "ffn_split": 1,
    "mixed_sum": 0.4,
    "attend_back": 0.207,
    "qkv_grads": 0.0144,
    "da": 1.5,
    "qkv_to_planes": 0.8,
    "qkv_gather": 9,
    "last_packet": 0.5,
    "ffn_total": 0.4,
    "ffn_gather": 0.5,
    "qkv_sum": 0.4,
    "last": 0.6,
    "ffn_owned": 0.066,
    "qkv_owned": 1.7,
}


def dot(left, right):
    return lax.dot_general(left, right, (((1,), (0,)), ((), ())), preferred_element_type=f32)


def dot_t(left, right):
    return lax.dot_general(left, right, (((1,), (1,)), ((), ())), preferred_element_type=f32)


def t_dot(left, right):
    return lax.dot_general(left, right, (((0,), (0,)), ((), ())), preferred_element_type=f32)


def swap_seq(value, bits):
    count = lax.axis_size("seq")
    return lax.ppermute(value, "seq", [(i, i ^ bits) for i in range(count)])


def swap_shard(value, bits):
    count = lax.axis_size("shard")
    return lax.ppermute(value, "shard", [(i, i ^ bits) for i in range(count)])


def swap_core(value):
    return swap_seq(value, 1)


def over_chips(value):
    return [value] + [swap_seq(value, CORES * j) for j in range(CHIPS - 1, 0, -1)][::-1]


def over_planes(value):
    return [value] + [swap_shard(value, i) for i in range(1, PLANES)]


def shape(*dims, dtype=bf16):
    return jax.ShapeDtypeStruct(dims, dtype)


def places():
    me = lax.axis_index("seq")
    return (me % MEMBERS) // CORES, me % CORES, lax.axis_index("shard")


def size_of(value):
    return math.prod(value.shape) * jnp.dtype(value.dtype).itemsize


def call(kernel, name, outs, *operands, after=(), scratch=(), held=0):
    taken = len(operands)
    specs = [pl.BlockSpec(memory_space=pltpu.HBM)] * held
    specs += [pl.BlockSpec(memory_space=pltpu.VMEM)] * (taken - held)
    specs += [pl.BlockSpec(memory_space=pl.ANY)] * len(after)
    us = TIMES.get(name, 0.5)
    held_size = sum(size_of(o) for o in operands[held:])
    held_size += sum(size_of(o) for o in jax.tree.leaves(outs))

    def body(*refs):
        kernel(places(), *refs[:taken], *refs[taken + len(after) :])

    return pl.pallas_call(
        body,
        out_shape=outs,
        in_specs=specs,
        out_specs=jax.tree.map(lambda _: pl.BlockSpec(memory_space=pltpu.VMEM), outs),
        scratch_shapes=list(scratch),
        cost_estimate=pl.CostEstimate(
            flops=int(us * 2e10), bytes_accessed=int(us * 10), transcendentals=0
        ),
        compiler_params=pltpu.CompilerParams(vmem_limit_bytes=2 * held_size + ROOM),
        name=name,
    )(*operands, *after)


def norm_parts(values):
    center = values - jnp.mean(values, axis=-1, keepdims=True)
    factor = lax.rsqrt(jnp.mean(center * center, axis=-1, keepdims=True) + 1e-05)
    return center * factor, factor


def norm_inward(upward, gain, normed, factor):
    scaled = upward * gain
    return factor * (
        scaled
        - jnp.mean(scaled, axis=-1, keepdims=True)
        - normed * jnp.mean(scaled * normed, axis=-1, keepdims=True)
    )


def first_half(shape_of):
    return lax.broadcasted_iota(jnp.int32, shape_of, 1) % HEAD_DIM < HEAD_DIM // 2


def shifted(values):
    return pltpu.roll(values, 96, 1), pltpu.roll(values, 32, 1)


def rows_at(start, size):
    return pl.ds(pl.multiple_of(start, 16), size)


def lanes_at(start, size):
    return pl.ds(pl.multiple_of(start, 128), size)


def extra_rows(first, second, lanes):
    row = lax.broadcasted_iota(jnp.int32, (EXTRA, lanes), 0)
    pad = jnp.zeros((1, lanes - first.shape[1]), f32)
    first = jnp.concatenate([first, pad], axis=1)
    second = jnp.concatenate([second, pad], axis=1)
    return jnp.where(row == 0, first, jnp.where(row == 1, second, 0.0))


def copied(pairs, sems):
    copies = [pltpu.make_async_copy(src, dst, sems.at[i]) for i, (src, dst) in enumerate(pairs)]
    for copy in copies:
        copy.start()
    for copy in copies:
        copy.wait()


def qkv_piece_kernel(where, w_qkv, part, gains, out, rows, sems):
    chip, core = where[0], where[1]
    half = w_qkv.shape[0] // CORES
    width = w_qkv.shape[1] // 3
    local = width // CHIPS
    size, lanes = part.shape
    copied(((w_qkv.at[rows_at(core * half, half), :], rows),), sems)
    for b in range(CHIPS):

        @pl.when(chip == b)
        def _():
            for p in range(3):
                at = p * width + b * local
                out[:half, p * local : (p + 1) * local] = rows[:, at : at + local]

    both = gains[...].astype(f32)[None]
    share = both.shape[1] // 2
    out[half:, :] = extra_rows(both[:, :share], both[:, share:], out.shape[1]).astype(bf16)
    out[:size, 3 * local :] = part[:, :local]
    out[size:half, 3 * local :] = part[:, local:]


def ffn_piece_kernel(where, w_in, w_back, out, rows, back, sems):
    chip, core = where[0], where[1]
    half = w_in.shape[0] // CORES
    units = FF // PLANES // CHIPS
    lanes = back.shape[1]
    copied(
        (
            (w_in.at[rows_at(core * half, half), :], rows),
            (w_back.at[:, lanes_at(core * lanes, lanes)], back),
        ),
        sems,
    )
    spare = half - units
    side = units * lanes // half
    rest = lanes - side
    at_back = 2 * PLANES * units
    for b in range(CHIPS):

        @pl.when(chip == b)
        def _():
            for p in range(2):
                for z in range(PLANES):
                    at = p * FF + z * units * CHIPS + b * units
                    to = (p * PLANES + z) * units
                    out[:, to : to + units] = rows[:, at : at + units]
            own = back[b * units : (b + 1) * units, :]
            out[:units, at_back:] = own[:, :side]
            for i in range(units // spare):
                to = at_back + i * rest
                out[units:, to : to + rest] = own[i * spare : (i + 1) * spare, side:]


def unpacked(block, units):
    spare = block.shape[0] - units
    rest = block.shape[1] // (units // spare)
    last = [block[units:, i * rest : (i + 1) * rest] for i in range(units // spare)]
    return jnp.concatenate([block[:units], jnp.concatenate(last, axis=0)], axis=1)


def place_kernel(slot, where, p0, p1, p2, p3, out):
    for i, ref in enumerate((p0, p1, p2, p3)):
        out[where[slot] ^ i] = ref[...]


def qkv_place_kernel(where, p0, p1, p2, p3, out, packet):
    lanes = out.shape[2]
    size = packet.shape[1]
    for i, ref in enumerate((p0, p1, p2, p3)):
        z = where[2] ^ i
        out[z] = ref[:, :lanes]
        packet[z] = jnp.concatenate([ref[:size, lanes:], ref[size : 2 * size, lanes:]], axis=1)


def up_pair_kernel(where, own, both, out):
    out[0] = own[...]
    out[1] = both[own.shape[0] :, :]


def last_packet_kernel(where, total, *refs):
    half, lanes = total.shape
    rows, width = refs[0].shape
    spare = lanes - width
    for ref, out in zip(refs[: len(refs) // 2], refs[len(refs) // 2 :]):
        out[:rows, :] = ref[...]
        out[rows : rows + half, :] = total[:, :width]
        for i in range(half // 32):
            at = slice(i * spare, (i + 1) * spare)
            out[rows + half :, at] = total[i * 32 : (i + 1) * 32, width:]
        blank = width - half // 32 * spare
        out[rows + half :, width - blank :] = jnp.zeros((32, blank), bf16)


def ffn_gather_kernel(where, total, r1, r2, r3, out):
    half, lanes = total.shape
    width = r1.shape[1]
    spare = lanes - width
    rows = r1.shape[0] - half - 32
    out[where[0]] = total[...]
    for j, ref in enumerate((r1, r2, r3)):
        at = where[0] ^ (j + 1)
        out[at, :, :width] = ref[rows : rows + half, :]
        for i in range(half // 32):
            piece = ref[rows + half :, i * spare : (i + 1) * spare]
            out[at, i * 32 : (i + 1) * 32, width:] = piece


def pair_kernel(where, first, second, out):
    out[0] = first[...]
    out[1] = second[...]


def ffn_place_kernel(where, near, far, p01, p23, out):
    half = near.shape[1]
    p0, p1, p2, p3 = p01.at[0], p01.at[1], p23.at[0], p23.at[1]
    size, lanes = p0.shape[1:]
    for i, ref in enumerate((near.at[0], far.at[0], near.at[1], far.at[1])):
        z = where[2] ^ i
        out[z, :, 2 * lanes :] = ref[...]
    for i, ref in enumerate((p0, p1, p2, p3)):
        b = where[0] ^ i
        at = rows_at((b % 2) * size, size)

        for half_at in range(2):

            @pl.when(b // 2 == half_at)
            def _():
                for z in range(PLANES):
                    out[z, at, half_at * lanes : (half_at + 1) * lanes] = ref[z]


def qkv_kernel(where, x0, x1, x2, x3, mine, other, cos, sin, a_out, q_out, kv_out, w_out, g_out):
    rows = x0.shape[0]
    half = mine.shape[1] - EXTRA
    local = mine.shape[2] // 3
    share = CORES * half
    core = where[1]
    for z in range(PLANES):
        w_out[rows_at(z * share + core * half, half), :] = mine[z, :half, :]
        w_out[rows_at(z * share + (1 - core) * half, half), :] = other[z, :half, :]
        tail = mine[z, half:, :share].astype(f32)
        g_out[:, z * share : (z + 1) * share] = tail[:8]
    gain = g_out[0:1, :]
    for j, ref in enumerate((x0, x1, x2, x3)):
        normed, _ = norm_parts(ref[:rows, :].astype(f32))
        a_out[j * rows : (j + 1) * rows, :] = (normed * gain).astype(bf16)
    out = dot(a_out[...], w_out[...])
    front = first_half((CHIPS * rows, 128))
    parts = []
    for at in range(0, 2 * local, 128):
        u = out[:, at : at + 128]
        up, down = shifted(u)
        parts.append((u * cos[...] + jnp.where(front, -up, down) * sin[...]).astype(bf16))
    qk = jnp.concatenate(parts, axis=1)
    value = out[:, 2 * local :].astype(bf16)
    for j in range(CHIPS):
        at = slice(j * rows, (j + 1) * rows)
        q_out[j] = qk[at, :local]
        kv_out[j, :, :local] = qk[at, local:]
        kv_out[j, :, local:] = value[at]


def block_of(pairs, j, local):
    return pairs[j // 2, :, j % 2 * local : (j % 2 + 1) * local]


def extended(where, j, kv, other, rim):
    chip, core = where[0], where[1]
    length = kv.shape[1]
    b = chip ^ j
    below = jnp.where(core == 0, jnp.maximum(b - 1, 0), b) ^ chip
    above = jnp.where(core == 0, b, jnp.minimum(b + 1, CHIPS - 1)) ^ chip
    before = other[below, length - HALF :, :]
    after = other[above, :HALF, :]
    if rim is not None:
        before = jnp.where((core == 0) & (b == 0), rim[...], before)
        after = jnp.where((core == 1) & (b == CHIPS - 1), rim[...], after)
    return jnp.concatenate([before, kv[j], after], axis=0)


def probs_of(q, k, bias):
    logits = dot_t(q, k) * SCALE + bias
    highest = jnp.max(logits, axis=-1, keepdims=True)
    exponent = jnp.exp(logits - highest)
    return exponent / jnp.sum(exponent, axis=-1, keepdims=True)


def attend_kernel(edges, where, q, kv, other, bias, *rest):
    rim, out, kept = rest if edges else (None, *rest)
    local = q.shape[-1]
    extent = bias.shape[-1]
    for j in range(CHIPS):
        ext = extended(where, j, kv, other, rim)
        parts = []
        for h in range(local // HEAD_DIM):
            lanes = slice(h * HEAD_DIM, (h + 1) * HEAD_DIM)
            prob = probs_of(q[j, :, lanes], ext[:, lanes], bias[j]).astype(bf16)
            kept[j, :, h * extent : (h + 1) * extent] = prob
            parts.append(dot(prob, ext[:, local + h * HEAD_DIM : local + (h + 1) * HEAD_DIM]))
        out[j // 2, :, j % 2 * local : (j % 2 + 1) * local] = jnp.concatenate(parts, axis=1).astype(bf16)


def ffn_kernel(
    where, t0, t1, t2, t3, x0, x1, x2, x3, y02, y13, mine, other, gains,
    own_out, d1_out, d2_out, d3_out, hid_out, a_out, m_out, dgu_out, gain_out, wb_out, wc_out,
    wi, wo,
):
    chip, core = where[0], where[1]
    rows = x0.shape[0]
    width = x0.shape[1]
    half = mine.shape[1]
    share = CORES * half
    units = FF // CHIPS
    part = units // PLANES
    lanes = width // CORES
    local = width // CHIPS
    for z in range(PLANES):
        for k, ref in ((core, mine), (1 - core, other)):
            wi[rows_at(z * share + k * half, half), :] = ref[z, :, width : width + 2 * units]
            for p in range(CORES):
                at = slice(z * share + p * half, z * share + (p + 1) * half)
                wo[at, lanes_at(k * lanes, lanes)] = ref[z, :, p * lanes : (p + 1) * lanes]
    own_back, other_back = [
        jnp.concatenate(
            [unpacked(ref[z, :, width + 2 * units :], part) for z in range(PLANES)], axis=0
        )
        for ref in (mine, other)
    ]
    wb_out[:, :lanes] = jnp.where(core == 0, own_back, other_back)
    wb_out[:, lanes:] = jnp.where(core == 0, other_back, own_back)
    wc_out[...] = wo[rows_at(chip * local, local), :]
    xs = (x0, x1, x2, x3)
    gain = gains[1:2, :]
    outward = [
        (ref, wo[rows_at((chip ^ i) * local, local), :]) for i, ref in enumerate((t0, t1, t2, t3))
    ]
    normed = []
    for j in range(CHIPS):
        hidden = xs[j][:rows, :].astype(f32)
        for i, (ref, weight) in enumerate(outward):
            hidden = hidden + dot(block_of(ref, j ^ i, local), weight)
        if j == 0:
            hid_out[...] = hidden
        norm, _ = norm_parts(hidden)
        normed.append(norm)
        a_out[j * rows : (j + 1) * rows, :] = (norm * gain).astype(bf16)
    total = jnp.zeros((1, width), f32)
    for j in range(CHIPS):
        at = slice(j * rows, (j + 1) * rows)
        gu = dot(a_out[at, :], wi[...])
        entering, gating = gu[:, :units], gu[:, units:]
        rise = 0.5 * (1.0 + lax.erf(entering * (0.5**0.5)))
        slope = rise + entering * jnp.exp(-0.5 * entering * entering) * 0.3989422804014327
        act = entering * rise
        m_out[at, :] = (act * gating).astype(bf16)
        dm = dot_t((y02, y13)[j % 2][j // 2], wb_out[...])
        dgu = jnp.concatenate([dm * gating * slope, dm * act], axis=1).astype(bf16)
        dgu_out[at, :] = dgu
        da = dot_t(dgu, wi[...])
        total = total + jnp.sum(da * normed[j], axis=0, keepdims=True)
        if j == 0:
            own_out[...] = da
        else:
            (d1_out, d2_out, d3_out)[j - 1][...] = da.astype(bf16)
    gain_out[...] = jnp.broadcast_to(total, gain_out.shape)


def mixed_kernel(where, m, wb, own, m1, m2, m3):
    rows = own.shape[0]
    own[...] = dot(m[:rows, :], wb[...])
    for j, ref in enumerate((m1, m2, m3)):
        ref[...] = dot(m[(j + 1) * rows : (j + 2) * rows, :], wb[...]).astype(bf16)


def mixed_sum_kernel(where, own, r1, r2, r3, hidden, out):
    total = own[...] + r1[...].astype(f32) + r2[...].astype(f32) + r3[...].astype(f32)
    out[0] = (hidden[...] + total).astype(bf16)


def ffn_grads_kernel(where, a, m, dgu, y02, y13, keep, away, gin, gb):
    core = where[1]
    half = keep.shape[1]
    share = CORES * half
    units = m.shape[1]
    part = units // PLANES
    lanes = y02.shape[2] // CORES
    gin[...] = t_dot(a[...], dgu[...])
    upward = jnp.concatenate([y02[0], y13[0], y02[1], y13[1]], axis=0)
    back = t_dot(m[...], upward)
    first, second = back[:, :lanes], back[:, lanes:]
    gb[0] = jnp.where(core == 0, first, second)
    gb[1] = jnp.where(core == 0, second, first)
    for z in range(PLANES):
        at = slice(z * part, (z + 1) * part)
        blank = jnp.zeros((half - part, lanes), f32)
        keep[z, :, : 2 * units] = gin[rows_at(z * share + core * half, half), :]
        keep[z, :, 2 * units :] = jnp.concatenate([gb[0, at, :], blank], axis=0)
        away[z, :, : 2 * units] = gin[rows_at(z * share + (1 - core) * half, half), :].astype(bf16)
        away[z, :, 2 * units :] = jnp.concatenate([gb[1, at, :], blank], axis=0).astype(bf16)


def dh_kernel(where, own, r1, r2, r3, y02, hidden, gains, dh_out, low_out):
    total = own[...] + r1[...].astype(f32) + r2[...].astype(f32) + r3[...].astype(f32)
    normed, factor = norm_parts(hidden[...])
    dh = y02[0].astype(f32) + norm_inward(total, gains[1:2, :], normed, factor)
    dh_out[...] = dh
    low_out[...] = dh.astype(bf16)


def attend_back_kernel(edges, where, q, kv, other, probs, h0, h1, h2, h3, w_out, *rest):
    rim, rest = (rest[0], rest[1:]) if edges else (None, rest)
    dq_out, dkv_out, back_out = rest[:3]
    chip, core = where[0], where[1]
    local = q.shape[-1]
    length = q.shape[1]
    extent = length + 2 * HALF
    back_out[...] = jnp.zeros_like(back_out)
    for j, dh in enumerate((h0, h1, h2, h3)):
        dctx = dot_t(dh[...], w_out[...]).astype(bf16)
        ext = extended(where, j, kv, other, rim)
        dqs, dks, dvs = [], [], []
        for h in range(local // HEAD_DIM):
            lanes = slice(h * HEAD_DIM, (h + 1) * HEAD_DIM)
            qh = q[j, :, lanes]
            kh = ext[:, lanes]
            vh = ext[:, local + h * HEAD_DIM : local + (h + 1) * HEAD_DIM]
            dch = dctx[:, lanes]
            low = probs[j, :, h * extent : (h + 1) * extent]
            prob = low.astype(f32)
            dprob = dot_t(dch, vh)
            inner = jnp.sum(prob * dprob, axis=-1, keepdims=True)
            dscore = (prob * (dprob - inner) * SCALE).astype(bf16)
            dqs.append(dot(dscore, kh))
            dks.append(t_dot(dscore, qh))
            dvs.append(t_dot(low, dch))
        dq_out[j] = jnp.concatenate(dqs, axis=1)
        grads = jnp.concatenate(dks + dvs, axis=1)
        dkv_out[j] = grads[HALF : HALF + length]
        before = grads[:HALF].astype(bf16)
        after = grads[HALF + length :].astype(bf16)
        b = chip ^ j
        below = jnp.where(core == 0, b - 1, b)
        above = jnp.where(core == 0, b, b + 1)

        @pl.when(below >= 0)
        def _():
            back_out[jnp.maximum(below, 0) ^ chip, length - HALF :, :] = before

        @pl.when(above < CHIPS)
        def _():
            back_out[jnp.minimum(above, CHIPS - 1) ^ chip, :HALF, :] = after

        if edges:
            rim_out = rest[3]

            @pl.when(below < 0)
            def _():
                rim_out[...] = before

            @pl.when(above >= CHIPS)
            def _():
                rim_out[...] = after


def qkv_grads_kernel(edges, where, dq, dkv, back, cos, sin, a, t0, t1, t2, t3, h0, h1, h2, h3, *rest):
    rim, rest = (rest[0], rest[1:]) if edges else (None, rest)
    keep, away, d_out, acc, cols = rest
    chip, core = where[0], where[1]
    length = dq.shape[1]
    local = dq.shape[2]
    width = a.shape[1]
    front = first_half((length, 128))
    for j in range(CHIPS):
        at = slice(j * length, (j + 1) * length)
        gkv = dkv[j] + back[j].astype(f32)
        if edges:
            b = chip ^ j
            blank = jnp.zeros((length - HALF, 2 * local), f32)
            value = rim[...].astype(f32)
            gkv = gkv + jnp.where(
                (core == 0) & (b == 0), jnp.concatenate([value, blank], axis=0), 0.0
    )
            gkv = gkv + jnp.where(
                (core == 1) & (b == CHIPS - 1), jnp.concatenate([blank, value], axis=0), 0.0
    )
        g = jnp.concatenate([dq[j], gkv[:, :local]], axis=1)
        for lane in range(0, 2 * local, 128):
            u = g[:, lane : lane + 128]
            up, down = shifted(u * sin[at, :])
            d_out[at, lane : lane + 128] = (
                u * cos[at, :] + jnp.where(front, up, -down)
            ).astype(bf16)
        d_out[at, 2 * local :] = gkv[:, local:].astype(bf16)
    acc[:, : 3 * local] = t_dot(a[...], d_out[...])
    for b in range(CHIPS):

        @pl.when(chip == b)
        def _():
            for j, ref in enumerate((h0, h1, h2, h3)):
                cols[j * length : (j + 1) * length, :] = ref[:, b * local : (b + 1) * local]

    for i, ref in enumerate((t0, t1, t2, t3)):
        rows = jnp.concatenate([block_of(ref, j ^ i, local) for j in range(CHIPS)], axis=0)
        acc[rows_at((chip ^ i) * local, local), 3 * local :] = t_dot(rows, cols[...])
    half = keep.shape[1]
    share = CORES * half
    for z in range(PLANES):
        keep[z] = acc[rows_at(z * share + core * half, half), :]
        away[z] = acc[rows_at(z * share + (1 - core) * half, half), :].astype(bf16)


def da_kernel(where, d, w, x0, x1, x2, x3, gain_two, own_out, o1, o2, o3, gain_out):
    rows = x0.shape[0]
    total = jnp.zeros((1, w.shape[0]), f32)
    for j, ref in enumerate((x0, x1, x2, x3)):
        da = dot_t(d[j * rows : (j + 1) * rows, :], w[...])
        normed, _ = norm_parts(ref[:rows, :].astype(f32))
        total = total + jnp.sum(da * normed, axis=0, keepdims=True)
        if j == 0:
            own_out[...] = da
        else:
            (o1, o2, o3)[j - 1][...] = da.astype(bf16)
    share = w.shape[0] // PLANES
    for z in range(PLANES):
        at = slice(z * share, (z + 1) * share)
        gain_out[z] = extra_rows(total[:, at], gain_two[0:1, at], gain_out.shape[2])


def copy_kernel(where, value, out):
    out[...] = value[...]


def ffn_split_kernel(where, keep, got, near, far):
    for i in range(PLANES):
        at = where[2] ^ i
        total = keep[at] + got[at].astype(f32)
        if i % 2 == 0:
            near[i // 2] = total
        else:
            far[i // 2] = total.astype(bf16)


def ffn_near_kernel(where, near, got, own, sent):
    own[...] = near[0] + got[0].astype(f32)
    sent[...] = (near[1] + got[1].astype(f32)).astype(bf16)


def ffn_total_kernel(where, own, got, out):
    out[...] = (own[...] + got[...].astype(f32)).astype(out.dtype)


def to_near_plane_kernel(where, keep, got, gains, out):
    half = keep.shape[1]
    at = where[2] ^ 1
    out[:half, :] = (keep[at] + got[at].astype(f32)).astype(bf16)
    out[half:, :] = gains[at].astype(bf16)


def to_planes_gains_kernel(where, keep, got, gains, own, o2, o3):
    plane = where[2]
    half = keep.shape[1]
    own[:half, :] = keep[plane] + got[plane].astype(f32)
    own[half:, :] = gains[plane]
    for i, ref in enumerate((o2, o3)):
        at = plane ^ (i + 2)
        ref[:half, :] = (keep[at] + got[at].astype(f32)).astype(bf16)
        ref[half:, :] = gains[at].astype(bf16)


def sum_kernel(where, own, r1, r2, r3, out):
    total = own[...] + r1[...].astype(f32) + r2[...].astype(f32) + r3[...].astype(f32)
    out[...] = total.astype(out.dtype)


def last_kernel(where, own, r1, r2, r3, x0, dh, gains, grad_out):
    total = own[...]
    for ref in (r1, r2, r3):
        total = total + ref[: own.shape[0], :].astype(f32)
    normed, factor = norm_parts(x0[...].astype(f32))
    grad = dh[...] + norm_inward(total, gains[0:1, :], normed, factor)
    grad_out[0] = grad.astype(bf16)


def ffn_owned_kernel(where, mine, other, in_out, back_out):
    core = where[1]
    half = mine.shape[1]
    units = FF // CHIPS
    part = units // PLANES
    lanes = mine.shape[2] - 2 * units
    for k, ref in ((core, mine), (1 - core, other)):
        rows = rows_at(k * half, half)
        for p in range(2):
            for z in range(PLANES):
                at = (p * PLANES + z) * part
                for b in range(CHIPS):
                    to = p * FF + (z * CHIPS + b) * part
                    in_out[rows, to : to + part] = ref[b, :, at : at + part].astype(f32)
    for b in range(CHIPS):
        own = mine[b, :part, 2 * units :].astype(f32)
        got = other[b, :part, 2 * units :].astype(f32)
        back_out[b * part : (b + 1) * part, :lanes] = jnp.where(core == 0, own, got)
        back_out[b * part : (b + 1) * part, lanes:] = jnp.where(core == 0, got, own)


def qkv_owned_kernel(where, mine, other, qkv_out, w_out, one_out, two_out):
    core = where[1]
    half = mine.shape[1] - EXTRA
    local = w_out.shape[1] // CHIPS
    total = jnp.zeros((EXTRA, local), f32)
    for k, ref in ((core, mine), (1 - core, other)):
        rows = rows_at(k * half, half)
        for b in range(CHIPS):
            for p in range(3):
                to = (p * CHIPS + b) * local
                qkv_out[rows, to : to + local] = ref[b, :half, p * local : (p + 1) * local].astype(f32)
            w_out[rows, b * local : (b + 1) * local] = ref[b, :half, 3 * local :].astype(f32)
            total = total + ref[b, half:, :local].astype(f32)
    one_out[...] = total[0]
    two_out[...] = total[1]


def shards(tokens, norm_gain, w_qkv, w_out, ffn_gain, w_in, w_back, seq_ids, cotangent):
    length, width = tokens.shape[1:]
    me = lax.axis_index("seq")
    seq_count = lax.axis_size("seq")
    edges = seq_count > MEMBERS
    group = me // MEMBERS
    chip = (me % MEMBERS) // CORES
    core = me % CORES
    local = width // CHIPS
    units = FF // CHIPS
    many = CHIPS * length
    half = width // PLANES // CORES
    lanes = width // CORES
    extent = length + 2 * HALF
    kept = half + EXTRA
    in_sent = 2 * units + units // PLANES * lanes // half
    in_lanes = width + in_sent
    ffn_lanes = 2 * units + lanes
    qkv_lanes = 4 * local

    out_rows = w_out.shape[0] // CHIPS
    piece = call(
        qkv_piece_kernel,
        "qkv_piece",
        shape(kept, 4 * local),
        w_qkv,
        lax.dynamic_slice(w_out, (chip * out_rows, core * lanes), (out_rows, lanes)),
        jnp.concatenate([norm_gain, ffn_gain]),
        held=1,
        scratch=(pltpu.VMEM((half, 3 * width), bf16), pltpu.SemaphoreType.DMA((1,))),
    )
    pieces = over_planes(piece)
    both = jnp.concatenate([tokens[0], cotangent[0]], axis=0)
    both_near = swap_seq(both, 2 * CORES)
    xs = [tokens[0], swap_seq(tokens[0], CORES), both_near, swap_seq(tokens[0], 3 * CORES)]
    mine, out_own = call(
        qkv_place_kernel,
        "qkv_place",
        (
            shape(PLANES, kept, 3 * local),
            shape(PLANES, out_rows, lanes),
        ),
        *pieces,
    )
    piece = call(
        ffn_piece_kernel,
        "ffn_piece",
        shape(half, in_sent),
        w_in,
        w_back,
        held=2,
        scratch=(
            pltpu.VMEM((half, 2 * FF), bf16),
            pltpu.VMEM((w_back.shape[0], lanes), bf16),
            pltpu.SemaphoreType.DMA((2,)),
        ),
        after=(mine,),
    )
    in_near = swap_shard(piece, 2)
    out_near = swap_seq(out_own, CORES)
    other = swap_core(mine)

    block = (group * CHIPS + (chip ^ jnp.arange(CHIPS))) * CORES + core
    position = (block[:, None] * length + jnp.arange(length)[None]).astype(f32).reshape(many)
    frequency = 10000.0 ** (-jnp.arange(0, HEAD_DIM, 2).astype(f32) / HEAD_DIM)
    angles = position[:, None] * jnp.tile(frequency, 4)[None]
    cosine, sine = jnp.cos(angles), jnp.sin(angles)
    spans = length // HALF
    ids = jnp.pad(seq_ids[0], (1, 1), constant_values=-1)
    key_ids = jnp.stack(
        [lax.dynamic_slice_in_dim(ids, block[j] * spans, spans + 2, 0) for j in range(CHIPS)]
    )
    key_ids = jnp.repeat(key_ids, HALF, axis=1)
    query_ids = key_ids[:, HALF : HALF + length]
    offset = jnp.arange(extent)[None, :] - HALF - jnp.arange(length)[:, None]
    allowed = (jnp.abs(offset) <= HALF)[None] & (query_ids[:, :, None] == key_ids[:, None, :])
    bias = jnp.where(allowed, 0.0, -1e30).astype(f32)

    low_one, query, kv, wq, gains = call(
        qkv_kernel,
        "qkv",
        (
            shape(many, width),
            shape(CHIPS, length, local),
            shape(CHIPS, length, 2 * local),
            shape(width, 3 * local),
            shape(8, width, dtype=f32),
        ),
        *xs,
        mine,
        other,
        cosine,
        sine,
    )
    kv_other = swap_core(kv)

    def beyond(value):
        pairs = []
        for m in range(seq_count):
            to = m - MEMBERS + 1 if m % CORES == 0 else m + MEMBERS - 1
            if 0 <= to < seq_count:
                pairs.append((m, to))
        return lax.ppermute(value, "seq", pairs)

    rim = ()
    if edges:
        first = lax.dynamic_index_in_dim(kv, chip, 0, False)[:HALF]
        last = lax.dynamic_index_in_dim(kv, chip ^ (CHIPS - 1), 0, False)[length - HALF :]
        rim = (beyond(jnp.where(core == 0, first, last)),)

    up_pair = call(up_pair_kernel, "up_pair", shape(2, length, width), cotangent[0], both_near, after=(gains,))
    gys = (up_pair, swap_seq(up_pair, CORES))
    out_pair = call(pair_kernel, "out_pair", shape(2, *out_own.shape), out_own, out_near, after=(up_pair,))
    out_far = swap_seq(out_pair, 2 * CORES)
    attn, probs = call(
        functools.partial(attend_kernel, edges),
        "attend",
        (shape(2, length, 2 * local), shape(CHIPS, length, local // HEAD_DIM * extent)),
        query,
        kv,
        kv_other,
        bias,
        *rim,
    )
    in_pair = call(
        pair_kernel, "in_pair", shape(2, half, in_sent), piece, in_near, after=(attn,)
    )
    in_far = swap_shard(in_pair, 1)
    last_attn = call(copy_kernel, "attn_copy", shape(*attn.shape), attn, after=(gys[1],))
    attns = [attn, swap_seq(attn, CORES), swap_seq(attn, 2 * CORES), swap_seq(last_attn, 3 * CORES)]
    in_mine = call(
        ffn_place_kernel,
        "ffn_place",
        shape(PLANES, half, in_lanes),
        in_pair,
        in_far,
        out_pair,
        out_far,
        after=tuple(attns[1:]),
    )
    in_other = swap_core(in_mine)
    own, d1, d2, d3, hidden, low_two, hidden_low, grad_expanded, gain_two, wb, wo = call(
        ffn_kernel,
        "ffn",
        (shape(length, width, dtype=f32),)
        + (shape(length, width),) * 3
        + (
            shape(length, width, dtype=f32),
            shape(many, width),
            shape(many, units),
            shape(many, 2 * units),
            shape(8, width, dtype=f32),
            shape(units, width),
            shape(local, width),
        ),
        *attns,
        *xs,
        *gys,
        in_mine,
        in_other,
        gains,
        scratch=(pltpu.VMEM((width, 2 * units), bf16), pltpu.VMEM((width, width), bf16)),
    )
    received = [swap_seq(d, CORES * (j + 1)) for j, d in enumerate((d1, d2, d3))]
    keep_ffn, away = call(
        ffn_grads_kernel,
        "ffn_grads",
        (shape(PLANES, half, ffn_lanes, dtype=f32), shape(PLANES, half, ffn_lanes)),
        low_two,
        hidden_low,
        grad_expanded,
        *gys,
        scratch=(pltpu.VMEM((width, 2 * units), f32), pltpu.VMEM((CORES, units, lanes), f32)),
    )
    got_ffn = swap_core(away)
    near, far = call(
        ffn_split_kernel,
        "ffn_split",
        (shape(2, half, ffn_lanes, dtype=f32), shape(2, half, ffn_lanes)),
        keep_ffn,
        got_ffn,
    )
    got_far = swap_shard(far, 1)
    dh, dh_low = call(
        dh_kernel, "dh", (shape(length, width, dtype=f32), shape(length, width)), own, *received, gys[0], hidden, gains, after=(far,)
    )
    dhs = over_chips(dh_low)
    partial_mixed = call(
        mixed_kernel,
        "mixed",
        (shape(length, width, dtype=f32),) + (shape(length, width),) * 3,
        hidden_low,
        wb,
        after=(dh_low,),
    )
    got_mixed = [swap_seq(o, CORES * (j + 1)) for j, o in enumerate(partial_mixed[1:])]

    backs = call(
        functools.partial(attend_back_kernel, edges),
        "attend_back",
        (
            shape(CHIPS, length, local, dtype=f32),
            shape(CHIPS, length, 2 * local, dtype=f32),
            shape(CHIPS, length, 2 * local),
        )
        + ((shape(HALF, 2 * local),) if edges else ()),
        query,
        kv,
        kv_other,
        probs,
        *dhs,
        wo,
        *rim,
        after=(far,),
    )
    dq, dkv, back = backs[:3]
    back = swap_core(back)
    if edges:
        rim = (beyond(backs[3]),)

    def over_groups(total, kept_type):
        step = MEMBERS
        while step < seq_count:
            total = total + swap_seq(total.astype(bf16), step).astype(f32)
            step *= 2
        return total.astype(kept_type)

    def summed(own, parts, name, after=()):
        out = call(
            sum_kernel, name, shape(*own.shape, dtype=f32 if edges else bf16), own, *parts, after=after
        )
        return over_groups(out, bf16)

    mixed = call(
        mixed_sum_kernel, "mixed_sum", shape(1, length, width), partial_mixed[0], *got_mixed, hidden, after=(away,)
    )

    keep, away, dqkv = call(
        functools.partial(qkv_grads_kernel, edges),
        "qkv_grads",
        (
            shape(PLANES, half, qkv_lanes, dtype=f32),
            shape(PLANES, half, qkv_lanes),
            shape(many, 3 * local),
        ),
        dq,
        dkv,
        back,
        cosine,
        sine,
        low_one,
        *attns,
        *dhs,
        *rim,
        scratch=(pltpu.VMEM((width, qkv_lanes), f32), pltpu.VMEM((many, local), bf16)),
    )
    got = swap_core(away)
    own_ffn, sent_near = call(
        ffn_near_kernel,
        "ffn_near",
        (shape(half, ffn_lanes, dtype=f32), shape(half, ffn_lanes)),
        near,
        got_far,
        after=(dq,),
    )
    total = call(
        ffn_total_kernel,
        "ffn_total",
        shape(half, ffn_lanes, dtype=f32 if edges else bf16),
        own_ffn,
        swap_shard(sent_near, 2),
        after=(got,),
    )
    total = over_groups(total, bf16)
    last_own, o1, o2, o3, gain_sums = call(
        da_kernel,
        "da",
        (shape(length, width, dtype=f32),)
        + (shape(length, width),) * 3
        + (shape(PLANES, EXTRA, qkv_lanes, dtype=f32),),
        dqkv,
        wq,
        *xs,
        gain_two,
        after=(mixed,),
    )
    to_near = call(
        to_near_plane_kernel, "qkv_to_near", shape(kept, qkv_lanes), keep, got, gain_sums
    )
    from_near = swap_shard(to_near, 1)
    sent = call(
        to_planes_gains_kernel,
        "qkv_to_planes",
        (shape(kept, qkv_lanes, dtype=f32),)
        + (shape(kept, qkv_lanes),) * 2,
        keep,
        got,
        gain_sums,
        after=(to_near,),
    )
    got = [from_near] + [swap_shard(s, i + 2) for i, s in enumerate(sent[1:3])]
    packet = shape(length + half + 32, width)
    packets = call(last_packet_kernel, "last_packet", (packet,) * 2, total, o1, o2, after=(sent[1],))
    packets += call(last_packet_kernel, "third_packet", (packet,), total, o3, after=(got[0],))
    received = [swap_seq(o, CORES * (j + 1)) for j, o in enumerate(packets)]

    mine = call(
        ffn_gather_kernel,
        "ffn_gather",
        shape(CHIPS, half, ffn_lanes),
        total,
        *received,
    )
    owned_in, owned_back = call(
        ffn_owned_kernel,
        "ffn_owned",
        (shape(*w_in.shape, dtype=f32), shape(*w_back.shape, dtype=f32)),
        mine,
        swap_core(mine),
    )
    grad_tokens = call(
        last_kernel,
        "last",
        shape(1, length, width),
        last_own,
        *received,
        xs[0],
        dh,
        gains,
        after=(sent[1],),
    )
    mine = call(
        functools.partial(place_kernel, 0),
        "qkv_gather",
        shape(CHIPS, kept, qkv_lanes),
        *over_chips(summed(sent[0], got, "qkv_sum")),
        after=(grad_tokens, owned_back),
    )
    owned_qkv, owned_out, grad_gain_one, grad_gain_two = call(
        qkv_owned_kernel,
        "qkv_owned",
        (
            shape(*w_qkv.shape, dtype=f32),
            shape(*w_out.shape, dtype=f32),
            shape(local, dtype=f32),
            shape(local, dtype=f32),
        ),
        mine,
        swap_core(mine),
    )
    return (mixed, grad_tokens, grad_gain_one, owned_qkv, owned_out, grad_gain_two, owned_in, owned_back)


def solution(mesh):
    return jax.shard_map(
        shards,
        mesh=mesh,
        in_specs=(
            P("shard", "seq", None),
            P("shard"),
            P("shard", None),
            P("shard", None),
            P("shard"),
            P("shard", None),
            P("shard", None),
            P("shard", None),
            P("shard", "seq", None),
        ),
        out_specs=(
            P("shard", "seq", None),
            P("shard", "seq", None),
            P("shard"),
            P("shard", None),
            P("shard", None),
            P("shard"),
            P("shard", None),
            P("shard", None),
        ),
        check_vma=False,
    )
```
